32 devices in a mesh: dp: 2 (over core), blk: 8 (over z, y), tensor: 2 (over x).
Axes of the slice: x: 2, y: 2, z: 4, core: 2. Of those that a mesh axis runs over, the one named last changes fastest.
Arguments:
- tokens: bfloat16 [14, 2048, 1024], P('dp', 'blk'), may hold values from -6 to 6
- ln_gain: float32 [1024], replicated, may hold values from 0.5 to 1.5
- ln_bias: float32 [1024], replicated, may hold values from -2 to 2
- w_qkv: bfloat16 [1024, 3, 1024], P(('dp', 'blk'), None, 'tensor'), may hold values from -0.1875 to 0.1875
- b_qkv: float32 [3, 1024], P(None, 'tensor'), may hold values from -3 to 3
- w_out: bfloat16 [1024, 1024], P('tensor', ('dp', 'blk')), may hold values from -1.5 to 1.5
- w_fc: bfloat16 [1024, 4096], P(('dp', 'blk'), 'tensor'), may hold values from -0.1875 to 0.1875
- b_fc: float32 [4096], P('tensor'), may hold values from -3 to 3
- w_proj: bfloat16 [4096, 1024], P('tensor', ('dp', 'blk')), may hold values from -0.09375 to 0.09375
- b_out: float32 [1024], replicated, may hold values from -2 to 2
- bounds: int32 [14, 5], P('dp'), may hold values from 0 to 2047, as said below
- cotangent: bfloat16 [14, 2048, 1024], P('dp', 'blk'), may hold values from -6 to 6
Outputs:
- result: bfloat16 [14, 2048, 1024], P('dp', 'blk')
- grad_tokens: bfloat16 [14, 2048, 1024], P('dp', 'blk')
- grad_ln_gain: float32 [1024], replicated
- grad_ln_bias: float32 [1024], replicated
- grad_w_qkv: float32 [1024, 3, 1024], P(('dp', 'blk'), None, 'tensor')
- grad_b_qkv: float32 [3, 1024], P(None, 'tensor')
- grad_w_out: float32 [1024, 1024], P('tensor', ('dp', 'blk'))
- grad_w_fc: float32 [1024, 4096], P(('dp', 'blk'), 'tensor')
- grad_b_fc: float32 [4096], P('tensor')
- grad_w_proj: float32 [4096, 1024], P('tensor', ('dp', 'blk'))
- grad_b_out: float32 [1024], replicated
The draws below stay inside these ranges and needn't reach their ends.
Inputs may be any that keep to these rules, and one draw needn't show every extreme that they name: `bounds`: each row lists the first positions of its 5 packed documents, strictly increasing, the first 0; a document runs to the next start or to the row's end at 2048.
All inputs are finite; a program needn't handle non-finite values.
Results may differ from the reference program's by a relative error of at most 0.015.
Values may be sent and summed in bfloat16 or wider, within the bound.
A program may use at most 256 MiB of HBM per device.

```python
import jax
import jax.numpy as jnp
from jax import lax

D = 1024
HEADS = 16
HEAD_DIM = 64
ROT_DIM = 16
FF = 4096
GROUP = 256
LEN = 2048
ROWS = 14


def draw_bounds(key, part):
    key = jax.random.fold_in(key, 7)
    key_a, key_b, key_c, key_d = jax.random.split(key, 4)
    long_first = jax.random.randint(key_a, (ROWS,), 2, GROUP)
    early_cut = jax.random.randint(key_b, (ROWS,), 1, long_first)
    long_end = jax.random.randint(key_c, (ROWS,), LEN - GROUP + 1, LEN - 1)
    late_cut = jax.random.randint(key_d, (ROWS,), long_end + 1, LEN)
    zeros_col = jnp.zeros((ROWS,), jnp.int32)
    return jnp.stack([zeros_col, early_cut, long_first, long_end, late_cut], 1).astype(jnp.int32)


def level_of(key, shape, pieces, least, high):
    level, own = 1.0, jax.random.fold_in(key, 6)
    for dim, blocks in pieces:
        heights = jnp.exp(jax.random.uniform(jax.random.fold_in(own, dim), (blocks,), jnp.float32, least / len(pieces), high / len(pieces)))
        level = level * jnp.repeat(heights, shape[dim] // blocks).reshape([-1 if axis == dim else 1 for axis in range(len(shape))])
    return level


def gaussian(rng, dims, deviation, most, shards=(), kind=jnp.bfloat16):
    level = level_of(rng, dims, shards, -0.22, 0.18) if shards else 1.0
    array = jax.random.normal(rng, dims, jnp.float32) * deviation * level
    return jnp.minimum(jnp.maximum(array, -most), most).astype(kind)


def setup_inputs(seed: int = 0) -> dict:
    key_list = jax.random.split(jax.random.key(seed), 13)
    return {
        "tokens": gaussian(key_list[0], (ROWS, LEN, D), 1.0, 6.0, ((0, 2), (1, 8))),
        "ln_gain": jnp.clip(1.0 + 0.1 * jax.random.normal(key_list[1], (D,), jnp.float32), 0.5, 1.5),
        "ln_bias": gaussian(key_list[2], (D,), 0.3, 2.0, (), jnp.float32),
        "w_qkv": gaussian(key_list[3], (D, 3, D), D ** -0.5, 0.1875, ((0, 16), (2, 2))),
        "b_qkv": gaussian(key_list[4], (3, D), 0.5, 3.0, ((1, 2),), jnp.float32),
        "w_out": gaussian(key_list[5], (D, D), (D // 64) ** -0.5, 1.5, ((0, 2), (1, 16))),
        "w_fc": gaussian(key_list[6], (D, FF), D ** -0.5, 0.1875, ((0, 16), (1, 2))),
        "b_fc": gaussian(key_list[7], (FF,), 0.5, 3.0, ((0, 2),), jnp.float32),
        "w_proj": gaussian(key_list[8], (FF, D), FF ** -0.5, 0.09375, ((0, 2), (1, 16))),
        "b_out": gaussian(key_list[9], (D,), 0.3, 2.0, (), jnp.float32),
        "bounds": draw_bounds(jax.random.fold_in(key_list[12], 71), 0),
        "cotangent": gaussian(key_list[11], (ROWS, LEN, D), 1.0, 6.0, ((0, 2), (1, 8))),
    }


@jax.custom_vjp
def low(v):
    return lax.optimization_barrier(v.astype(jnp.bfloat16)).astype(jnp.float32)

@jax.custom_vjp
def low_back(v):
    return v

def low_keep(v):
    return (low(v), None)

def low_pass(kept, grad):
    return (grad,)

def back_keep(v):
    return (v, None)

def back_low(kept, grad):
    return (low(grad),)
low.defvjp(low_keep, low_pass)
low_back.defvjp(back_keep, back_low)
epsilon = 1e-05
highest = lax.Precision.HIGHEST

def layer_norm(values, gain, shift):
    center = values - lax.optimization_barrier(jnp.mean(values, -1, keepdims=True))
    spread = lax.optimization_barrier(jnp.mean(center * center, -1, keepdims=True))
    return center * lax.rsqrt(spread + epsilon) * gain + shift

def rotary(values, cosine, sine):
    half = ROT_DIM // 2
    rot_part = values[..., :ROT_DIM]
    turned = jnp.concatenate([-rot_part[..., half:], rot_part[..., :half]], -1)
    return jnp.concatenate([rot_part * cosine + turned * sine, values[..., ROT_DIM:]], -1)

def angles(positions):
    freqs = 10000.0 ** (-jnp.arange(0, ROT_DIM, 2, dtype=jnp.float32) / ROT_DIM)
    phase = positions[..., None] * freqs
    phase = jnp.concatenate([phase, phase], -1)[..., None, :]
    return (jnp.cos(phase), jnp.sin(phase))

def doc_starts(bounds, token_index):
    return lax.optimization_barrier(jnp.max(jnp.where(bounds[:, None, :] <= token_index[None, :, None], bounds[:, None, :], 0), -1))

def exact_gelu(values):
    return jax.nn.gelu(values, approximate=False)

def reference(tokens, ln_gain, ln_bias, w_qkv, b_qkv, w_out, w_fc, b_fc, w_proj, b_out, bounds, cotangent):
    token_index = jnp.arange(LEN, dtype=jnp.int32)
    starts = doc_starts(bounds, token_index)
    cosine, sine = angles((token_index[None, :] - starts).astype(jnp.float32))
    scale = HEAD_DIM ** (-0.5)
    q_block = min(512, LEN)

    def forward(inputs, gain, shift, weight_qkv, bias_qkv, weight_out, weight_fc, bias_fc, weight_proj, bias_out):
        hidden = low(layer_norm(inputs, gain, shift))
        packed = low_back(jnp.einsum('rtd,dkf->rtkf', hidden, weight_qkv, precision=highest) + bias_qkv)
        queries = low(rotary(packed[:, :, 0].reshape(ROWS, LEN, HEADS, HEAD_DIM), cosine, sine))
        keys = low(rotary(packed[:, :, 1].reshape(ROWS, LEN, HEADS, HEAD_DIM), cosine, sine))
        values = low(packed[:, :, 2].reshape(ROWS, LEN, HEADS, HEAD_DIM))

        def attend_row(row_items):
            row_q, row_k, row_v, row_start = row_items

            def attend_block(block_index):
                first = block_index * q_block
                block_q = lax.dynamic_slice_in_dim(row_q, first, q_block, 0)
                block_start = lax.dynamic_slice_in_dim(row_start, first, q_block, 0)
                query_index = first + jnp.arange(q_block, dtype=jnp.int32)
                scores = low_back(jnp.einsum('qhd,khd->hqk', block_q, row_k, precision=highest) * scale)
                allowed = (token_index[None, :] <= query_index[:, None]) & (token_index[None, :] >= block_start[:, None])
                scores = jnp.where(allowed[None], scores, -1e+30)
                weights = jax.nn.softmax(scores, -1)
                return jnp.einsum('hqk,khd->qhd', low(weights), row_v, precision=highest)
            blocks = lax.map(jax.checkpoint(attend_block), jnp.arange(LEN // q_block, dtype=jnp.int32))
            return blocks.reshape(LEN, HEADS, HEAD_DIM)
        attended = lax.map(jax.checkpoint(attend_row), (queries, keys, values, starts))
        mixed = low(low_back(attended.reshape(ROWS, LEN, D)))
        attn_branch = jnp.einsum('rtf,fd->rtd', mixed, weight_out, precision=highest)
        inner = low_back(jnp.einsum('rtd,df->rtf', hidden, weight_fc, precision=highest) + bias_fc)
        activated = low(exact_gelu(inner))
        mlp_branch = jnp.einsum('rtf,fd->rtd', activated, weight_proj, precision=highest)
        return inputs + attn_branch + mlp_branch + bias_out
    output, pullback = jax.vjp(forward, tokens.astype(jnp.float32), ln_gain, ln_bias, w_qkv.astype(jnp.float32), b_qkv, w_out.astype(jnp.float32), w_fc.astype(jnp.float32), b_fc, w_proj.astype(jnp.float32), b_out)
    grads = pullback(cotangent.astype(jnp.float32))
    return (output.astype(jnp.bfloat16), grads[0].astype(jnp.bfloat16), grads[1], grads[2], grads[3], grads[4], grads[5], grads[6], grads[7], grads[8], grads[9])
```

```python
import functools
import jax
import jax.numpy as jnp
from jax import lax
from jax.experimental import pallas as pl
from jax.experimental.pallas import tpu as pltpu
from jax.sharding import PartitionSpec as P

HEAD_DIM = 64
ROT_DIM = 16
LANES = 128
BF = jnp.bfloat16
F32 = jnp.float32


def nt(a, b):
    return lax.dot_general(a, b, (((1,), (1,)), ((), ())), preferred_element_type=F32)


def nn(a, b):
    return lax.dot_general(a, b, (((1,), (0,)), ((), ())), preferred_element_type=F32)


def attn_kernel(bq, bk, q_ref, k_ref, v_ref, do_ref, c_ref, sa_ref, sb_ref, st_ref,
                o_ref, g_ref, q2, qt, ks, vx, s_buf, p_buf, dkt, dvt):
    length = q_ref.shape[0]
    nq = length // bq
    lane = lax.broadcasted_iota(jnp.int32, (1, LANES), 1)
    first = lane < HEAD_DIM
    half = ROT_DIM // 2
    c2 = HEAD_DIM ** (-0.5) * 1.4426950408889634

    def rot(u, rows):
        return (u * c_ref[rows, :] + pltpu.roll(u, LANES - half, 1) * sa_ref[rows, :]
                + pltpu.roll(u, half, 1) * sb_ref[rows, :])

    def rot_back(u, rows):
        return (u * c_ref[rows, :] + pltpu.roll(u * sb_ref[rows, :], LANES - half, 1)
                + pltpu.roll(u * sa_ref[rows, :], half, 1))

    def prep(i, _):
        rows = pl.ds(i * bq, bq)
        q = rot(q_ref[rows, :].astype(F32), rows)
        qs = (q * c2).astype(BF)
        zero = jnp.zeros_like(qs)
        q2[0, rows, :] = jnp.where(first, qs, zero)
        q2[1, rows, :] = jnp.where(first, zero, qs)
        qt[:, rows] = q.T.astype(BF)
        ks[rows, :] = rot(k_ref[rows, :].astype(F32), rows).astype(BF)
        vx[rows, :LANES] = v_ref[rows, :].astype(BF)
        vx[rows, LANES:] = jnp.ones((bq, LANES), BF)
        dkt[:, rows] = jnp.zeros((LANES, bq), F32)
        dvt[:, rows] = jnp.zeros((LANES, bq), F32)
        return 0

    lax.fori_loop(0, nq, prep, 0)

    def q_block(i, _):
        rows = pl.ds(i * bq, bq)
        nj = (i * bq) // bk + 1
        start = st_ref[rows, :]
        qidx = i * bq + lax.broadcasted_iota(jnp.int32, (bq, 1), 0)
        q_h = (q2[0, rows, :], q2[1, rows, :])

        def pass1(j, mx):
            cols = pl.ds(j * bk, bk)
            k = ks[cols, :]
            kidx = j * bk + lax.broadcasted_iota(jnp.int32, (1, bk), 1)
            ok = (kidx >= start) & (kidx <= qidx)
            out = []
            for h in range(2):
                s = jnp.where(ok, nt(q_h[h], k), -1e30)
                s_buf[h, :, cols] = s
                m = mx[h]
                for t in range(bk // LANES):
                    m = jnp.maximum(m, s[:, t * LANES:(t + 1) * LANES])
                out.append(m)
            return tuple(out)

        neg = jnp.full((bq, LANES), -1e30, F32)
        mx = lax.fori_loop(0, nj, pass1, (neg, neg))
        mx = [jnp.max(m, -1, keepdims=True) for m in mx]

        def pass2(j, acc):
            cols = pl.ds(j * bk, bk)
            v = vx[cols, :]
            out = []
            for h in range(2):
                p = jnp.exp2(s_buf[h, :, cols] - mx[h]).astype(BF)
                p_buf[h, :, cols] = p
                out.append(acc[h] + nn(p, v))
            return tuple(out)

        zero = jnp.zeros((bq, 2 * LANES), F32)
        acc = lax.fori_loop(0, nj, pass2, (zero, zero))
        inv = [1.0 / a[:, LANES:] for a in acc]
        outs = [a[:, :LANES] * r for a, r in zip(acc, inv)]
        o = jnp.where(first, outs[0], outs[1])
        o_ref[rows, :] = o.astype(BF)
        do = do_ref[rows, :].astype(F32)
        dos, dots, deltas = [], [], []
        for h in range(2):
            mine = first if h == 0 else jnp.logical_not(first)
            d = jnp.where(mine, do * inv[h], 0.0)
            db = d.astype(BF)
            dos.append(db)
            df = db.astype(F32)
            deltas.append(jnp.sum(df * o, -1, keepdims=True))
            dots.append(df.T[h * HEAD_DIM:(h + 1) * HEAD_DIM].astype(BF))
        q_t = qt[:, rows]

        def pass3(j, acc):
            cols = pl.ds(j * bk, bk)
            v = vx[cols, :LANES]
            k = ks[cols, :]
            out = []
            for h in range(2):
                part = slice(h * HEAD_DIM, (h + 1) * HEAD_DIM)
                p = p_buf[h, :, cols]
                dp = nt(dos[h], v)
                ds = (p.astype(F32) * (dp - deltas[h])).astype(BF)
                dvt[part, cols] += nn(dots[h], p)
                dkt[part, cols] += nn(q_t[part], ds)
                out.append(acc[h] + nn(ds, k))
            return tuple(out)

        zero = jnp.zeros((bq, LANES), F32)
        dq = lax.fori_loop(0, nj, pass3, (zero, zero))
        dq = jnp.where(first, dq[0], dq[1]) * HEAD_DIM ** (-0.5)
        g_ref[0, rows, :] = rot_back(dq, rows).astype(BF)
        return 0

    lax.fori_loop(0, nq, q_block, 0)

    def finish(i, _):
        rows = pl.ds(i * bq, bq)
        g_ref[1, rows, :] = rot_back(dkt[:, rows].T * HEAD_DIM ** (-0.5), rows).astype(BF)
        g_ref[2, rows, :] = dvt[:, rows].T.astype(BF)
        return 0

    lax.fori_loop(0, nq, finish, 0)


def attention(packed, do, cos, sa, sb, start, bq=512, bk=512):
    length, width = do.shape
    bq = min(bq, 2 ** 20 // length)
    bk = max(bq, min(bk, length))
    n = width // LANES
    blk = lambda off: pl.BlockSpec((length, LANES), lambda g: (0, off + g))
    full = lambda w: pl.BlockSpec((length, w), lambda g: (0, 0))
    out = jax.ShapeDtypeStruct((length, width), BF)
    return pl.pallas_call(
        functools.partial(attn_kernel, bq, bk),
        grid=(n,),
        out_shape=[out, jax.ShapeDtypeStruct((3, length, width), BF)],
        in_specs=[blk(0), blk(n), blk(2 * n), blk(0), full(LANES), full(LANES), full(LANES), full(1)],
        out_specs=[blk(0), pl.BlockSpec((3, length, LANES), lambda g: (0, 0, g))],
        scratch_shapes=[
            pltpu.VMEM((2, length, LANES), BF),
            pltpu.VMEM((LANES, length), BF),
            pltpu.VMEM((length, LANES), BF),
            pltpu.VMEM((length, 2 * LANES), BF),
            pltpu.VMEM((2, bq, length), F32),
            pltpu.VMEM((2, bq, length), BF),
            pltpu.VMEM((LANES, length), F32),
            pltpu.VMEM((LANES, length), F32),
        ],
        compiler_params=pltpu.CompilerParams(vmem_limit_bytes=50 * 1024 * 1024),
        cost_estimate=pl.CostEstimate(flops=12 * length * length * width // 2 * 4, bytes_accessed=length * width * 22, transcendentals=length * length * n),
    )(packed, packed, packed, do, cos, sa, sb, start)


EPSILON = 1e-05


def normalize(values):
    center = values - jnp.mean(values, -1, keepdims=True)
    spread = jnp.mean(center * center, -1, keepdims=True)
    scale = lax.rsqrt(spread + EPSILON)
    return center * scale, scale


def exact_gelu(values):
    return jax.nn.gelu(values, approximate=False)


def rotary_tables(position):
    half = ROT_DIM // 2
    freqs = 10000.0 ** (-jnp.arange(0, ROT_DIM, 2, dtype=F32) / ROT_DIM)
    phase = position[:, None].astype(F32) * freqs
    cosine, sine = jnp.cos(phase), jnp.sin(phase)
    length = position.shape[0]
    rest = HEAD_DIM - ROT_DIM
    zero, one = jnp.zeros((length, half), F32), jnp.ones((length, rest), F32)
    keep = jnp.concatenate([cosine, cosine, one] * 2, 1)
    ahead = jnp.concatenate([-sine, zero, 0 * one] * 2, 1)
    behind = jnp.concatenate([zero, sine, 0 * one] * 2, 1)
    return keep, ahead, behind


def swap(value):
    return lax.ppermute(value, "tensor", [(0, 1), (1, 0)])


def split_tensor(value, axis):
    shape = value.shape
    parts = lax.axis_size("tensor")
    return value.reshape(shape[:axis] + (parts, shape[axis] // parts) + shape[axis + 1:])


def own_part(value, axis):
    return lax.dynamic_index_in_dim(
        split_tensor(value, axis), lax.axis_index("tensor"), axis, keepdims=False
    )


def sum_parts(value, axis):
    parts = lax.axis_size("tensor")
    mine = lax.axis_index("tensor")
    pieces = split_tensor(value, axis)
    if parts == 2:
        other = lax.dynamic_index_in_dim(pieces, 1 - mine, axis, keepdims=False).astype(BF)
        own = lax.dynamic_index_in_dim(pieces, mine, axis, keepdims=False)
        return own.astype(F32) + swap(other).astype(F32)
    return lax.psum_scatter(
        value.astype(BF), "tensor", scatter_dimension=axis, tiled=True
    ).astype(F32)


def join_parts(value, axis):
    parts = lax.axis_size("tensor")
    if parts != 2:
        return lax.all_gather(value, "tensor", axis=axis, tiled=True)
    other = swap(value)
    first = lax.axis_index("tensor") == 0
    low, high = jnp.where(first, value, other), jnp.where(first, other, value)
    return jnp.concatenate([low, high], axis)


def to_rows(value):
    blocks = lax.axis_size("blk")
    pad = jnp.zeros((blocks - value.shape[0],) + value.shape[1:], value.dtype)
    return lax.all_to_all(jnp.concatenate([value, pad], 0), "blk", 0, 0, tiled=True)


def to_blocks(value, rows):
    return lax.all_to_all(value, "blk", 0, 0, tiled=True)[:rows]


def local(
    tokens, ln_gain, ln_bias, w_qkv, b_qkv, w_out, w_fc, b_fc, w_proj, b_out, bounds, cotangent
):
    rows, group, model = tokens.shape
    width = b_qkv.shape[1]
    blocks = lax.axis_size("blk")
    length = blocks * group

    full_out = lax.all_gather(w_out, ("dp", "blk"), axis=1, tiled=True)
    full_qkv = lax.all_gather(w_qkv, ("dp", "blk"), axis=0, tiled=True)
    full_fc = lax.all_gather(w_fc, ("dp", "blk"), axis=0, tiled=True)
    full_proj = lax.all_gather(w_proj, ("dp", "blk"), axis=1, tiled=True)

    hidden = (normalize(tokens.astype(F32))[0] * ln_gain + ln_bias).astype(BF)

    row_hidden = join_parts(to_rows(own_part(hidden, 1)), 1).reshape(length, model)
    row_bounds = lax.dynamic_index_in_dim(
        bounds, jnp.minimum(lax.axis_index("blk"), rows - 1), 0, keepdims=False
    )
    index = jnp.arange(length, dtype=jnp.int32)
    start = jnp.max(jnp.where(row_bounds[None] <= index[:, None], row_bounds[None], 0), -1)
    tables = rotary_tables(index - start)
    packed = (
        jnp.dot(row_hidden, full_qkv.reshape(model, 3 * width), preferred_element_type=F32)
        + b_qkv.reshape(-1)
    )
    grad_mixed = jnp.einsum("rcd,fd->rcf", cotangent, full_out, preferred_element_type=F32).astype(BF)
    row_grad = to_rows(grad_mixed).reshape(length, width)
    attended, grad_packed = attention(packed, row_grad, *tables, start[:, None])
    mixed = to_blocks(attended.reshape(blocks, group, width), rows)
    grad_bqkv = jnp.sum(grad_packed.astype(F32), 1)
    grad_wqkv = jnp.einsum("ld,clf->dcf", row_hidden, grad_packed, preferred_element_type=F32)
    row_back = jnp.einsum("clf,dcf->ld", grad_packed, full_qkv, preferred_element_type=F32)
    back = sum_parts(row_back.reshape(blocks, group, model), 1).astype(BF)
    back = to_blocks(back, rows).astype(F32)

    inner = jnp.einsum("rcd,df->rcf", hidden, full_fc, preferred_element_type=F32) + b_fc
    activated_f, gelu_back = jax.vjp(exact_gelu, inner)
    activated = activated_f.astype(BF)
    partial = jnp.einsum("rcf,fd->rcd", mixed, full_out, preferred_element_type=F32) + jnp.einsum(
        "rcf,fd->rcd", activated, full_proj, preferred_element_type=F32
    )
    own_tokens = own_part(tokens, 1).astype(F32)
    result = join_parts((sum_parts(partial, 1) + own_tokens + b_out).astype(BF), 1)

    grad_proj = jnp.einsum("rcf,rcd->fd", activated, cotangent, preferred_element_type=F32)
    grad_wout = jnp.einsum("rcf,rcd->fd", mixed, cotangent, preferred_element_type=F32)
    grad_act = jnp.einsum("rcd,fd->rcf", cotangent, full_proj, preferred_element_type=F32)
    grad_inner = gelu_back(grad_act)[0].astype(BF)
    grad_bfc = jnp.sum(grad_inner.astype(F32), (0, 1))
    grad_wfc = jnp.einsum("rcd,rcf->df", hidden, grad_inner, preferred_element_type=F32)
    mlp_back = jnp.einsum("rcf,df->rcd", grad_inner, full_fc, preferred_element_type=F32)
    grad_hidden = sum_parts(mlp_back, 1) + back

    normal, scale = normalize(own_tokens)
    own_cot = own_part(cotangent, 1).astype(F32)
    grad_gain = jnp.sum(grad_hidden * normal, (0, 1))
    grad_shift = jnp.sum(grad_hidden, (0, 1))
    grad_normal = grad_hidden * ln_gain
    grad_inputs = scale * (
        grad_normal
        - jnp.mean(grad_normal, -1, keepdims=True)
        - normal * jnp.mean(grad_normal * normal, -1, keepdims=True)
    )
    grad_tokens = join_parts((own_cot + grad_inputs).astype(BF), 1)
    grad_bout = jnp.sum(own_cot, (0, 1))

    def scatter(value, axis):
        return lax.psum_scatter(
            value.astype(BF), ("dp", "blk"), scatter_dimension=axis, tiled=True
        ).astype(F32)

    out_wqkv, out_wout = scatter(grad_wqkv, 0), scatter(grad_wout, 1)
    out_wfc, out_proj = scatter(grad_wfc, 0), scatter(grad_proj, 1)
    grad_gain, grad_shift, grad_bout = lax.psum(
        (grad_gain, grad_shift, grad_bout), ("dp", "blk", "tensor")
    )
    grad_bqkv, grad_bfc = lax.psum((grad_bqkv, grad_bfc), ("dp", "blk"))
    return (
        result,
        grad_tokens,
        grad_gain,
        grad_shift,
        out_wqkv,
        grad_bqkv,
        out_wout,
        out_wfc,
        grad_bfc,
        out_proj,
        grad_bout,
    )


def solution(mesh):
    in_specs = (
        P("dp", "blk", None),
        P(),
        P(),
        P(("dp", "blk"), None, "tensor"),
        P(None, "tensor"),
        P("tensor", ("dp", "blk")),
        P(("dp", "blk"), "tensor"),
        P("tensor"),
        P("tensor", ("dp", "blk")),
        P(),
        P("dp", None),
        P("dp", "blk", None),
    )
    out_specs = (
        P("dp", "blk", None),
        P("dp", "blk", None),
        P(),
        P(),
        P(("dp", "blk"), None, "tensor"),
        P(None, "tensor"),
        P("tensor", ("dp", "blk")),
        P(("dp", "blk"), "tensor"),
        P("tensor"),
        P("tensor", ("dp", "blk")),
        P(),
    )
    return jax.shard_map(local, mesh=mesh, in_specs=in_specs, out_specs=out_specs, check_vma=False)
```

```python
import functools

import jax
import jax.numpy as jnp
from jax import lax
from jax.experimental import pallas as pl
from jax.experimental.pallas import tpu as pltpu
from jax.sharding import PartitionSpec as P

HEAD_DIM = 64
ROT_DIM = 16
LANES = 128
EPSILON = 1e-05
BF = jnp.bfloat16
F32 = jnp.float32
MIB = 1024 * 1024


def nt(a, b):
    return lax.dot_general(a, b, (((1,), (1,)), ((), ())), preferred_element_type=F32)


def nn(a, b):
    return lax.dot_general(a, b, (((1,), (0,)), ((), ())), preferred_element_type=F32)


def attn_kernel(bq, bk, part, waits, lo_ref, hi_ref, *refs):
    count = 2 if part else 1
    hidden, refs = refs[:count], refs[count + waits:]
    w_ref, bias_ref, do_ref, cos_ref, sin_ref, start_ref, o_ref = refs[:7]
    grads, refs = refs[7:7 + count], refs[7 + count:]
    (q2, qt, ks, vx, s_buf, p_buf, d_buf, dkt, dvt, keep, ahead, behind, starts) = refs
    length = do_ref.shape[0]
    nq = length // bq
    lane = lax.broadcasted_iota(jnp.int32, (1, LANES), 1)
    first = lane < HEAD_DIM
    half = ROT_DIM // 2
    to_score = HEAD_DIM ** (-0.5) * 1.4426950408889634
    mine_first = lax.axis_index("tensor") == 0 if part else None

    def load(base, size):
        if part:
            rows = []
            for n in range(size // (2 * part)):
                at = pl.ds(pl.multiple_of(base // 2 + n * part, part), part)
                a, b = hidden[0][at, :], hidden[1][at, :]
                rows += [jnp.where(mine_first, a, b), jnp.where(mine_first, b, a)]
            rows = jnp.concatenate(rows, 0)
        else:
            rows = hidden[0][pl.ds(base, size), :]
        packed = nn(rows, w_ref[...]) + bias_ref[...]
        return [packed[:, n * LANES:(n + 1) * LANES] for n in range(3)]

    def store(base, which, value):
        cols = slice(which * LANES, (which + 1) * LANES)
        size = value.shape[0]
        if not part:
            grads[0][pl.ds(base, size), cols] = value.astype(BF)
            return
        for n in range(size // (2 * part)):
            at = pl.ds(pl.multiple_of(base // 2 + n * part, part), part)
            a = value[2 * n * part:(2 * n + 1) * part]
            b = value[(2 * n + 1) * part:(2 * n + 2) * part]
            grads[0][at, cols] = jnp.where(mine_first, a, b).astype(BF)
            grads[1][at, cols] = jnp.where(mine_first, b, a).astype(BF)

    def rot(u, rows):
        return (u * keep[rows, :] + pltpu.roll(u, LANES - half, 1) * ahead[rows, :]
                + pltpu.roll(u, half, 1) * behind[rows, :])

    def rot_back(u, rows):
        return (u * keep[rows, :] + pltpu.roll(u * behind[rows, :], LANES - half, 1)
                + pltpu.roll(u * ahead[rows, :], half, 1))

    def tables(i, _):
        rows = pl.ds(pl.multiple_of(i * bq, bq), bq)
        c, s = cos_ref[:, rows], sin_ref[:, rows]
        rest = HEAD_DIM - ROT_DIM
        one, zero, gap = jnp.ones((rest, bq), F32), jnp.zeros((rest, bq), F32), jnp.zeros((half, bq), F32)
        keep[rows, :] = jnp.concatenate([c, c, one] * 2, 0).T
        ahead[rows, :] = jnp.concatenate([-s, gap, zero] * 2, 0).T
        behind[rows, :] = jnp.concatenate([gap, s, zero] * 2, 0).T
        starts[rows, :] = jnp.broadcast_to(start_ref[:, rows], (LANES, bq)).T
        return 0

    @pl.when(pl.program_id(0) == 0)
    def _():
        lax.fori_loop(0, nq, tables, 0)

    def prep(i, _):
        base = pl.multiple_of(i * bq, bq)
        rows = pl.ds(base, bq)
        q, k, v = load(base, bq)
        q = rot(q, rows)
        qs = (q * to_score).astype(BF)
        zero = jnp.zeros_like(qs)
        q2[0, rows, :] = jnp.where(first, qs, zero)
        q2[1, rows, :] = jnp.where(first, zero, qs)
        qt[:, rows] = q.T.astype(BF)
        ks[rows, :] = rot(k, rows).astype(BF)
        vx[rows, :LANES] = v.astype(BF)
        vx[rows, LANES:] = jnp.ones((bq, LANES), BF)
        dkt[:, rows] = jnp.zeros((LANES, bq), F32)
        dvt[:, rows] = jnp.zeros((LANES, bq), F32)
        return 0

    lax.fori_loop(0, nq, prep, 0)

    def q_block(i, _):
        rows = pl.ds(pl.multiple_of(i * bq, bq), bq)
        last = (i * bq) // bk
        least = lo_ref[i] // bk
        masked = jnp.clip((hi_ref[i] + bk - 1) // bk, least, last)
        q_h = (q2[0, rows, :], q2[1, rows, :])
        start = starts[rows, :]

        def scores(j, mx, mode):
            cols = pl.ds(pl.multiple_of(j * bk, bk), bk)
            k = ks[cols, :]
            out = []
            for h in range(2):
                s = nt(q_h[h], k)
                m = mx[h]
                for t in range(bk // LANES):
                    piece = s[:, t * LANES:(t + 1) * LANES]
                    if mode:
                        kidx = (j * bk + t * LANES + lane).astype(F32)
                        ok = kidx >= start
                        if mode == 2:
                            qidx = (i * bq + lax.broadcasted_iota(jnp.int32, (bq, 1), 0)).astype(F32)
                            ok = ok & (kidx <= qidx)
                        piece = jnp.where(ok, piece, -1e30)
                    s_buf[h, :, pl.ds(pl.multiple_of(j * bk + t * LANES, LANES), LANES)] = piece
                    m = jnp.maximum(m, piece)
                out.append(m)
            return tuple(out)

        mx = (jnp.full((bq, LANES), -1e30, F32),) * 2
        mx = lax.fori_loop(least, masked, lambda j, m: scores(j, m, 1), mx)
        mx = lax.fori_loop(masked, last, lambda j, m: scores(j, m, 0), mx)
        mx = scores(last, mx, 2)
        mx = [jnp.max(m, -1, keepdims=True) for m in mx]

        def weigh(j, acc):
            cols = pl.ds(pl.multiple_of(j * bk, bk), bk)
            v = vx[cols, :]
            out = []
            for h in range(2):
                p = jnp.exp2(s_buf[h, :, cols] - mx[h]).astype(BF)
                p_buf[h, :, cols] = p
                out.append(acc[h] + nn(p, v))
            return tuple(out)

        acc = (jnp.zeros((bq, 2 * LANES), F32),) * 2
        acc = lax.fori_loop(least, last + 1, weigh, acc)
        inv = [1.0 / a[:, LANES:] for a in acc]
        outs = [a[:, :LANES] * r for a, r in zip(acc, inv)]
        o = jnp.where(first, outs[0], outs[1])
        o_ref[rows, :] = o.astype(BF)
        do = do_ref[rows, :].astype(F32)
        dos, dots, deltas = [], [], []
        for h in range(2):
            mine = first if h == 0 else jnp.logical_not(first)
            d = jnp.where(mine, do * inv[h], 0.0).astype(BF)
            dos.append(d)
            df = d.astype(F32)
            deltas.append(jnp.sum(df * o, -1, keepdims=True))
            dots.append(df.T[h * HEAD_DIM:(h + 1) * HEAD_DIM].astype(BF))
        q_t = qt[:, rows]

        def back(j, acc):
            cols = pl.ds(pl.multiple_of(j * bk, bk), bk)
            v = vx[cols, :LANES]
            k = ks[cols, :]
            out = []
            for h in range(2):
                rows_h = slice(h * HEAD_DIM, (h + 1) * HEAD_DIM)
                p = p_buf[h, :, cols]
                dp = nt(dos[h], v)
                ds = (p.astype(F32) * (dp - deltas[h])).astype(BF)
                dvt[rows_h, cols] += nn(dots[h], p)
                dkt[rows_h, cols] += nn(q_t[rows_h], ds)
                out.append(acc[h] + nn(ds, k))
            return tuple(out)

        acc = (jnp.zeros((bq, LANES), F32),) * 2
        acc = lax.fori_loop(least, last + 1, back, acc)
        dq = jnp.where(first, acc[0], acc[1]) * HEAD_DIM ** (-0.5)
        store(i * bq, 0, rot_back(dq, rows))
        return 0

    def static_block(i):
        rows = slice(i * bq, (i + 1) * bq)
        width = (i + 1) * bq
        start = starts[rows, :]
        q_h = (q2[0, rows, :], q2[1, rows, :])
        mx = []
        for h in range(2):
            m = jnp.full((bq, LANES), -1e30, F32)
            for j in range(0, width, bk):
                s = nt(q_h[h], ks[j:j + bk, :])
                for t in range(0, bk, LANES):
                    kidx = (j + t + lane).astype(F32)
                    ok = kidx >= start
                    if j + t + LANES > i * bq:
                        qidx = (i * bq + lax.broadcasted_iota(jnp.int32, (bq, 1), 0)).astype(F32)
                        ok = ok & (kidx <= qidx)
                    piece = jnp.where(ok, s[:, t:t + LANES], -1e30)
                    s_buf[h, :, j + t:j + t + LANES] = piece
                    m = jnp.maximum(m, piece)
            mx.append(jnp.broadcast_to(jnp.max(m, -1, keepdims=True), (bq, LANES)))
        acc = []
        for h in range(2):
            for t in range(0, width, LANES):
                p_buf[h, :, t:t + LANES] = jnp.exp2(s_buf[h, :, t:t + LANES] - mx[h]).astype(BF)
            acc.append(nn(p_buf[h, :, :width], vx[:width, :]))
        inv = [1.0 / v[:, LANES:] for v in acc]
        outs = [v[:, :LANES] * r for v, r in zip(acc, inv)]
        o = jnp.where(first, outs[0], outs[1])
        o_ref[rows, :] = o.astype(BF)
        do = do_ref[rows, :].astype(F32)
        dq = []
        for h in range(2):
            mine = first if h == 0 else jnp.logical_not(first)
            rows_h = slice(h * HEAD_DIM, (h + 1) * HEAD_DIM)
            d = jnp.where(mine, do * inv[h], 0.0).astype(BF)
            df = d.astype(F32)
            delta = jnp.broadcast_to(jnp.sum(df * o, -1, keepdims=True), (bq, LANES))
            d_t = df.T[rows_h].astype(BF)
            q_t = qt[rows_h, rows]
            for j in range(0, width, bk):
                cols = slice(j, j + bk)
                dp = nt(d, vx[cols, :LANES])
                dvt[rows_h, cols] += nn(d_t, p_buf[h, :, cols])
                for t in range(0, bk, LANES):
                    at = slice(j + t, j + t + LANES)
                    d_buf[h, :, at] = (p_buf[h, :, at].astype(F32) * (dp[:, t:t + LANES] - delta)).astype(BF)
                dkt[rows_h, cols] += nn(q_t, d_buf[h, :, cols])
            dq.append(nn(d_buf[h, :, :width], ks[:width, :]))
        dq = jnp.where(first, dq[0], dq[1]) * HEAD_DIM ** (-0.5)
        store(i * bq, 0, rot_back(dq, rows))

    if nq <= 4:
        for i in range(nq):
            static_block(i)
    else:
        lax.fori_loop(0, nq, q_block, 0)

    def finish(i, _):
        base = pl.multiple_of(i * bq, bq)
        rows = pl.ds(base, bq)
        store(base, 1, rot_back(dkt[:, rows].T * HEAD_DIM ** (-0.5), rows))
        store(base, 2, dvt[:, rows].T)
        return 0

    lax.fori_loop(0, nq, finish, 0)


def attention(hidden, weights, bias, first_pair, do, position, start, part=0, waits=(), bq=512, bk=512):
    length, width = do.shape
    bq = min(bq, 2 ** 20 // length)
    bk = max(bq, min(bk, length))
    pairs = width // LANES
    freqs = 10000.0 ** (-jnp.arange(0, ROT_DIM, 2, dtype=F32) / ROT_DIM)
    phase = position.astype(F32)[None] * freqs[:, None]
    by_block = start.reshape(length // bq, bq)
    rows, model = hidden[0].shape
    once = pl.Buffered(1)
    columns = pl.BlockSpec((length, LANES), lambda g, *_: (0, g))
    triple = pl.BlockSpec((rows, 3 * LANES), lambda g, *_: (0, g))
    whole = lambda n: pl.BlockSpec((n, length), lambda g, *_: (0, 0), pipeline_mode=once)
    tri_out = jax.ShapeDtypeStruct((rows, 3 * width), BF)
    static = length // bq <= 4
    out = pl.pallas_call(
        functools.partial(attn_kernel, bq, bk, part, len(waits)),
        out_shape=[jax.ShapeDtypeStruct((length, width), BF)] + [tri_out] * len(hidden),
        grid_spec=pltpu.PrefetchScalarGridSpec(
            num_scalar_prefetch=2,
            grid=(pairs,),
            in_specs=[pl.BlockSpec((rows, model), lambda g, *_: (0, 0), pipeline_mode=once)] * len(hidden)
            + [pl.BlockSpec(memory_space=pl.ANY)] * len(waits)
            + [
                pl.BlockSpec((model, 3 * LANES), lambda g, *_: (0, first_pair + g)),
                pl.BlockSpec((1, 3 * LANES), lambda g, *_: (0, first_pair + g)),
                columns, whole(ROT_DIM // 2), whole(ROT_DIM // 2), whole(1),
            ],
            out_specs=[columns] + [triple] * len(hidden),
            scratch_shapes=[
                pltpu.VMEM((2, length, LANES), BF),
                pltpu.VMEM((LANES, length), BF),
                pltpu.VMEM((length, LANES), BF),
                pltpu.VMEM((length, 2 * LANES), BF),
                pltpu.VMEM((2, bq, length), F32),
                pltpu.VMEM((2, bq, length), BF),
                pltpu.VMEM((2, bq, length) if static else (8, LANES), BF),
                pltpu.VMEM((LANES, length), F32),
                pltpu.VMEM((LANES, length), F32),
            ] + [pltpu.VMEM((length, LANES), F32)] * 4,
        ),
        compiler_params=pltpu.CompilerParams(vmem_limit_bytes=56 * MIB),
        cost_estimate=pl.CostEstimate(flops=1000, bytes_accessed=1000, transcendentals=0),
    )(by_block.min(1), by_block.max(1), *hidden, *waits, weights, bias, do, jnp.cos(phase), jnp.sin(phase),
      start.astype(F32)[None])
    return out[0], list(out[1:])


def gather_kernel(x_ref, out_ref, local_sem, recv, up, down, across, over):
    size = x_ref.shape[0]
    core, block = lax.axis_index("dp"), lax.axis_index("blk")
    z, y = block // 2, lax.rem(block, 2)
    depth = lax.axis_size("blk") // 2
    above, below = {"blk": block + 2}, {"blk": block - 2}
    beside, sibling = {"blk": block + 1 - 2 * y}, {"dp": 1 - core}

    def place(c, zz, yy):
        return (c * depth + zz) * 2 + yy

    def chunk(at):
        return out_ref.at[pl.ds(pl.multiple_of(at * size, size), size)]

    def copy(src, at, sem, target):
        return pltpu.make_async_remote_copy(
            src_ref=src, dst_ref=chunk(at), send_sem=sem, recv_sem=recv.at[at],
            device_id=target, device_id_type=pl.DeviceIdType.MESH,
        )

    def arrived(at):
        copy(chunk(at), at, local_sem, sibling).wait_recv()

    barrier = pltpu.get_barrier_semaphore()

    def greet(target):
        pl.semaphore_signal(barrier, inc=1, device_id=target, device_id_type=pl.DeviceIdType.MESH)

    def not_top(action):
        pl.when(z < depth - 1)(action)

    def not_bottom(action):
        pl.when(z > 0)(action)

    not_top(lambda: greet(above))
    not_bottom(lambda: greet(below))
    greet(beside)
    greet(sibling)
    pl.semaphore_wait(barrier, 2 + jnp.where(z > 0, 1, 0) + jnp.where(z < depth - 1, 1, 0))

    mine = place(core, z, y)
    keep = pltpu.make_async_copy(x_ref, chunk(mine), local_sem)
    not_top(lambda: copy(x_ref, mine, up.at[z], above).start())
    not_bottom(lambda: copy(x_ref, mine, down.at[z], below).start())
    copy(x_ref, mine, across.at[z], beside).start()
    copy(x_ref, mine, over.at[z * 2 + y], sibling).start()
    keep.start()

    def from_beside(zz):
        at = place(core, zz, 1 - y)
        arrived(at)
        copy(chunk(at), at, over.at[zz * 2 + 1 - y], sibling).start()

    def from_line(zz, onward, sems, target):
        at = place(core, zz, y)
        arrived(at)
        onward(lambda: copy(chunk(at), at, sems.at[zz], target).start())
        copy(chunk(at), at, across.at[zz], beside).start()
        copy(chunk(at), at, over.at[zz * 2 + y], sibling).start()

    for step in range(1, depth):
        pl.when(z >= step)(lambda: from_line(z - step, not_top, up, above))
        pl.when(z + step < depth)(lambda: from_line(z + step, not_bottom, down, below))
    from_beside(z)
    for step in range(1, depth):
        pl.when(z >= step)(lambda: from_beside(z - step))
        pl.when(z + step < depth)(lambda: from_beside(z + step))

    keep.wait()
    for zz in range(depth):
        for yy in range(2):
            arrived(place(1 - core, zz, yy))
            copy(x_ref, mine, over.at[zz * 2 + yy], sibling).wait_send()
        copy(x_ref, mine, across.at[zz], beside).wait_send()
        pl.when((zz <= z) & (z < depth - 1))(lambda: copy(x_ref, mine, up.at[zz], above).wait_send())
        pl.when((zz >= z) & (z > 0))(lambda: copy(x_ref, mine, down.at[zz], below).wait_send())


def gather_weights(shard):
    cores, blocks = lax.axis_size("dp"), lax.axis_size("blk")
    if (cores, blocks) != (2, 8):
        return lax.all_gather(shard, ("dp", "blk"), axis=0, tiled=True)
    rows, columns = shard.shape
    dma = pltpu.SemaphoreType.DMA
    return pl.pallas_call(
        gather_kernel,
        out_shape=jax.ShapeDtypeStruct((cores * blocks * rows, columns), shard.dtype),
        in_specs=[pl.BlockSpec(memory_space=pl.ANY)],
        out_specs=pl.BlockSpec(memory_space=pl.ANY),
        scratch_shapes=[
            dma, dma((cores * blocks,)), dma((blocks // 2,)), dma((blocks // 2,)),
            dma((blocks // 2,)), dma((blocks,)),
        ],
        compiler_params=pltpu.CompilerParams(collective_id=0, has_side_effects=True),
    )(shard)


def weight_grad_kernel(half, waits, a_ref, b_ref, *refs):
    x_ref, y_ref, out_ref, turned = refs[waits:]
    step = pl.program_id(0)

    @pl.when(step == 0)
    def _():
        turned[...] = a_ref[...].T

    @pl.when(step == half)
    def _():
        turned[...] = b_ref[...].T

    @pl.when(step < half)
    def _():
        out_ref[...] = nn(turned[...], x_ref[...]).astype(BF)

    @pl.when(step >= half)
    def _():
        out_ref[...] = nn(turned[...], y_ref[...]).astype(BF)


def weight_grads(a, x, b, y, waits=(), tile=512):
    count, model = a.shape
    inner = x.shape[1]
    tile = min(tile, inner)
    half = inner // tile
    whole = pl.BlockSpec((count, model), lambda i: (0, 0), pipeline_mode=pl.Buffered(1))
    return pl.pallas_call(
        functools.partial(weight_grad_kernel, half, len(waits)),
        grid=(2 * half,),
        out_shape=jax.ShapeDtypeStruct((model, 2 * inner), BF),
        in_specs=[
            whole, whole, *[pl.BlockSpec(memory_space=pl.ANY)] * len(waits),
            pl.BlockSpec((count, tile), lambda i: (0, jnp.minimum(i, half - 1))),
            pl.BlockSpec((count, tile), lambda i: (0, jnp.maximum(i - half, 0))),
        ],
        out_specs=pl.BlockSpec((model, tile), lambda i: (0, i)),
        scratch_shapes=[pltpu.VMEM((model, count), BF)],
        compiler_params=pltpu.CompilerParams(vmem_limit_bytes=48 * MIB),
        cost_estimate=pl.CostEstimate(flops=1000, bytes_accessed=1000, transcendentals=0),
    )(a, b, *waits, x, y)


def back_kernel(waits, g_ref, w_ref, *refs):
    out_ref = refs[waits]
    out_ref[...] = nt(g_ref[...], w_ref[...]).astype(BF)


def input_grad(grad, weights, waits=(), size=256):
    count, depth = grad.shape
    model = weights.shape[0]
    return pl.pallas_call(
        functools.partial(back_kernel, len(waits)),
        grid=(count // size,),
        out_shape=jax.ShapeDtypeStruct((count, model), BF),
        in_specs=[
            pl.BlockSpec((size, depth), lambda i: (i, 0)),
            pl.BlockSpec((model, depth), lambda i: (0, 0), pipeline_mode=pl.Buffered(1)),
            *[pl.BlockSpec(memory_space=pl.ANY)] * len(waits),
        ],
        out_specs=pl.BlockSpec((size, model), lambda i: (i, 0)),
        compiler_params=pltpu.CompilerParams(vmem_limit_bytes=32 * MIB),
        cost_estimate=pl.CostEstimate(flops=1000, bytes_accessed=1000, transcendentals=0),
    )(grad, weights, *waits)


def mlp_kernel(tile, waits, hid_ref, cot_ref, wf_ref, wp_ref, bias_ref, *refs):
    act_ref, gin_ref, res_ref, back_ref, gb_ref = refs[waits:]
    hid, cot = hid_ref[...], cot_ref[...]

    @pl.when(pl.program_id(0) == 0)
    def _():
        gb_ref[...] = jnp.zeros_like(gb_ref)

    res = back = None
    for n in range(wf_ref.shape[1] // tile):
        cols = slice(n * tile, (n + 1) * tile)
        wf, wp = wf_ref[:, cols], wp_ref[:, cols]
        inner = nn(hid, wf) + bias_ref[:, cols]
        grad_act = nn(cot, wp)
        size = jnp.abs(inner)
        t = 1.0 / (1.0 + (0.3275911 * 0.7071067811865476) * size)
        bell = jnp.exp2((-0.5 * 1.4426950408889634) * inner * inner)
        tail = ((((0.5 * 1.061405429 * t - 0.5 * 1.453152027) * t + 0.5 * 1.421413741) * t
                 - 0.5 * 0.284496736) * t + 0.5 * 0.254829592) * t * bell
        below = jnp.where(inner < 0, tail, 1.0 - tail)
        act = (inner * below).astype(BF)
        grad_inner = (grad_act * (below + inner * (bell * 0.3989422804014327))).astype(BF)
        act_ref[:, cols] = act
        gin_ref[:, cols] = grad_inner
        gb_ref[:, cols] += jnp.sum(grad_inner.astype(F32), 0, keepdims=True)
        r, b = nt(act, wp), nt(grad_inner, wf)
        res, back = (r, b) if res is None else (res + r, back + b)
    res_ref[...] = res.astype(BF)
    back_ref[...] = back.astype(BF)


def mlp(hidden, cot, weights, first_block, bias, waits=(), size=256, tile=512):
    count, model = hidden.shape
    inner = bias.shape[1]
    tile = min(tile, inner)
    rows = lambda n: pl.BlockSpec((size, n), lambda i: (i, 0))
    matrix = lambda n: pl.BlockSpec((model, inner), lambda i: (0, first_block + n), pipeline_mode=pl.Buffered(1))
    vector = pl.BlockSpec((1, inner), lambda i: (0, 0))
    shape = lambda n: jax.ShapeDtypeStruct((count, n), BF)
    return pl.pallas_call(
        functools.partial(mlp_kernel, tile, len(waits)),
        grid=(count // size,),
        out_shape=[shape(inner), shape(inner), shape(model), shape(model), jax.ShapeDtypeStruct((1, inner), F32)],
        in_specs=[rows(model), rows(model), matrix(0), matrix(1), vector]
        + [pl.BlockSpec(memory_space=pl.ANY)] * len(waits),
        out_specs=[rows(inner), rows(inner), rows(model), rows(model), vector],
        compiler_params=pltpu.CompilerParams(vmem_limit_bytes=56 * MIB),
        cost_estimate=pl.CostEstimate(flops=1000, bytes_accessed=1000, transcendentals=0),
    )(hidden, cot, weights, weights, bias, *waits)


def normalize(values):
    center = values - jnp.mean(values, -1, keepdims=True)
    spread = jnp.mean(center * center, -1, keepdims=True)
    scale = lax.rsqrt(spread + EPSILON)
    return center * scale, scale


def swap(value):
    return lax.ppermute(value, "tensor", [(0, 1), (1, 0)])


def split_tensor(value, axis):
    shape = value.shape
    parts = lax.axis_size("tensor")
    return value.reshape(shape[:axis] + (parts, shape[axis] // parts) + shape[axis + 1:])


def part_of(value, axis, which):
    return lax.dynamic_index_in_dim(split_tensor(value, axis), which, axis, keepdims=False)


def sum_parts(value, axis):
    mine = lax.axis_index("tensor")
    if lax.axis_size("tensor") == 2:
        other = swap(part_of(value, axis, 1 - mine).astype(BF))
        return part_of(value, axis, mine).astype(F32) + other.astype(F32)
    return lax.psum_scatter(
        value.astype(BF), "tensor", scatter_dimension=axis, tiled=True
    ).astype(F32)


def join_parts(value, axis):
    if lax.axis_size("tensor") != 2:
        return lax.all_gather(value, "tensor", axis=axis, tiled=True)
    other = swap(value)
    first = lax.axis_index("tensor") == 0
    low, high = jnp.where(first, value, other), jnp.where(first, other, value)
    return jnp.concatenate([low, high], axis)


def to_rows(value):
    blocks = lax.axis_size("blk")
    pad = jnp.zeros((blocks - value.shape[0],) + value.shape[1:], value.dtype)
    return lax.all_to_all(jnp.concatenate([value, pad], 0), "blk", 0, 0, tiled=True)


def to_blocks(value, rows):
    return lax.all_to_all(value, "blk", 0, 0, tiled=True)[:rows]


def sum_all(value, axes):
    for axis in axes:
        size = lax.axis_size(axis)
        step = 1
        while step < size:
            value = value + lax.ppermute(value, axis, [(i, i ^ step) for i in range(size)])
            step *= 2
    return value


def by_pair(value, width):
    count = value.shape[0]
    return value.reshape(count, 3, width // LANES, LANES).transpose(0, 2, 1, 3).reshape(count, 3 * width)


def by_kind(value, width):
    count = value.shape[0]
    return value.reshape(count, width // LANES, 3, LANES).transpose(0, 2, 1, 3).reshape(count, 3, width)


def scatter(value):
    return lax.psum_scatter(value, ("dp", "blk"), scatter_dimension=0, tiled=True).astype(F32)


def dot(a, b):
    return jnp.dot(a, b, preferred_element_type=F32)


def local(
    tokens, ln_gain, ln_bias, w_qkv, b_qkv, w_out, w_fc, b_fc, w_proj, b_out, bounds, cotangent
):
    rows, group, model = tokens.shape
    width, inner = b_qkv.shape[1], b_fc.shape[0]
    blocks, parts = lax.axis_size("blk"), lax.axis_size("tensor")
    length = blocks * group
    count = rows * group
    part = group // parts

    mine = lax.axis_index("tensor")
    pair = parts == 2
    hidden = (normalize(tokens.astype(F32))[0] * ln_gain + ln_bias).astype(BF)
    flat_hidden, cot = hidden.reshape(count, model), cotangent.reshape(count, model)

    shard = jnp.concatenate([by_pair(w_qkv, width), w_out.T, w_fc, w_proj.T], 1)
    weights = gather_weights(shard)
    full_qkv, full_out = weights[:, :3 * width], weights[:, 3 * width:4 * width]

    row_hidden = to_rows(part_of(hidden, 1, mine) + weights[0, 0] * 0)

    row_bounds = lax.dynamic_index_in_dim(
        bounds, jnp.minimum(lax.axis_index("blk"), rows - 1), 0, keepdims=False
    )
    index = jnp.arange(length, dtype=jnp.int32)
    start = jnp.max(jnp.where(row_bounds[:, None] <= index[None], row_bounds[:, None], 0), 0)

    groups = max(1, width // (2 * LANES))
    wide = width // groups
    cuts = [slice(n * wide, (n + 1) * wide) for n in range(groups)]
    grad_mixed = dot(cot, full_out).astype(BF).reshape(rows, group, width)
    row_grads = [to_rows(grad_mixed[:, :, cut]).reshape(length, wide) for cut in cuts]

    if pair:
        row_hidden = row_hidden.reshape(length // 2, model)
        row_hidden = [row_hidden, swap(row_hidden)]
    else:
        row_hidden = [join_parts(row_hidden, 1).reshape(length, model)]
    activated, grad_inner, mlp_out, mlp_back, grad_bfc = mlp(
        flat_hidden, cot, weights, 4 * width // inner, b_fc[None], (grad_mixed,)
    )
    grad_mlp = weight_grads(flat_hidden, grad_inner, cot, activated, (row_hidden[0],))
    other_out = swap(full_out + row_hidden[1][0, 0] * 0) if pair else None
    if pair:
        clear = row_hidden[1][0, 0] * 0
        mlp_back = sum_parts(mlp_back.reshape(rows, group, model) + clear, 1)
        other_mlp = [swap(mlp_out + clear)]
    else:
        mlp_back = sum_parts(mlp_back.reshape(rows, group, model), 1)

    bias = by_pair(b_qkv[None], width)
    grad_packed, mixed, other_mixed = [], [], []
    waits = [grad_mlp, *row_grads]
    for n, (cut, row_grad) in enumerate(zip(cuts, row_grads)):
        attended, grads = attention(
            row_hidden, weights, bias, n * (wide // LANES), row_grad, index - start, start,
            part if pair else 0, waits,
        )
        mixed.append(to_blocks(attended.reshape(blocks, group, wide), rows).reshape(count, wide))
        other_mixed.append(swap(mixed[-1]) if pair else None)
        grad_packed.append(grads)
        waits = [attended, mlp_back]
    grad_mlp = scatter(grad_mlp)
    grad_packed = [jnp.concatenate(grads, 1) for grads in zip(*grad_packed)]
    if pair:
        sent = swap(input_grad(grad_packed[1], weights))
        waits = [*other_mlp, other_out, *other_mixed[:-1], grad_mlp]
        kept = input_grad(grad_packed[0], weights, waits)
        back = [(kept.astype(F32) + sent.astype(F32)).astype(BF).reshape(blocks, part, model)]
    else:
        back = [sum_parts(nt(grad_packed[0], full_qkv).reshape(blocks, group, model), 1).astype(BF)]
    back = jnp.concatenate([to_blocks(piece, rows) for piece in back], 2).astype(F32)
    grad_bqkv = sum(jnp.sum(g.astype(F32), 0) for g in grad_packed)
    grad_qkv = sum(dot(h.T, g) for h, g in zip(row_hidden, grad_packed))

    own_tokens = part_of(tokens, 1, mine).astype(F32)
    if pair:
        branches = mlp_out.astype(F32) + jnp.concatenate(other_mlp, 0).astype(F32)
        for cut, piece, other in zip(cuts, mixed, other_mixed):
            branches += nt(piece, full_out[:, cut]) + nt(other, other_out[:, cut])
        result = (tokens.astype(F32) + branches.reshape(rows, group, model) + b_out).astype(BF)
    else:
        branches = mlp_out.astype(F32) + sum(nt(m, full_out[:, cut]) for m, cut in zip(mixed, cuts))
        branches = sum_parts(branches.reshape(rows, group, model), 1)
        result = join_parts((own_tokens + branches + b_out).astype(BF), 1)
    mixed = jnp.concatenate(mixed, 1)
    grad_hidden = mlp_back + back

    normal, scale = normalize(own_tokens)
    own_cot = part_of(cotangent, 1, mine).astype(F32)
    grad_normal = grad_hidden * ln_gain
    grad_inputs = scale * (
        grad_normal
        - jnp.mean(grad_normal, -1, keepdims=True)
        - normal * jnp.mean(grad_normal * normal, -1, keepdims=True)
    )
    grad_tokens = join_parts((own_cot + grad_inputs).astype(BF), 1)

    grad_attn = scatter(
        jnp.concatenate([grad_qkv.astype(BF), dot(cot.T, mixed).astype(BF)], 1)
    )

    norm_sums = jnp.concatenate(
        [jnp.sum(grad_hidden * normal, (0, 1)), jnp.sum(grad_hidden, (0, 1)), jnp.sum(own_cot, (0, 1))]
    ).reshape(-1, LANES)
    sums = jnp.concatenate([norm_sums, grad_bqkv.reshape(-1, LANES), grad_bfc.reshape(-1, LANES)], 0)
    sums = sum_all(sums, ("dp", "blk"))
    bias_sums = sums[norm_sums.shape[0]:].reshape(-1)
    norm_sums = sum_all(sums[:norm_sums.shape[0]], ("tensor",)).reshape(3, model)
    return (
        result,
        grad_tokens,
        norm_sums[0],
        norm_sums[1],
        by_kind(grad_attn[:, :3 * width], width),
        by_kind(bias_sums[None, :3 * width], width)[0],
        grad_attn[:, 3 * width:].T,
        grad_mlp[:, :inner],
        bias_sums[3 * width:],
        grad_mlp[:, inner:].T,
        norm_sums[2],
    )


def solution(mesh):
    in_specs = (
        P("dp", "blk", None),
        P(),
        P(),
        P(("dp", "blk"), None, "tensor"),
        P(None, "tensor"),
        P("tensor", ("dp", "blk")),
        P(("dp", "blk"), "tensor"),
        P("tensor"),
        P("tensor", ("dp", "blk")),
        P(),
        P("dp", None),
        P("dp", "blk", None),
    )
    out_specs = (
        P("dp", "blk", None),
        P("dp", "blk", None),
        P(),
        P(),
        P(("dp", "blk"), None, "tensor"),
        P(None, "tensor"),
        P("tensor", ("dp", "blk")),
        P(("dp", "blk"), "tensor"),
        P("tensor"),
        P("tensor", ("dp", "blk")),
        P(),
    )
    return jax.shard_map(local, mesh=mesh, in_specs=in_specs, out_specs=out_specs, check_vma=False)
```

```python
import functools

import jax
import jax.numpy as jnp
from jax import lax
from jax.experimental import pallas as pl
from jax.experimental.pallas import tpu as pltpu
from jax.sharding import PartitionSpec as P

HEAD_DIM = 64
ROT_DIM = 16
LANES = 128
EPSILON = 1e-05
BF = jnp.bfloat16
F32 = jnp.float32
MIB = 1024 * 1024


def nt(a, b):
    return lax.dot_general(a, b, (((1,), (1,)), ((), ())), preferred_element_type=F32)


def nn(a, b):
    return lax.dot_general(a, b, (((1,), (0,)), ((), ())), preferred_element_type=F32)


def attn_kernel(bq, bk, part, waits, lo_ref, hi_ref, *refs):
    count = 2 if part else 1
    hidden, refs = refs[:count], refs[count + waits:]
    w_ref, bias_ref, do_ref, cos_ref, sin_ref, start_ref, o_ref = refs[:7]
    grads, refs = refs[7:7 + count], refs[7 + count:]
    (q2, qt, ks, vx, s_buf, p_buf, d_buf, dkt, dvt, keep, ahead, behind, starts) = refs
    length = do_ref.shape[0]
    nq = length // bq
    lane = lax.broadcasted_iota(jnp.int32, (1, LANES), 1)
    first = lane < HEAD_DIM
    half = ROT_DIM // 2
    to_score = HEAD_DIM ** (-0.5) * 1.4426950408889634
    mine_first = lax.axis_index("tensor") == 0 if part else None

    def load(base, size):
        if part:
            rows = []
            for n in range(size // (2 * part)):
                at = pl.ds(pl.multiple_of(base // 2 + n * part, part), part)
                a, b = hidden[0][at, :], hidden[1][at, :]
                rows += [jnp.where(mine_first, a, b), jnp.where(mine_first, b, a)]
            rows = jnp.concatenate(rows, 0)
        else:
            rows = hidden[0][pl.ds(base, size), :]
        packed = nn(rows, w_ref[...]) + bias_ref[...]
        return [packed[:, n * LANES:(n + 1) * LANES] for n in range(3)]

    def store(base, which, value):
        cols = slice(which * LANES, (which + 1) * LANES)
        size = value.shape[0]
        if not part:
            grads[0][pl.ds(base, size), cols] = value.astype(BF)
            return
        for n in range(size // (2 * part)):
            at = pl.ds(pl.multiple_of(base // 2 + n * part, part), part)
            a = value[2 * n * part:(2 * n + 1) * part]
            b = value[(2 * n + 1) * part:(2 * n + 2) * part]
            grads[0][at, cols] = jnp.where(mine_first, a, b).astype(BF)
            grads[1][at, cols] = jnp.where(mine_first, b, a).astype(BF)

    def rot(u, rows):
        return (u * keep[rows, :] + pltpu.roll(u, LANES - half, 1) * ahead[rows, :]
                + pltpu.roll(u, half, 1) * behind[rows, :])

    def rot_back(u, rows):
        return (u * keep[rows, :] + pltpu.roll(u * behind[rows, :], LANES - half, 1)
                + pltpu.roll(u * ahead[rows, :], half, 1))

    def tables(i, _):
        rows = pl.ds(pl.multiple_of(i * bq, bq), bq)
        c, s = cos_ref[:, rows], sin_ref[:, rows]
        rest = HEAD_DIM - ROT_DIM
        one, zero, gap = jnp.ones((rest, bq), F32), jnp.zeros((rest, bq), F32), jnp.zeros((half, bq), F32)
        keep[rows, :] = jnp.concatenate([c, c, one] * 2, 0).T
        ahead[rows, :] = jnp.concatenate([-s, gap, zero] * 2, 0).T
        behind[rows, :] = jnp.concatenate([gap, s, zero] * 2, 0).T
        starts[rows, :] = jnp.broadcast_to(start_ref[:, rows], (LANES, bq)).T
        return 0

    @pl.when(pl.program_id(0) == 0)
    def _():
        lax.fori_loop(0, nq, tables, 0)

    def prep(i, _):
        base = pl.multiple_of(i * bq, bq)
        rows = pl.ds(base, bq)
        q, k, v = load(base, bq)
        q = rot(q, rows)
        qs = (q * to_score).astype(BF)
        zero = jnp.zeros_like(qs)
        q2[0, rows, :] = jnp.where(first, qs, zero)
        q2[1, rows, :] = jnp.where(first, zero, qs)
        qt[:, rows] = q.T.astype(BF)
        ks[rows, :] = rot(k, rows).astype(BF)
        vx[rows, :LANES] = v.astype(BF)
        vx[rows, LANES:] = jnp.ones((bq, LANES), BF)
        dkt[:, rows] = jnp.zeros((LANES, bq), F32)
        dvt[:, rows] = jnp.zeros((LANES, bq), F32)
        return 0

    lax.fori_loop(0, nq, prep, 0)

    def q_block(i, _):
        rows = pl.ds(pl.multiple_of(i * bq, bq), bq)
        last = (i * bq) // bk
        least = lo_ref[i] // bk
        masked = jnp.clip((hi_ref[i] + bk - 1) // bk, least, last)
        q_h = (q2[0, rows, :], q2[1, rows, :])
        start = starts[rows, :]

        def scores(j, mx, mode):
            cols = pl.ds(pl.multiple_of(j * bk, bk), bk)
            k = ks[cols, :]
            out = []
            for h in range(2):
                s = nt(q_h[h], k)
                m = mx[h]
                for t in range(bk // LANES):
                    piece = s[:, t * LANES:(t + 1) * LANES]
                    if mode:
                        kidx = (j * bk + t * LANES + lane).astype(F32)
                        ok = kidx >= start
                        if mode == 2:
                            qidx = (i * bq + lax.broadcasted_iota(jnp.int32, (bq, 1), 0)).astype(F32)
                            ok = ok & (kidx <= qidx)
                        piece = jnp.where(ok, piece, -1e30)
                    s_buf[h, :, pl.ds(pl.multiple_of(j * bk + t * LANES, LANES), LANES)] = piece
                    m = jnp.maximum(m, piece)
                out.append(m)
            return tuple(out)

        mx = (jnp.full((bq, LANES), -1e30, F32),) * 2
        mx = lax.fori_loop(least, masked, lambda j, m: scores(j, m, 1), mx)
        mx = lax.fori_loop(masked, last, lambda j, m: scores(j, m, 0), mx)
        mx = scores(last, mx, 2)
        mx = [jnp.max(m, -1, keepdims=True) for m in mx]

        def weigh(j, acc):
            cols = pl.ds(pl.multiple_of(j * bk, bk), bk)
            v = vx[cols, :]
            out = []
            for h in range(2):
                p = jnp.exp2(s_buf[h, :, cols] - mx[h]).astype(BF)
                p_buf[h, :, cols] = p
                out.append(acc[h] + nn(p, v))
            return tuple(out)

        acc = (jnp.zeros((bq, 2 * LANES), F32),) * 2
        acc = lax.fori_loop(least, last + 1, weigh, acc)
        inv = [1.0 / a[:, LANES:] for a in acc]
        outs = [a[:, :LANES] * r for a, r in zip(acc, inv)]
        o = jnp.where(first, outs[0], outs[1])
        o_ref[rows, :] = o.astype(BF)
        do = do_ref[rows, :].astype(F32)
        dos, dots, deltas = [], [], []
        for h in range(2):
            mine = first if h == 0 else jnp.logical_not(first)
            d = jnp.where(mine, do * inv[h], 0.0).astype(BF)
            dos.append(d)
            df = d.astype(F32)
            deltas.append(jnp.sum(df * o, -1, keepdims=True))
            dots.append(df.T[h * HEAD_DIM:(h + 1) * HEAD_DIM].astype(BF))
        q_t = qt[:, rows]

        def back(j, acc):
            cols = pl.ds(pl.multiple_of(j * bk, bk), bk)
            v = vx[cols, :LANES]
            k = ks[cols, :]
            out = []
            for h in range(2):
                rows_h = slice(h * HEAD_DIM, (h + 1) * HEAD_DIM)
                p = p_buf[h, :, cols]
                dp = nt(dos[h], v)
                ds = (p.astype(F32) * (dp - deltas[h])).astype(BF)
                dvt[rows_h, cols] += nn(dots[h], p)
                dkt[rows_h, cols] += nn(q_t[rows_h], ds)
                out.append(acc[h] + nn(ds, k))
            return tuple(out)

        acc = (jnp.zeros((bq, LANES), F32),) * 2
        acc = lax.fori_loop(least, last + 1, back, acc)
        dq = jnp.where(first, acc[0], acc[1]) * HEAD_DIM ** (-0.5)
        store(i * bq, 0, rot_back(dq, rows))
        return 0

    def static_block(i):
        rows = slice(i * bq, (i + 1) * bq)
        width = (i + 1) * bq
        start = starts[rows, :]
        q_h = (q2[0, rows, :], q2[1, rows, :])
        mx = []
        for h in range(2):
            m = jnp.full((bq, LANES), -1e30, F32)
            for j in range(0, width, bk):
                s = nt(q_h[h], ks[j:j + bk, :])
                for t in range(0, bk, LANES):
                    kidx = (j + t + lane).astype(F32)
                    ok = kidx >= start
                    if j + t + LANES > i * bq:
                        qidx = (i * bq + lax.broadcasted_iota(jnp.int32, (bq, 1), 0)).astype(F32)
                        ok = ok & (kidx <= qidx)
                    piece = jnp.where(ok, s[:, t:t + LANES], -1e30)
                    s_buf[h, :, j + t:j + t + LANES] = piece
                    m = jnp.maximum(m, piece)
            mx.append(jnp.broadcast_to(jnp.max(m, -1, keepdims=True), (bq, LANES)))
        acc = []
        for h in range(2):
            for t in range(0, width, LANES):
                p_buf[h, :, t:t + LANES] = jnp.exp2(s_buf[h, :, t:t + LANES] - mx[h]).astype(BF)
            acc.append(nn(p_buf[h, :, :width], vx[:width, :]))
        inv = [1.0 / v[:, LANES:] for v in acc]
        outs = [v[:, :LANES] * r for v, r in zip(acc, inv)]
        o = jnp.where(first, outs[0], outs[1])
        o_ref[rows, :] = o.astype(BF)
        do = do_ref[rows, :].astype(F32)
        dq = []
        for h in range(2):
            mine = first if h == 0 else jnp.logical_not(first)
            rows_h = slice(h * HEAD_DIM, (h + 1) * HEAD_DIM)
            d = jnp.where(mine, do * inv[h], 0.0).astype(BF)
            df = d.astype(F32)
            delta = jnp.broadcast_to(jnp.sum(df * o, -1, keepdims=True), (bq, LANES))
            d_t = df.T[rows_h].astype(BF)
            q_t = qt[rows_h, rows]
            for j in range(0, width, bk):
                cols = slice(j, j + bk)
                dp = nt(d, vx[cols, :LANES])
                dvt[rows_h, cols] += nn(d_t, p_buf[h, :, cols])
                for t in range(0, bk, LANES):
                    at = slice(j + t, j + t + LANES)
                    d_buf[h, :, at] = (p_buf[h, :, at].astype(F32) * (dp[:, t:t + LANES] - delta)).astype(BF)
                dkt[rows_h, cols] += nn(q_t, d_buf[h, :, cols])
            dq.append(nn(d_buf[h, :, :width], ks[:width, :]))
        dq = jnp.where(first, dq[0], dq[1]) * HEAD_DIM ** (-0.5)
        store(i * bq, 0, rot_back(dq, rows))

    if nq <= 4:
        for i in range(nq):
            static_block(i)
    else:
        lax.fori_loop(0, nq, q_block, 0)

    def finish(i, _):
        base = pl.multiple_of(i * bq, bq)
        rows = pl.ds(base, bq)
        store(base, 1, rot_back(dkt[:, rows].T * HEAD_DIM ** (-0.5), rows))
        store(base, 2, dvt[:, rows].T)
        return 0

    lax.fori_loop(0, nq, finish, 0)


def attention(hidden, weights, bias, first_pair, do, position, start, part=0, waits=(), bq=512, bk=512):
    length, width = do.shape
    bq = min(bq, 2 ** 20 // length)
    bk = max(bq, min(bk, length))
    pairs = width // LANES
    freqs = 10000.0 ** (-jnp.arange(0, ROT_DIM, 2, dtype=F32) / ROT_DIM)
    phase = position.astype(F32)[None] * freqs[:, None]
    by_block = start.reshape(length // bq, bq)
    rows, model = hidden[0].shape
    once = pl.Buffered(1)
    columns = pl.BlockSpec((length, LANES), lambda g, *_: (0, g))
    triple = pl.BlockSpec((rows, 3 * LANES), lambda g, *_: (0, g))
    whole = lambda n: pl.BlockSpec((n, length), lambda g, *_: (0, 0), pipeline_mode=once)
    tri_out = jax.ShapeDtypeStruct((rows, 3 * width), BF)
    static = length // bq <= 4
    out = pl.pallas_call(
        functools.partial(attn_kernel, bq, bk, part, len(waits)),
        out_shape=[jax.ShapeDtypeStruct((length, width), BF)] + [tri_out] * len(hidden),
        grid_spec=pltpu.PrefetchScalarGridSpec(
            num_scalar_prefetch=2,
            grid=(pairs,),
            in_specs=[pl.BlockSpec((rows, model), lambda g, *_: (0, 0), pipeline_mode=once)] * len(hidden)
            + [pl.BlockSpec(memory_space=pl.ANY)] * len(waits)
            + [
                pl.BlockSpec((model, 3 * LANES), lambda g, *_: (0, first_pair + g)),
                pl.BlockSpec((1, 3 * LANES), lambda g, *_: (0, first_pair + g)),
                columns, whole(ROT_DIM // 2), whole(ROT_DIM // 2), whole(1),
            ],
            out_specs=[columns] + [triple] * len(hidden),
            scratch_shapes=[
                pltpu.VMEM((2, length, LANES), BF),
                pltpu.VMEM((LANES, length), BF),
                pltpu.VMEM((length, LANES), BF),
                pltpu.VMEM((length, 2 * LANES), BF),
                pltpu.VMEM((2, bq, length), F32),
                pltpu.VMEM((2, bq, length), BF),
                pltpu.VMEM((2, bq, length) if static else (8, LANES), BF),
                pltpu.VMEM((LANES, length), F32),
                pltpu.VMEM((LANES, length), F32),
            ] + [pltpu.VMEM((length, LANES), F32)] * 4,
        ),
        compiler_params=pltpu.CompilerParams(vmem_limit_bytes=56 * MIB),
        cost_estimate=pl.CostEstimate(flops=1000, bytes_accessed=1000, transcendentals=0),
    )(by_block.min(1), by_block.max(1), *hidden, *waits, weights, bias, do, jnp.cos(phase), jnp.sin(phase),
      start.astype(F32)[None])
    return out[0], list(out[1:])


MESH = pl.DeviceIdType.MESH


def remote(src, dst, send, recv, target):
    return pltpu.make_async_remote_copy(
        src_ref=src, dst_ref=dst, send_sem=send, recv_sem=recv, device_id=target, device_id_type=MESH
    )


def meet(others):
    barrier = pltpu.get_barrier_semaphore()
    for target in others:
        pl.semaphore_signal(barrier, inc=1, device_id=target, device_id_type=MESH)
    pl.semaphore_wait(barrier, len(others))


def gather_kernel(x_ref, out_ref, local_sem, recv, up, down, across, over):
    size = x_ref.shape[0]
    core, block = lax.axis_index("dp"), lax.axis_index("blk")
    z, y = block // 2, lax.rem(block, 2)
    depth = lax.axis_size("blk") // 2
    above, below = {"blk": block + 2}, {"blk": block - 2}
    beside, sibling = {"blk": block + 1 - 2 * y}, {"dp": 1 - core}

    def place(c, zz, yy):
        return (c * depth + zz) * 2 + yy

    def chunk(at):
        return out_ref.at[pl.ds(pl.multiple_of(at * size, size), size)]

    def copy(src, at, sem, target):
        return pltpu.make_async_remote_copy(
            src_ref=src, dst_ref=chunk(at), send_sem=sem, recv_sem=recv.at[at],
            device_id=target, device_id_type=pl.DeviceIdType.MESH,
        )

    def arrived(at):
        copy(chunk(at), at, local_sem, sibling).wait_recv()

    barrier = pltpu.get_barrier_semaphore()

    def greet(target):
        pl.semaphore_signal(barrier, inc=1, device_id=target, device_id_type=pl.DeviceIdType.MESH)

    def not_top(action):
        pl.when(z < depth - 1)(action)

    def not_bottom(action):
        pl.when(z > 0)(action)

    not_top(lambda: greet(above))
    not_bottom(lambda: greet(below))
    greet(beside)
    greet(sibling)
    pl.semaphore_wait(barrier, 2 + jnp.where(z > 0, 1, 0) + jnp.where(z < depth - 1, 1, 0))

    mine = place(core, z, y)
    keep = pltpu.make_async_copy(x_ref, chunk(mine), local_sem)
    not_top(lambda: copy(x_ref, mine, up.at[z], above).start())
    not_bottom(lambda: copy(x_ref, mine, down.at[z], below).start())
    copy(x_ref, mine, across.at[z], beside).start()
    copy(x_ref, mine, over.at[z * 2 + y], sibling).start()
    keep.start()

    def from_beside(zz):
        at = place(core, zz, 1 - y)
        arrived(at)
        copy(chunk(at), at, over.at[zz * 2 + 1 - y], sibling).start()

    def from_line(zz, onward, sems, target):
        at = place(core, zz, y)
        arrived(at)
        onward(lambda: copy(chunk(at), at, sems.at[zz], target).start())
        copy(chunk(at), at, across.at[zz], beside).start()
        copy(chunk(at), at, over.at[zz * 2 + y], sibling).start()

    for step in range(1, depth):
        pl.when(z >= step)(lambda: from_line(z - step, not_top, up, above))
        pl.when(z + step < depth)(lambda: from_line(z + step, not_bottom, down, below))
    from_beside(z)
    for step in range(1, depth):
        pl.when(z >= step)(lambda: from_beside(z - step))
        pl.when(z + step < depth)(lambda: from_beside(z + step))

    keep.wait()
    for zz in range(depth):
        for yy in range(2):
            arrived(place(1 - core, zz, yy))
            copy(x_ref, mine, over.at[zz * 2 + yy], sibling).wait_send()
        copy(x_ref, mine, across.at[zz], beside).wait_send()
        pl.when((zz <= z) & (z < depth - 1))(lambda: copy(x_ref, mine, up.at[zz], above).wait_send())
        pl.when((zz >= z) & (z > 0))(lambda: copy(x_ref, mine, down.at[zz], below).wait_send())


def gather_weights(shard):
    cores, blocks = lax.axis_size("dp"), lax.axis_size("blk")
    rows, columns = shard.shape
    dma = pltpu.SemaphoreType.DMA
    return pl.pallas_call(
        gather_kernel,
        out_shape=jax.ShapeDtypeStruct((cores * blocks * rows, columns), shard.dtype),
        in_specs=[pl.BlockSpec(memory_space=pl.ANY)],
        out_specs=pl.BlockSpec(memory_space=pl.ANY),
        scratch_shapes=[
            dma, dma((cores * blocks,)), dma((blocks // 2,)), dma((blocks // 2,)),
            dma((blocks // 2,)), dma((blocks,)),
        ],
        compiler_params=pltpu.CompilerParams(collective_id=0, has_side_effects=True),
    )(shard)


class RowTransfer:
    def __init__(self, hid_ref, mine_ref, other_ref, blank, blank_sem, hid_send, hid_recv, side_send, side_recv):
        self.refs = hid_ref, mine_ref, other_ref, blank
        self.sems = blank_sem, hid_send, hid_recv, side_send, side_recv
        self.rows, group, _ = hid_ref.shape
        self.part = group // 2
        self.block, self.half = lax.axis_index("blk"), lax.axis_index("tensor")
        self.blocks = lax.axis_size("blk")
        self.has_row = self.block < self.rows
        self.facing = {"tensor": 1 - self.half}

    def piece(self, ref, at):
        return ref.at[pl.ds(pl.multiple_of(at * self.part, self.part), self.part)]

    def source(self, r):
        return self.refs[0].at[r, pl.ds(pl.multiple_of(self.half * self.part, self.part), self.part)]

    def row_copy(self, r):
        _, hid_send, hid_recv, _, _ = self.sems
        mine = self.piece(self.refs[1], self.block)
        return remote(self.source(r), mine, hid_send.at[r], hid_recv.at[self.block], {"blk": r})

    def own_row(self):
        return pltpu.make_async_copy(
            self.source(self.block), self.piece(self.refs[1], self.block), self.sems[1].at[self.block]
        )

    def side_copy(self, s):
        _, _, _, side_send, side_recv = self.sems
        _, mine, other, _ = self.refs
        return remote(self.piece(mine, s), self.piece(other, s), side_send.at[s], side_recv.at[s], self.facing)

    def blanks(self):
        _, mine, other, blank = self.refs
        return [
            pltpu.make_async_copy(blank, self.piece(ref, s), self.sems[0].at[n * self.blocks + s])
            for n, ref in enumerate((mine, other)) for s in range(self.blocks)
        ]

    def to_block(self, n, action):
        r = lax.rem(self.block + n, self.blocks)
        pl.when(r < self.rows)(lambda: action(self.row_copy(r)))

    def start(self):
        meet([{"blk": lax.rem(self.block + n, self.blocks)} for n in range(1, self.blocks)] + [self.facing])
        for n in range(1, self.blocks):
            self.to_block(n, lambda copy: copy.start())

        @pl.when(self.has_row)
        def _():
            self.own_row().start()
            self.own_row().wait()
            self.side_copy(self.block).start()

        @pl.when(jnp.logical_not(self.has_row))
        def _():
            self.refs[3][...] = jnp.zeros_like(self.refs[3])
            for copy in self.blanks():
                copy.start()

    def onward(self, n):
        @pl.when(self.has_row)
        def _():
            s = lax.rem(self.block + self.blocks - n, self.blocks)
            mine = self.piece(self.refs[1], s)
            remote(mine, mine, self.sems[3].at[s], self.sems[2].at[s], self.facing).wait_recv()
            self.side_copy(s).start()

    def finish(self):
        for n in range(1, self.blocks):
            self.to_block(n, lambda copy: copy.wait_send())

        @pl.when(self.has_row)
        def _():
            for s in range(self.blocks):
                self.side_copy(s).wait()

        @pl.when(jnp.logical_not(self.has_row))
        def _():
            for copy in self.blanks():
                copy.wait()


def tail_kernel(groups, waits, *refs):
    g_mine, g_other = refs[:groups], refs[groups:2 * groups]
    (w_ref, tok_ref, cot_ref, add_ref, gain_ref, out_ref, sum_ref,
     sent, got, home_send, home, grads, a_send, a_recv, b_send, b_recv, c_send, c_recv, c_local) = refs[2 * groups + waits:]
    rows, part, model = tok_ref.shape
    block, half = lax.axis_index("blk"), lax.axis_index("tensor")
    blocks = lax.axis_size("blk")
    facing = {"tensor": 1 - half}
    has_row = block < rows
    meet([{"blk": lax.rem(block + n, blocks)} for n in range(1, blocks)] + [facing])

    def product(parts, s):
        at, total, first = pl.ds(pl.multiple_of(s * part, part), part), None, 0
        for g in parts:
            width = g.shape[1]
            term = nt(g[at, :], w_ref[:, first:first + width])
            total, first = term if total is None else total + term, first + width
        return total

    def across(s):
        return remote(sent.at[s], got.at[s], a_send.at[s], a_recv.at[s], facing)

    def homeward(s):
        return remote(home_send.at[s], home.at[block], b_send.at[s], b_recv.at[block], {"blk": s})

    def own_half(ref, r):
        return ref.at[r, pl.ds(pl.multiple_of(half * part, part), part)]

    def share(r):
        return remote(grads.at[r], own_half(out_ref, r), c_send.at[r], c_recv.at[r], facing)

    def keep(r):
        return pltpu.make_async_copy(grads.at[r], own_half(out_ref, r), c_local.at[r])

    @pl.when(has_row)
    def _():
        for n in range(blocks):
            s = lax.rem(block + n, blocks)
            sent[s] = product(g_other, s).astype(BF)
            across(s).start()

    sum_ref[...] = jnp.zeros_like(sum_ref)

    def forward(n):
        s = lax.rem(block + n, blocks)

        @pl.when(has_row)
        def _():
            total = product(g_mine, s)
            across(s).wait_recv()
            total = (total + got[s].astype(F32)).astype(BF)
            if n == 0:
                home[s] = total
            else:
                home_send[s] = total
                homeward(s).start()

    def norm(n):
        r = lax.rem(block + blocks - n, blocks)

        @pl.when(r < rows)
        def _():
            if n:
                remote(home_send.at[r], home.at[r], b_send.at[r], b_recv.at[r], facing).wait_recv()
            grad = home[r].astype(F32) + add_ref[r].astype(F32)
            x = tok_ref[r].astype(F32)
            x = x - jnp.mean(x, -1, keepdims=True)
            scale = lax.rsqrt(jnp.mean(x * x, -1, keepdims=True) + EPSILON)
            x = x * scale
            sum_ref[0:1, :] += jnp.sum(grad * x, 0, keepdims=True)
            sum_ref[1:2, :] += jnp.sum(grad, 0, keepdims=True)
            grad = grad * gain_ref[...]
            grad = grad - jnp.mean(grad, -1, keepdims=True) - x * jnp.mean(grad * x, -1, keepdims=True)
            grads[r] = (cot_ref[r].astype(F32) + scale * grad).astype(BF)
            share(r).start()
            keep(r).start()

    lag = 2
    for n in range(blocks + lag):
        if n < blocks:
            forward(n)
        if n >= lag:
            norm(n - lag)

    for r in range(rows):
        share(r).wait()
        keep(r).wait()

    @pl.when(has_row)
    def _():
        for s in range(blocks):
            across(s).wait_send()
        for n in range(1, blocks):
            homeward(lax.rem(block + n, blocks)).wait_send()


def input_grads(g_mine, g_other, weights, tokens, cot, add, gain, waits=()):
    rows, part, model = tokens.shape
    blocks = lax.axis_size("blk")
    wide = sum(g.shape[1] for g in g_mine)
    dma = pltpu.SemaphoreType.DMA
    vmem = pl.BlockSpec(memory_space=pltpu.VMEM)
    return pl.pallas_call(
        functools.partial(tail_kernel, len(g_mine), len(waits)),
        grid=(1,),
        out_shape=[jax.ShapeDtypeStruct((rows, 2 * part, model), BF), jax.ShapeDtypeStruct((8, model), F32)],
        in_specs=[vmem] * (2 * len(g_mine)) + [pl.BlockSpec(memory_space=pl.ANY)] * len(waits)
        + [pl.BlockSpec((model, wide), lambda i: (0, 0))] + [vmem] * 4,
        out_specs=[pl.BlockSpec(memory_space=pl.ANY), vmem],
        scratch_shapes=[pltpu.VMEM((blocks, part, model), BF)] * 4 + [pltpu.VMEM((rows, part, model), BF)]
        + [dma((blocks,))] * 4 + [dma((rows,))] * 3,
        compiler_params=pltpu.CompilerParams(
            collective_id=1, has_side_effects=True, vmem_limit_bytes=48 * MIB
        ),
        cost_estimate=pl.CostEstimate(flops=1000, bytes_accessed=1000, transcendentals=0),
    )(*g_mine, *g_other, *waits, weights, tokens, cot, add, gain)


def weight_grad_kernel(half, waits, a_ref, b_ref, *refs):
    x_ref, y_ref, ax_ref, by_ref, turned = refs[waits:]
    step = pl.program_id(0)

    @pl.when(step == 0)
    def _():
        turned[...] = a_ref[...].T

    @pl.when(step == half)
    def _():
        turned[...] = b_ref[...].T

    @pl.when(step < half)
    def _():
        ax_ref[...] = nn(turned[...], x_ref[...]).astype(BF)

    @pl.when(step >= half)
    def _():
        by_ref[...] = nn(turned[...], y_ref[...]).astype(BF)


def weight_grads(a, x, b, y, waits=(), tile=512):
    count, model = a.shape
    inner = x.shape[1]
    tile = min(tile, inner)
    half = inner // tile
    whole = pl.BlockSpec((count, model), lambda i: (0, 0), pipeline_mode=pl.Buffered(1))
    return pl.pallas_call(
        functools.partial(weight_grad_kernel, half, len(waits)),
        grid=(2 * half,),
        out_shape=[jax.ShapeDtypeStruct((model, inner), BF)] * 2,
        in_specs=[
            whole, whole, *[pl.BlockSpec(memory_space=pl.ANY)] * len(waits),
            pl.BlockSpec((count, tile), lambda i: (0, jnp.minimum(i, half - 1))),
            pl.BlockSpec((count, tile), lambda i: (0, jnp.maximum(i - half, 0))),
        ],
        out_specs=[
            pl.BlockSpec((model, tile), lambda i: (0, jnp.minimum(i, half - 1))),
            pl.BlockSpec((model, tile), lambda i: (0, jnp.maximum(i - half, 0))),
        ],
        scratch_shapes=[pltpu.VMEM((model, count), BF)],
        compiler_params=pltpu.CompilerParams(vmem_limit_bytes=48 * MIB),
        cost_estimate=pl.CostEstimate(flops=1000, bytes_accessed=1000, transcendentals=0),
    )(a, b, *waits, x, y)


def mlp_kernel(tile, waits, moves, hid_ref, cot_ref, wf_ref, wp_ref, bias_ref, *refs):
    refs = refs[waits:]
    act_ref, gin_ref, res_ref, back_ref, gb_ref = refs[moves:moves + 5]
    if moves:
        step, steps = pl.program_id(0), pl.num_programs(0)
        rows = RowTransfer(refs[0], *refs[moves + 5:])
        pl.when(step == 0)(rows.start)
        for n in range(1, rows.blocks):
            pl.when(step == jnp.minimum(n, steps - 1))(lambda: rows.onward(n))
    hid, cot = hid_ref[...], cot_ref[...]

    @pl.when(pl.program_id(0) == 0)
    def _():
        gb_ref[...] = jnp.zeros_like(gb_ref)

    res = back = None
    for n in range(wf_ref.shape[1] // tile):
        cols = slice(n * tile, (n + 1) * tile)
        wf, wp = wf_ref[:, cols], wp_ref[:, cols]
        inner = nn(hid, wf) + bias_ref[:, cols]
        grad_act = nn(cot, wp)
        size = jnp.abs(inner)
        t = 1.0 / (1.0 + (0.3275911 * 0.7071067811865476) * size)
        bell = jnp.exp2((-0.5 * 1.4426950408889634) * inner * inner)
        tail = ((((0.5 * 1.061405429 * t - 0.5 * 1.453152027) * t + 0.5 * 1.421413741) * t
                 - 0.5 * 0.284496736) * t + 0.5 * 0.254829592) * t * bell
        below = jnp.where(inner < 0, tail, 1.0 - tail)
        act = (inner * below).astype(BF)
        grad_inner = (grad_act * (below + inner * (bell * 0.3989422804014327))).astype(BF)
        act_ref[:, cols] = act
        gin_ref[:, cols] = grad_inner
        gb_ref[:, cols] += jnp.sum(grad_inner.astype(F32), 0, keepdims=True)
        r, b = nt(act, wp), nt(grad_inner, wf)
        res, back = (r, b) if res is None else (res + r, back + b)
    res_ref[...] = res.astype(BF)
    back_ref[...] = back.astype(BF)
    if moves:
        pl.when(step == steps - 1)(rows.finish)


def mlp(hidden, cot, weights, first_block, bias, waits=(), moved=None, size=256, tile=512):
    count, model = hidden.shape
    inner = bias.shape[1]
    tile = min(tile, inner)
    rows = lambda n: pl.BlockSpec((size, n), lambda i: (i, 0))
    matrix = lambda n: pl.BlockSpec((model, inner), lambda i: (0, first_block + n), pipeline_mode=pl.Buffered(1))
    vector = pl.BlockSpec((1, inner), lambda i: (0, 0))
    hbm = pl.BlockSpec(memory_space=pl.ANY)
    shape = lambda n: jax.ShapeDtypeStruct((count, n), BF)
    moves, outs, scratch, params = (), [], [], {}
    if moved is not None:
        blocks, dma = lax.axis_size("blk"), pltpu.SemaphoreType.DMA
        part = moved.shape[1] // 2
        moves, outs = (moved,), [jax.ShapeDtypeStruct((blocks * part, model), BF)] * 2
        scratch = [pltpu.VMEM((part, model), BF), dma((2 * blocks,))] + [dma((blocks,))] * 4
        params = dict(collective_id=2, has_side_effects=True)
    return pl.pallas_call(
        functools.partial(mlp_kernel, tile, len(waits), len(moves)),
        grid=(count // size,),
        out_shape=[shape(inner), shape(inner), shape(model), shape(model), jax.ShapeDtypeStruct((1, inner), F32)] + outs,
        in_specs=[rows(model), rows(model), matrix(0), matrix(1), vector] + [hbm] * (len(waits) + len(moves)),
        out_specs=[rows(inner), rows(inner), rows(model), rows(model), vector] + [hbm] * len(outs),
        scratch_shapes=scratch,
        compiler_params=pltpu.CompilerParams(vmem_limit_bytes=56 * MIB, **params),
        cost_estimate=pl.CostEstimate(flops=1000, bytes_accessed=1000, transcendentals=0),
    )(hidden, cot, weights, weights, bias, *waits, *moves)


def normalize(values):
    center = values - jnp.mean(values, -1, keepdims=True)
    spread = jnp.mean(center * center, -1, keepdims=True)
    scale = lax.rsqrt(spread + EPSILON)
    return center * scale, scale


def swap(value):
    return lax.ppermute(value, "tensor", [(0, 1), (1, 0)])


def split_tensor(value, axis):
    shape = value.shape
    parts = lax.axis_size("tensor")
    return value.reshape(shape[:axis] + (parts, shape[axis] // parts) + shape[axis + 1:])


def part_of(value, axis, which):
    return lax.dynamic_index_in_dim(split_tensor(value, axis), which, axis, keepdims=False)


def sum_parts(value, axis):
    mine = lax.axis_index("tensor")
    if lax.axis_size("tensor") == 2:
        other = swap(part_of(value, axis, 1 - mine).astype(BF))
        return part_of(value, axis, mine).astype(F32) + other.astype(F32)
    return lax.psum_scatter(
        value.astype(BF), "tensor", scatter_dimension=axis, tiled=True
    ).astype(F32)


def join_parts(value, axis):
    if lax.axis_size("tensor") != 2:
        return lax.all_gather(value, "tensor", axis=axis, tiled=True)
    other = swap(value)
    first = lax.axis_index("tensor") == 0
    low, high = jnp.where(first, value, other), jnp.where(first, other, value)
    return jnp.concatenate([low, high], axis)


def to_rows(value):
    blocks = lax.axis_size("blk")
    pad = jnp.zeros((blocks - value.shape[0],) + value.shape[1:], value.dtype)
    return lax.all_to_all(jnp.concatenate([value, pad], 0), "blk", 0, 0, tiled=True)


def to_blocks(value, rows):
    return lax.all_to_all(value, "blk", 0, 0, tiled=True)[:rows]


def sum_all(value, axes):
    for axis in axes:
        size = lax.axis_size(axis)
        step = 1
        while step < size:
            value = value + lax.ppermute(value, axis, [(i, i ^ step) for i in range(size)])
            step *= 2
    return value


def by_pair(value, width):
    count = value.shape[0]
    return value.reshape(count, 3, width // LANES, LANES).transpose(0, 2, 1, 3).reshape(count, 3 * width)


def by_kind(value, width):
    count = value.shape[0]
    return value.reshape(count, width // LANES, 3, LANES).transpose(0, 2, 1, 3).reshape(count, 3, width)


def scatter(value):
    return lax.psum_scatter(value, ("dp", "blk"), scatter_dimension=0, tiled=True).astype(F32)


def dot(a, b):
    return jnp.dot(a, b, preferred_element_type=F32)


def local(
    tokens, ln_gain, ln_bias, w_qkv, b_qkv, w_out, w_fc, b_fc, w_proj, b_out, bounds, cotangent
):
    rows, group, model = tokens.shape
    width, inner = b_qkv.shape[1], b_fc.shape[0]
    blocks, parts = lax.axis_size("blk"), lax.axis_size("tensor")
    length = blocks * group
    count = rows * group
    part = group // parts

    mine = lax.axis_index("tensor")
    pair = parts == 2 and (lax.axis_size("dp"), blocks) == (2, 8)
    hidden = (normalize(tokens.astype(F32))[0] * ln_gain + ln_bias).astype(BF)
    flat_hidden, cot = hidden.reshape(count, model), cotangent.reshape(count, model)

    shard = jnp.concatenate([by_pair(w_qkv, width), w_out.T, w_fc, w_proj.T], 1)
    if pair:
        weights = gather_weights(shard)
    else:
        weights = lax.all_gather(shard, ("dp", "blk"), axis=0, tiled=True)
        row_hidden = [join_parts(to_rows(part_of(hidden, 1, mine)), 1).reshape(length, model)]
    full_qkv, full_out = weights[:, :3 * width], weights[:, 3 * width:4 * width]

    row_bounds = lax.dynamic_index_in_dim(
        bounds, jnp.minimum(lax.axis_index("blk"), rows - 1), 0, keepdims=False
    )
    index = jnp.arange(length, dtype=jnp.int32)
    start = jnp.max(jnp.where(row_bounds[:, None] <= index[None], row_bounds[:, None], 0), 0)

    groups = max(1, width // (2 * LANES))
    wide = width // groups
    cuts = [slice(n * wide, (n + 1) * wide) for n in range(groups)]
    grad_mixed = dot(cot, full_out).astype(BF).reshape(rows, group, width)

    activated, grad_inner, mlp_out, mlp_back, grad_bfc, *moved = mlp(
        flat_hidden, cot, weights, 4 * width // inner, b_fc[None], (grad_mixed,), hidden if pair else None
    )
    grad_mixed += grad_inner[0, 0] * 0
    row_grads = [to_rows(grad_mixed[:, :, cut]).reshape(length, wide) for cut in cuts]
    row_hidden = moved or row_hidden
    mlp_back = sum_parts(mlp_back.reshape(rows, group, model), 1)
    grad_fc, grad_proj = weight_grads(flat_hidden, grad_inner, cot, activated)
    grad_fc_sum, grad_proj_sum = scatter(grad_fc), scatter(grad_proj)
    if pair:
        mlp_back = mlp_back.astype(BF)
        other_out = swap(full_out)
        other_mlp = swap(mlp_out + mlp_back[0, 0, 0] * 0)

    bias = by_pair(b_qkv[None], width)
    own_tokens, own_cot = part_of(tokens, 1, mine), part_of(cotangent, 1, mine)
    grad_packed, grad_qkv, attended = [], [], []
    waits = [grad_fc, own_tokens, own_cot]
    for n, row_grad in enumerate(row_grads):
        out, grads = attention(
            row_hidden, weights, bias, n * (wide // LANES), row_grad, index - start, start,
            part if pair else 0, waits,
        )
        attended.append(out)
        grad_packed.append(grads)
        grad_qkv.append(sum(dot(h.T, g) for h, g in zip(row_hidden, grads)).astype(BF))
        waits = [out, grad_fc_sum, mlp_back]
        if pair:
            waits.append(other_out)
    mixed = to_blocks(jnp.concatenate(attended, 1).reshape(blocks, group, width), rows).reshape(count, width)
    grad_bqkv = jnp.concatenate([sum(jnp.sum(g.astype(F32), 0) for g in grads) for grads in grad_packed])
    grad_qkv = jnp.concatenate(grad_qkv, 1)
    grad_qkv_sum = scatter(grad_qkv)

    if pair:
        grad_tokens, norm_sums = input_grads(
            [g[0] for g in grad_packed], [g[1] for g in grad_packed], weights, own_tokens, own_cot, mlp_back,
            ln_gain[None], [grad_qkv, grad_proj_sum, other_mlp],
        )
        norm_sums = norm_sums[:2]
        branches = mlp_out.astype(F32) + other_mlp.astype(F32)
        branches += tokens.reshape(count, model).astype(F32) + (b_out + norm_sums[0, 0] * 0)
        branches += dot(jnp.concatenate([mixed, swap(mixed)], 1), jnp.concatenate([full_out, other_out], 1).T)
        result = branches.astype(BF).reshape(rows, group, model)
        norm_sums = norm_sums + mixed[0, 0].astype(F32) * 0
    else:
        grads = jnp.concatenate([g[0] for g in grad_packed], 1)
        back = sum_parts(nt(grads, full_qkv).reshape(blocks, group, model), 1).astype(BF)
        grad_hidden = mlp_back + to_blocks(back, rows).astype(F32)
        branches = mlp_out.astype(F32) + nt(mixed, full_out)
        branches = sum_parts(branches.reshape(rows, group, model), 1)
        result = join_parts((own_tokens.astype(F32) + branches + b_out).astype(BF), 1)
        normal, scale = normalize(own_tokens.astype(F32))
        grad_normal = grad_hidden * ln_gain
        grad_inputs = scale * (
            grad_normal
            - jnp.mean(grad_normal, -1, keepdims=True)
            - normal * jnp.mean(grad_normal * normal, -1, keepdims=True)
        )
        grad_tokens = join_parts((own_cot.astype(F32) + grad_inputs).astype(BF), 1)
        norm_sums = jnp.stack([jnp.sum(grad_hidden * normal, (0, 1)), jnp.sum(grad_hidden, (0, 1))])

    grad_out = lax.all_to_all(dot(cot.T, mixed).astype(BF), ("dp", "blk"), 0, 0, tiled=True)
    grad_out_sum = jnp.sum(grad_out.reshape(-1, shard.shape[0], width).astype(F32), 0)

    norm_sums = jnp.concatenate([norm_sums, jnp.sum(own_cot.astype(F32), (0, 1))[None]]).reshape(-1, LANES)
    sums = jnp.concatenate([norm_sums, grad_bqkv.reshape(-1, LANES), grad_bfc.reshape(-1, LANES)], 0)
    sums = sum_all(sums, ("dp", "blk"))
    bias_sums = sums[norm_sums.shape[0]:].reshape(-1)
    norm_sums = sum_all(sums[:norm_sums.shape[0]], ("tensor",)).reshape(3, model)
    return (
        result,
        grad_tokens,
        norm_sums[0],
        norm_sums[1],
        by_kind(grad_qkv_sum, width),
        by_kind(bias_sums[None, :3 * width], width)[0],
        grad_out_sum.T,
        grad_fc_sum,
        bias_sums[3 * width:],
        grad_proj_sum.T,
        norm_sums[2],
    )


def solution(mesh):
    in_specs = (
        P("dp", "blk", None),
        P(),
        P(),
        P(("dp", "blk"), None, "tensor"),
        P(None, "tensor"),
        P("tensor", ("dp", "blk")),
        P(("dp", "blk"), "tensor"),
        P("tensor"),
        P("tensor", ("dp", "blk")),
        P(),
        P("dp", None),
        P("dp", "blk", None),
    )
    out_specs = (
        P("dp", "blk", None),
        P("dp", "blk", None),
        P(),
        P(),
        P(("dp", "blk"), None, "tensor"),
        P(None, "tensor"),
        P("tensor", ("dp", "blk")),
        P(("dp", "blk"), "tensor"),
        P("tensor"),
        P("tensor", ("dp", "blk")),
        P(),
    )
    return jax.shard_map(local, mesh=mesh, in_specs=in_specs, out_specs=out_specs, check_vma=False)
```

```python
import functools

import jax
import jax.numpy as jnp
from jax import lax
from jax.experimental import pallas as pl
from jax.experimental.pallas import tpu as pltpu
from jax.sharding import PartitionSpec as P

HEAD_DIM = 64
ROT_DIM = 16
LANES = 128
EPSILON = 1e-05
BF = jnp.bfloat16
F32 = jnp.float32
MIB = 1024 * 1024


def nt(a, b):
    return lax.dot_general(a, b, (((1,), (1,)), ((), ())), preferred_element_type=F32)


def nn(a, b):
    return lax.dot_general(a, b, (((1,), (0,)), ((), ())), preferred_element_type=F32)


def attn_kernel(bq, bk, part, waits, lo_ref, hi_ref, *refs):
    count = 2 if part else 1
    hidden, refs = refs[:count], refs[count + waits:]
    w_ref, bias_ref, do_ref, cos_ref, sin_ref, start_ref, o_ref = refs[:7]
    grads, refs = refs[7:7 + count], refs[7 + count:]
    (q2, qt, ks, vx, s_buf, p_buf, d_buf, dkt, dvt, keep, ahead, behind, starts) = refs
    length = do_ref.shape[0]
    nq = length // bq
    lane = lax.broadcasted_iota(jnp.int32, (1, LANES), 1)
    first = lane < HEAD_DIM
    half = ROT_DIM // 2
    to_score = HEAD_DIM ** (-0.5) * 1.4426950408889634
    mine_first = lax.axis_index("tensor") == 0 if part else None

    def load(base, size):
        if part:
            rows = []
            for n in range(size // (2 * part)):
                at = pl.ds(pl.multiple_of(base // 2 + n * part, part), part)
                a, b = hidden[0][at, :], hidden[1][at, :]
                rows += [jnp.where(mine_first, a, b), jnp.where(mine_first, b, a)]
            rows = jnp.concatenate(rows, 0)
        else:
            rows = hidden[0][pl.ds(base, size), :]
        packed = nn(rows, w_ref[...]) + bias_ref[...]
        return [packed[:, n * LANES:(n + 1) * LANES] for n in range(3)]

    def store(base, which, value):
        cols = slice(which * LANES, (which + 1) * LANES)
        size = value.shape[0]
        if not part:
            grads[0][pl.ds(base, size), cols] = value.astype(BF)
            return
        for n in range(size // (2 * part)):
            at = pl.ds(pl.multiple_of(base // 2 + n * part, part), part)
            a = value[2 * n * part:(2 * n + 1) * part]
            b = value[(2 * n + 1) * part:(2 * n + 2) * part]
            grads[0][at, cols] = jnp.where(mine_first, a, b).astype(BF)
            grads[1][at, cols] = jnp.where(mine_first, b, a).astype(BF)

    def rot(u, rows):
        return (u * keep[rows, :] + pltpu.roll(u, LANES - half, 1) * ahead[rows, :]
                + pltpu.roll(u, half, 1) * behind[rows, :])

    def rot_back(u, rows):
        return (u * keep[rows, :] + pltpu.roll(u * behind[rows, :], LANES - half, 1)
                + pltpu.roll(u * ahead[rows, :], half, 1))

    def tables(i, _):
        rows = pl.ds(pl.multiple_of(i * bq, bq), bq)
        c, s = cos_ref[:, rows], sin_ref[:, rows]
        rest = HEAD_DIM - ROT_DIM
        one, zero, gap = jnp.ones((rest, bq), F32), jnp.zeros((rest, bq), F32), jnp.zeros((half, bq), F32)
        keep[rows, :] = jnp.concatenate([c, c, one] * 2, 0).T
        ahead[rows, :] = jnp.concatenate([-s, gap, zero] * 2, 0).T
        behind[rows, :] = jnp.concatenate([gap, s, zero] * 2, 0).T
        starts[rows, :] = jnp.broadcast_to(start_ref[:, rows], (LANES, bq)).T
        return 0

    @pl.when(pl.program_id(0) == 0)
    def _():
        lax.fori_loop(0, nq, tables, 0)

    def prep(i, _):
        base = pl.multiple_of(i * bq, bq)
        rows = pl.ds(base, bq)
        q, k, v = load(base, bq)
        q = rot(q, rows)
        qs = (q * to_score).astype(BF)
        zero = jnp.zeros_like(qs)
        q2[0, rows, :] = jnp.where(first, qs, zero)
        q2[1, rows, :] = jnp.where(first, zero, qs)
        qt[:, rows] = q.T.astype(BF)
        ks[rows, :] = rot(k, rows).astype(BF)
        vx[rows, :LANES] = v.astype(BF)
        vx[rows, LANES:] = jnp.ones((bq, LANES), BF)
        dkt[:, rows] = jnp.zeros((LANES, bq), F32)
        dvt[:, rows] = jnp.zeros((LANES, bq), F32)
        return 0

    lax.fori_loop(0, nq, prep, 0)

    def q_block(i, _):
        rows = pl.ds(pl.multiple_of(i * bq, bq), bq)
        last = (i * bq) // bk
        least = lo_ref[i] // bk
        masked = jnp.clip((hi_ref[i] + bk - 1) // bk, least, last)
        q_h = (q2[0, rows, :], q2[1, rows, :])
        start = starts[rows, :]

        def scores(j, mx, mode):
            cols = pl.ds(pl.multiple_of(j * bk, bk), bk)
            k = ks[cols, :]
            out = []
            for h in range(2):
                s = nt(q_h[h], k)
                m = mx[h]
                for t in range(bk // LANES):
                    piece = s[:, t * LANES:(t + 1) * LANES]
                    if mode:
                        kidx = (j * bk + t * LANES + lane).astype(F32)
                        ok = kidx >= start
                        if mode == 2:
                            qidx = (i * bq + lax.broadcasted_iota(jnp.int32, (bq, 1), 0)).astype(F32)
                            ok = ok & (kidx <= qidx)
                        piece = jnp.where(ok, piece, -1e30)
                    s_buf[h, :, pl.ds(pl.multiple_of(j * bk + t * LANES, LANES), LANES)] = piece
                    m = jnp.maximum(m, piece)
                out.append(m)
            return tuple(out)

        mx = (jnp.full((bq, LANES), -1e30, F32),) * 2
        mx = lax.fori_loop(least, masked, lambda j, m: scores(j, m, 1), mx)
        mx = lax.fori_loop(masked, last, lambda j, m: scores(j, m, 0), mx)
        mx = scores(last, mx, 2)
        mx = [jnp.max(m, -1, keepdims=True) for m in mx]

        def weigh(j, acc):
            cols = pl.ds(pl.multiple_of(j * bk, bk), bk)
            v = vx[cols, :]
            out = []
            for h in range(2):
                p = jnp.exp2(s_buf[h, :, cols] - mx[h]).astype(BF)
                p_buf[h, :, cols] = p
                out.append(acc[h] + nn(p, v))
            return tuple(out)

        acc = (jnp.zeros((bq, 2 * LANES), F32),) * 2
        acc = lax.fori_loop(least, last + 1, weigh, acc)
        inv = [1.0 / a[:, LANES:] for a in acc]
        outs = [a[:, :LANES] * r for a, r in zip(acc, inv)]
        o = jnp.where(first, outs[0], outs[1])
        o_ref[rows, :] = o.astype(BF)
        do = do_ref[rows, :].astype(F32)
        dos, dots, deltas = [], [], []
        for h in range(2):
            mine = first if h == 0 else jnp.logical_not(first)
            d = jnp.where(mine, do * inv[h], 0.0).astype(BF)
            dos.append(d)
            df = d.astype(F32)
            deltas.append(jnp.sum(df * o, -1, keepdims=True))
            dots.append(df.T[h * HEAD_DIM:(h + 1) * HEAD_DIM].astype(BF))
        q_t = qt[:, rows]

        def back(j, acc):
            cols = pl.ds(pl.multiple_of(j * bk, bk), bk)
            v = vx[cols, :LANES]
            k = ks[cols, :]
            out = []
            for h in range(2):
                rows_h = slice(h * HEAD_DIM, (h + 1) * HEAD_DIM)
                p = p_buf[h, :, cols]
                dp = nt(dos[h], v)
                ds = (p.astype(F32) * (dp - deltas[h])).astype(BF)
                dvt[rows_h, cols] += nn(dots[h], p)
                dkt[rows_h, cols] += nn(q_t[rows_h], ds)
                out.append(acc[h] + nn(ds, k))
            return tuple(out)

        acc = (jnp.zeros((bq, LANES), F32),) * 2
        acc = lax.fori_loop(least, last + 1, back, acc)
        dq = jnp.where(first, acc[0], acc[1]) * HEAD_DIM ** (-0.5)
        store(i * bq, 0, rot_back(dq, rows))
        return 0

    def static_block(i):
        rows = slice(i * bq, (i + 1) * bq)
        width = (i + 1) * bq
        start = starts[rows, :]
        q_h = (q2[0, rows, :], q2[1, rows, :])
        mx = []
        for h in range(2):
            m = jnp.full((bq, LANES), -1e30, F32)
            for j in range(0, width, bk):
                s = nt(q_h[h], ks[j:j + bk, :])
                for t in range(0, bk, LANES):
                    kidx = (j + t + lane).astype(F32)
                    ok = kidx >= start
                    if j + t + LANES > i * bq:
                        qidx = (i * bq + lax.broadcasted_iota(jnp.int32, (bq, 1), 0)).astype(F32)
                        ok = ok & (kidx <= qidx)
                    piece = jnp.where(ok, s[:, t:t + LANES], -1e30)
                    s_buf[h, :, j + t:j + t + LANES] = piece
                    m = jnp.maximum(m, piece)
            mx.append(jnp.broadcast_to(jnp.max(m, -1, keepdims=True), (bq, LANES)))
        acc = []
        for h in range(2):
            for t in range(0, width, LANES):
                p_buf[h, :, t:t + LANES] = jnp.exp2(s_buf[h, :, t:t + LANES] - mx[h]).astype(BF)
            acc.append(nn(p_buf[h, :, :width], vx[:width, :]))
        inv = [1.0 / v[:, LANES:] for v in acc]
        outs = [v[:, :LANES] * r for v, r in zip(acc, inv)]
        o = jnp.where(first, outs[0], outs[1])
        o_ref[rows, :] = o.astype(BF)
        do = do_ref[rows, :].astype(F32)
        dq = []
        for h in range(2):
            mine = first if h == 0 else jnp.logical_not(first)
            rows_h = slice(h * HEAD_DIM, (h + 1) * HEAD_DIM)
            d = jnp.where(mine, do * inv[h], 0.0).astype(BF)
            df = d.astype(F32)
            delta = jnp.broadcast_to(jnp.sum(df * o, -1, keepdims=True), (bq, LANES))
            d_t = df.T[rows_h].astype(BF)
            q_t = qt[rows_h, rows]
            for j in range(0, width, bk):
                cols = slice(j, j + bk)
                dp = nt(d, vx[cols, :LANES])
                dvt[rows_h, cols] += nn(d_t, p_buf[h, :, cols])
                for t in range(0, bk, LANES):
                    at = slice(j + t, j + t + LANES)
                    d_buf[h, :, at] = (p_buf[h, :, at].astype(F32) * (dp[:, t:t + LANES] - delta)).astype(BF)
                dkt[rows_h, cols] += nn(q_t, d_buf[h, :, cols])
            dq.append(nn(d_buf[h, :, :width], ks[:width, :]))
        dq = jnp.where(first, dq[0], dq[1]) * HEAD_DIM ** (-0.5)
        store(i * bq, 0, rot_back(dq, rows))

    if nq <= 4:
        for i in range(nq):
            static_block(i)
    else:
        lax.fori_loop(0, nq, q_block, 0)

    def finish(i, _):
        base = pl.multiple_of(i * bq, bq)
        rows = pl.ds(base, bq)
        store(base, 1, rot_back(dkt[:, rows].T * HEAD_DIM ** (-0.5), rows))
        store(base, 2, dvt[:, rows].T)
        return 0

    lax.fori_loop(0, nq, finish, 0)


def attention(hidden, weights, bias, first_pair, do, position, start, part=0, waits=(), bq=512, bk=512):
    length, width = do.shape
    bq = min(bq, 2 ** 20 // length)
    bk = max(bq, min(bk, length))
    pairs = width // LANES
    freqs = 10000.0 ** (-jnp.arange(0, ROT_DIM, 2, dtype=F32) / ROT_DIM)
    phase = position.astype(F32)[None] * freqs[:, None]
    by_block = start.reshape(length // bq, bq)
    rows, model = hidden[0].shape
    once = pl.Buffered(1)
    columns = pl.BlockSpec((length, LANES), lambda g, *_: (0, g))
    triple = pl.BlockSpec((rows, 3 * LANES), lambda g, *_: (0, g))
    whole = lambda n: pl.BlockSpec((n, length), lambda g, *_: (0, 0), pipeline_mode=once)
    tri_out = jax.ShapeDtypeStruct((rows, 3 * width), BF)
    static = length // bq <= 4
    out = pl.pallas_call(
        functools.partial(attn_kernel, bq, bk, part, len(waits)),
        out_shape=[jax.ShapeDtypeStruct((length, width), BF)] + [tri_out] * len(hidden),
        grid_spec=pltpu.PrefetchScalarGridSpec(
            num_scalar_prefetch=2,
            grid=(pairs,),
            in_specs=[pl.BlockSpec((rows, model), lambda g, *_: (0, 0), pipeline_mode=once)] * len(hidden)
            + [pl.BlockSpec(memory_space=pl.ANY)] * len(waits)
            + [
                pl.BlockSpec((model, 3 * LANES), lambda g, *_: (0, first_pair + g)),
                pl.BlockSpec((1, 3 * LANES), lambda g, *_: (0, first_pair + g)),
                columns, whole(ROT_DIM // 2), whole(ROT_DIM // 2), whole(1),
            ],
            out_specs=[columns] + [triple] * len(hidden),
            scratch_shapes=[
                pltpu.VMEM((2, length, LANES), BF),
                pltpu.VMEM((LANES, length), BF),
                pltpu.VMEM((length, LANES), BF),
                pltpu.VMEM((length, 2 * LANES), BF),
                pltpu.VMEM((2, bq, length), F32),
                pltpu.VMEM((2, bq, length), BF),
                pltpu.VMEM((2, bq, length) if static else (8, LANES), BF),
                pltpu.VMEM((LANES, length), F32),
                pltpu.VMEM((LANES, length), F32),
            ] + [pltpu.VMEM((length, LANES), F32)] * 4,
        ),
        compiler_params=pltpu.CompilerParams(vmem_limit_bytes=56 * MIB),
        cost_estimate=pl.CostEstimate(flops=1000, bytes_accessed=1000, transcendentals=0),
    )(by_block.min(1), by_block.max(1), *hidden, *waits, weights, bias, do, jnp.cos(phase), jnp.sin(phase),
      start.astype(F32)[None])
    return out[0], list(out[1:])


MESH = pl.DeviceIdType.MESH


def remote(src, dst, send, recv, target):
    return pltpu.make_async_remote_copy(
        src_ref=src, dst_ref=dst, send_sem=send, recv_sem=recv, device_id=target, device_id_type=MESH
    )


def meet(others):
    barrier = pltpu.get_barrier_semaphore()
    for target in others:
        pl.semaphore_signal(barrier, inc=1, device_id=target, device_id_type=MESH)
    pl.semaphore_wait(barrier, len(others))


def gather_kernel(x_ref, tok_ref, gain_ref, bias_ref, out_ref, hid_ref, local_sem, recv, up, down, across, over):
    size = x_ref.shape[0]
    core, block = lax.axis_index("dp"), lax.axis_index("blk")
    z, y = block // 2, lax.rem(block, 2)
    depth = lax.axis_size("blk") // 2
    above, below = {"blk": block + 2}, {"blk": block - 2}
    beside, sibling = {"blk": block + 1 - 2 * y}, {"dp": 1 - core}

    def place(c, zz, yy):
        return (c * depth + zz) * 2 + yy

    def chunk(at):
        return out_ref.at[pl.ds(pl.multiple_of(at * size, size), size)]

    def copy(src, at, sem, target):
        return pltpu.make_async_remote_copy(
            src_ref=src, dst_ref=chunk(at), send_sem=sem, recv_sem=recv.at[at],
            device_id=target, device_id_type=pl.DeviceIdType.MESH,
        )

    def arrived(at):
        copy(chunk(at), at, local_sem, sibling).wait_recv()

    barrier = pltpu.get_barrier_semaphore()

    def greet(target):
        pl.semaphore_signal(barrier, inc=1, device_id=target, device_id_type=pl.DeviceIdType.MESH)

    def not_top(action):
        pl.when(z < depth - 1)(action)

    def not_bottom(action):
        pl.when(z > 0)(action)

    not_top(lambda: greet(above))
    not_bottom(lambda: greet(below))
    greet(beside)
    greet(sibling)
    pl.semaphore_wait(barrier, 2 + jnp.where(z > 0, 1, 0) + jnp.where(z < depth - 1, 1, 0))

    mine = place(core, z, y)
    keep = pltpu.make_async_copy(x_ref, chunk(mine), local_sem)
    not_top(lambda: copy(x_ref, mine, up.at[z], above).start())
    not_bottom(lambda: copy(x_ref, mine, down.at[z], below).start())
    copy(x_ref, mine, across.at[z], beside).start()
    copy(x_ref, mine, over.at[z * 2 + y], sibling).start()
    keep.start()

    for r in range(tok_ref.shape[0]):
        x = tok_ref[r].astype(F32)
        x = x - jnp.mean(x, -1, keepdims=True)
        x = x * lax.rsqrt(jnp.mean(x * x, -1, keepdims=True) + EPSILON)
        hid_ref[r] = (x * gain_ref[...] + bias_ref[...]).astype(BF)

    def from_beside(zz):
        at = place(core, zz, 1 - y)
        arrived(at)
        copy(chunk(at), at, over.at[zz * 2 + 1 - y], sibling).start()

    def from_line(zz, onward, sems, target):
        at = place(core, zz, y)
        arrived(at)
        onward(lambda: copy(chunk(at), at, sems.at[zz], target).start())
        copy(chunk(at), at, across.at[zz], beside).start()
        copy(chunk(at), at, over.at[zz * 2 + y], sibling).start()

    for step in range(1, depth):
        pl.when(z >= step)(lambda: from_line(z - step, not_top, up, above))
        pl.when(z + step < depth)(lambda: from_line(z + step, not_bottom, down, below))
    from_beside(z)
    for step in range(1, depth):
        pl.when(z >= step)(lambda: from_beside(z - step))
        pl.when(z + step < depth)(lambda: from_beside(z + step))

    keep.wait()
    for zz in range(depth):
        for yy in range(2):
            arrived(place(1 - core, zz, yy))
            copy(x_ref, mine, over.at[zz * 2 + yy], sibling).wait_send()
        copy(x_ref, mine, across.at[zz], beside).wait_send()
        pl.when((zz <= z) & (z < depth - 1))(lambda: copy(x_ref, mine, up.at[zz], above).wait_send())
        pl.when((zz >= z) & (z > 0))(lambda: copy(x_ref, mine, down.at[zz], below).wait_send())


def gather_weights(shard, tokens, gain, bias):
    cores, blocks = lax.axis_size("dp"), lax.axis_size("blk")
    rows, columns = shard.shape
    dma = pltpu.SemaphoreType.DMA
    hbm, vmem = pl.BlockSpec(memory_space=pl.ANY), pl.BlockSpec(memory_space=pltpu.VMEM)
    return pl.pallas_call(
        gather_kernel,
        out_shape=[
            jax.ShapeDtypeStruct((cores * blocks * rows, columns), shard.dtype),
            jax.ShapeDtypeStruct(tokens.shape, BF),
        ],
        in_specs=[hbm, vmem, vmem, vmem],
        out_specs=[hbm, vmem],
        scratch_shapes=[
            dma, dma((cores * blocks,)), dma((blocks // 2,)), dma((blocks // 2,)),
            dma((blocks // 2,)), dma((blocks,)),
        ],
        compiler_params=pltpu.CompilerParams(
            collective_id=0, has_side_effects=True, vmem_limit_bytes=32 * MIB
        ),
    )(shard, tokens, gain, bias)


class RowTransfer:
    def __init__(self, hid_ref, mine_ref, other_ref, blank, blank_sem, hid_send, hid_recv, side_send, side_recv):
        self.refs = hid_ref, mine_ref, other_ref, blank
        self.sems = blank_sem, hid_send, hid_recv, side_send, side_recv
        self.rows, group, _ = hid_ref.shape
        self.part = group // 2
        self.block, self.half = lax.axis_index("blk"), lax.axis_index("tensor")
        self.blocks = lax.axis_size("blk")
        self.has_row = self.block < self.rows
        self.facing = {"tensor": 1 - self.half}

    def piece(self, ref, at):
        return ref.at[pl.ds(pl.multiple_of(at * self.part, self.part), self.part)]

    def source(self, r):
        return self.refs[0].at[r, pl.ds(pl.multiple_of(self.half * self.part, self.part), self.part)]

    def row_copy(self, r):
        _, hid_send, hid_recv, _, _ = self.sems
        mine = self.piece(self.refs[1], self.block)
        return remote(self.source(r), mine, hid_send.at[r], hid_recv.at[self.block], {"blk": r})

    def own_row(self):
        return pltpu.make_async_copy(
            self.source(self.block), self.piece(self.refs[1], self.block), self.sems[1].at[self.block]
        )

    def side_copy(self, s):
        _, _, _, side_send, side_recv = self.sems
        _, mine, other, _ = self.refs
        return remote(self.piece(mine, s), self.piece(other, s), side_send.at[s], side_recv.at[s], self.facing)

    def blanks(self):
        _, mine, other, blank = self.refs
        return [
            pltpu.make_async_copy(blank, self.piece(ref, s), self.sems[0].at[n * self.blocks + s])
            for n, ref in enumerate((mine, other)) for s in range(self.blocks)
        ]

    def to_block(self, n, action):
        r = lax.rem(self.block + n, self.blocks)
        pl.when(r < self.rows)(lambda: action(self.row_copy(r)))

    def start(self):
        meet([{"blk": lax.rem(self.block + n, self.blocks)} for n in range(1, self.blocks)] + [self.facing])
        for n in range(1, self.blocks):
            self.to_block(n, lambda copy: copy.start())

        @pl.when(self.has_row)
        def _():
            self.own_row().start()
            self.own_row().wait()
            self.side_copy(self.block).start()

        @pl.when(jnp.logical_not(self.has_row))
        def _():
            self.refs[3][...] = jnp.zeros_like(self.refs[3])
            for copy in self.blanks():
                copy.start()

    def onward(self, n):
        @pl.when(self.has_row)
        def _():
            s = lax.rem(self.block + self.blocks - n, self.blocks)
            mine = self.piece(self.refs[1], s)
            remote(mine, mine, self.sems[3].at[s], self.sems[2].at[s], self.facing).wait_recv()
            self.side_copy(s).start()

    def finish(self):
        for n in range(1, self.blocks):
            self.to_block(n, lambda copy: copy.wait_send())

        @pl.when(self.has_row)
        def _():
            for s in range(self.blocks):
                self.side_copy(s).wait()

        @pl.when(jnp.logical_not(self.has_row))
        def _():
            for copy in self.blanks():
                copy.wait()


def tail_kernel(groups, waits, *refs):
    g_mine, g_other, heads = refs[:groups], refs[groups:2 * groups], refs[2 * groups:3 * groups]
    (w_ref, tok_ref, cot_ref, add_ref, gain_ref, extra_ref, out_ref, sum_ref, wgrad_ref, mixed_ref, facing_ref,
     sent, got, home_send, home, grads, mix, total, terms, inbox, norms, small, small_in, small_box, small_out,
     a_send, a_recv, b_send, b_recv, c_send, c_recv, c_local, d_send, d_recv, e_send, e_recv, e_local,
     f_send, f_recv, g_send, g_recv, h_send, h_recv, i_send, i_recv) = refs[3 * groups + waits:]
    rows, part, model = tok_ref.shape
    block, half = lax.axis_index("blk"), lax.axis_index("tensor")
    blocks = lax.axis_size("blk")
    facing = {"tensor": 1 - half}
    has_row = block < rows
    count = lax.axis_size("dp") * blocks
    me = lax.axis_index("dp") * blocks + block

    def peers():
        return [lax.rem(me + n, count) for n in range(1, count)]

    def device(j):
        return {"dp": j // blocks, "blk": lax.rem(j, blocks)}

    meet([device(j) for j in peers()] + [facing])

    def product(parts, s):
        at, total, first = pl.ds(pl.multiple_of(s * part, part), part), None, 0
        for g in parts:
            width = g.shape[1]
            term = nt(g[at, :], w_ref[:, first:first + width])
            total, first = term if total is None else total + term, first + width
        return total

    def across(s):
        return remote(sent.at[s], got.at[s], a_send.at[s], a_recv.at[s], facing)

    def homeward(s):
        return remote(home_send.at[s], home.at[block], b_send.at[s], b_recv.at[block], {"blk": s})

    def own_half(ref, r):
        return ref.at[r, pl.ds(pl.multiple_of(half * part, part), part)]

    def share(r):
        return remote(grads.at[r], own_half(out_ref, r), c_send.at[r], c_recv.at[r], facing)

    def keep(r):
        return pltpu.make_async_copy(grads.at[r], own_half(out_ref, r), c_local.at[r])

    def heads_of(ref, k, r):
        wide = heads[k].shape[1]
        return ref.at[r, :, k * wide:(k + 1) * wide]

    def attended(k, s):
        return heads[k].at[pl.ds(pl.multiple_of(s * 2 * part, 2 * part), 2 * part)]

    def heads_home(k, s):
        return remote(attended(k, s), heads_of(mix, k, block), d_send.at[k * blocks + s],
                      d_recv.at[k * blocks + block], {"blk": s})

    def own_heads(k):
        return pltpu.make_async_copy(attended(k, block), heads_of(mix, k, block), d_send.at[k * blocks + block])

    def heads_across(k, r):
        return remote(heads_of(mix, k, r), heads_of(facing_ref, k, r), e_send.at[k * blocks + r],
                      e_recv.at[k * blocks + r], facing)

    @pl.when(has_row)
    def _():
        for n in range(blocks):
            s = lax.rem(block + n, blocks)
            sent[s] = product(g_other, s).astype(BF)
            across(s).start()
            for k in range(groups):
                if n == 0:
                    own_heads(k).start()
                else:
                    heads_home(k, s).start()

    def keep_heads(r):
        return pltpu.make_async_copy(mix.at[r], mixed_ref.at[r], e_local.at[r])

    norms[...] = jnp.zeros_like(norms)
    total[...] = jnp.zeros_like(total)

    def forward(n):
        s = lax.rem(block + n, blocks)

        @pl.when(has_row)
        def _():
            grad = product(g_mine, s)
            across(s).wait_recv()
            grad = (grad + got[s].astype(F32)).astype(BF)
            if n == 0:
                home[s] = grad
            else:
                home_send[s] = grad
                homeward(s).start()

    def norm(n):
        r = lax.rem(block + blocks - n, blocks)

        @pl.when(r < rows)
        def _():
            for k in range(groups):
                if n:
                    here = heads_of(mix, k, r)
                    remote(here, here, e_send.at[k * blocks + r], d_recv.at[k * blocks + r], facing).wait_recv()
                else:
                    own_heads(k).wait()
                heads_across(k, r).start()
            keep_heads(r).start()
            if n:
                remote(home_send.at[r], home.at[r], b_send.at[r], b_recv.at[r], facing).wait_recv()
            grad = home[r].astype(F32) + add_ref[r].astype(F32)
            x = tok_ref[r].astype(F32)
            x = x - jnp.mean(x, -1, keepdims=True)
            scale = lax.rsqrt(jnp.mean(x * x, -1, keepdims=True) + EPSILON)
            x = x * scale
            norms[0:1, :] += jnp.sum(grad * x, 0, keepdims=True)
            norms[1:2, :] += jnp.sum(grad, 0, keepdims=True)
            grad = grad * gain_ref[...]
            grad = grad - jnp.mean(grad, -1, keepdims=True) - x * jnp.mean(grad * x, -1, keepdims=True)
            own = cot_ref[r, pl.ds(pl.multiple_of(half * part, part), part), :]
            grads[r] = (own.astype(F32) + scale * grad).astype(BF)
            share(r).start()
            keep(r).start()
            total[...] += nn(cot_ref[r].T, mix[r])

    lag = 2
    for n in range(blocks + lag):
        if n < blocks:
            forward(n)
        if n >= lag:
            norm(n - lag)

    size = terms.shape[1]
    for j in range(count):
        terms[j] = total[j * size:(j + 1) * size].astype(BF)

    def term(j):
        return remote(terms.at[j], inbox.at[me], f_send.at[j], f_recv.at[me], device(j))

    for j in peers():
        term(j).start()

    small[...] = extra_ref[...]
    lines = norms.shape[1] // LANES
    for n in range(2):
        for k in range(lines):
            small[n * lines + k:n * lines + k + 1, :] = norms[n:n + 1, k * LANES:(k + 1) * LANES]
    shared = small.at[pl.ds(0, 3 * lines)]
    swapped = remote(shared, small_in, g_send, g_recv, facing)
    swapped.start()
    swapped.wait()
    small[:3 * lines, :] += small_in[...]

    def line(ref, j):
        return ref.at[pl.ds(pl.multiple_of(j * 8, 8), 8)]

    def small_term(j):
        return remote(line(small, j), small_box.at[me], h_send.at[j], h_recv.at[me], device(j))

    def small_sum(j):
        return remote(line(small_out, me), line(small_out, me), i_send.at[j], i_recv.at[me], device(j))

    for j in peers():
        small_term(j).start()
    small_box[me] = small[pl.ds(pl.multiple_of(me * 8, 8), 8), :]
    for j in peers():
        remote(small_box.at[j], small_box.at[j], h_send.at[j], h_recv.at[j], device(j)).wait_recv()
    added = small_box[0]
    for j in range(1, count):
        added = added + small_box[j]
    small_out[pl.ds(pl.multiple_of(me * 8, 8), 8), :] = added
    for j in peers():
        small_sum(j).start()
    inbox[me] = terms[me]
    for j in peers():
        remote(inbox.at[j], inbox.at[j], f_send.at[j], f_recv.at[j], device(j)).wait_recv()
    added = inbox[0].astype(F32)
    for j in range(1, count):
        added = added + inbox[j].astype(F32)
    wgrad_ref[...] = added
    for j in peers():
        remote(line(small_out, j), line(small_out, j), i_send.at[j], i_recv.at[j], device(j)).wait_recv()
    sum_ref[...] = small_out[...]
    for j in peers():
        term(j).wait_send()
        small_term(j).wait_send()
        small_sum(j).wait_send()

    for r in range(rows):
        share(r).wait()
        keep(r).wait()
        keep_heads(r).wait()
        for k in range(groups):
            heads_across(k, r).wait()

    @pl.when(has_row)
    def _():
        for s in range(blocks):
            across(s).wait_send()
        for n in range(1, blocks):
            homeward(lax.rem(block + n, blocks)).wait_send()
            for k in range(groups):
                heads_home(k, lax.rem(block + n, blocks)).wait_send()


def go_home(g_mine, g_other, attended, weights, tokens, cot, add, gain, extra, waits=()):
    rows, part, model = tokens.shape
    blocks = lax.axis_size("blk")
    wide = sum(g.shape[1] for g in g_mine)
    dma = pltpu.SemaphoreType.DMA
    groups, hbm = len(g_mine), pl.BlockSpec(memory_space=pl.ANY)
    count = lax.axis_size("dp") * blocks
    wide_heads = sum(o.shape[1] for o in attended)
    lines = 3 * model // LANES
    heads = jax.ShapeDtypeStruct((rows, 2 * part, wide_heads), BF)
    vmem = pl.BlockSpec(memory_space=pltpu.VMEM)
    return pl.pallas_call(
        functools.partial(tail_kernel, groups, len(waits)),
        grid=(1,),
        out_shape=[jax.ShapeDtypeStruct((rows, 2 * part, model), BF), jax.ShapeDtypeStruct((8 * count, LANES), F32),
                   jax.ShapeDtypeStruct((model // count, wide_heads), F32), heads, heads],
        in_specs=[vmem] * (2 * groups) + [hbm] * (groups + len(waits))
        + [pl.BlockSpec((model, wide), lambda i: (0, 0))] + [vmem] * 5,
        out_specs=[hbm, vmem, vmem, hbm, hbm],
        scratch_shapes=[pltpu.VMEM((blocks, part, model), BF)] * 4 + [pltpu.VMEM((rows, part, model), BF)]
        + [pltpu.VMEM(heads.shape, BF), pltpu.VMEM((model, wide_heads), F32)]
        + [pltpu.VMEM((count, model // count, wide_heads), BF)] * 2
        + [pltpu.VMEM((8, model), F32), pltpu.VMEM((8 * count, LANES), F32), pltpu.VMEM((lines, LANES), F32)]
        + [pltpu.VMEM((count, 8, LANES), F32), pltpu.VMEM((8 * count, LANES), F32)]
        + [dma((blocks,))] * 4 + [dma((rows,))] * 3 + [dma((groups * blocks,))] * 4 + [dma((rows,))]
        + [dma((count,))] * 2 + [dma] * 2 + [dma((count,))] * 4,
        compiler_params=pltpu.CompilerParams(
            collective_id=1, has_side_effects=True, vmem_limit_bytes=56 * MIB
        ),
        cost_estimate=pl.CostEstimate(flops=1000, bytes_accessed=1000, transcendentals=0),
    )(*g_mine, *g_other, *attended, *waits, weights, tokens, cot, add, gain, extra)


def weight_grad_kernel(half, waits, a_ref, b_ref, *refs):
    x_ref, y_ref, ax_ref, by_ref, turned = refs[waits:]
    step = pl.program_id(0)

    @pl.when(step == 0)
    def _():
        turned[...] = a_ref[...].T

    @pl.when(step == half)
    def _():
        turned[...] = b_ref[...].T

    @pl.when(step < half)
    def _():
        ax_ref[...] = nn(turned[...], x_ref[...]).astype(BF)

    @pl.when(step >= half)
    def _():
        by_ref[...] = nn(turned[...], y_ref[...]).astype(BF)


def weight_grads(a, x, b, y, waits=(), tile=512):
    count, model = a.shape
    inner = x.shape[1]
    tile = min(tile, inner)
    half = inner // tile
    whole = pl.BlockSpec((count, model), lambda i: (0, 0), pipeline_mode=pl.Buffered(1))
    return pl.pallas_call(
        functools.partial(weight_grad_kernel, half, len(waits)),
        grid=(2 * half,),
        out_shape=[jax.ShapeDtypeStruct((model, inner), BF)] * 2,
        in_specs=[
            whole, whole, *[pl.BlockSpec(memory_space=pl.ANY)] * len(waits),
            pl.BlockSpec((count, tile), lambda i: (0, jnp.minimum(i, half - 1))),
            pl.BlockSpec((count, tile), lambda i: (0, jnp.maximum(i - half, 0))),
        ],
        out_specs=[
            pl.BlockSpec((model, tile), lambda i: (0, jnp.minimum(i, half - 1))),
            pl.BlockSpec((model, tile), lambda i: (0, jnp.maximum(i - half, 0))),
        ],
        scratch_shapes=[pltpu.VMEM((model, count), BF)],
        compiler_params=pltpu.CompilerParams(vmem_limit_bytes=48 * MIB),
        cost_estimate=pl.CostEstimate(flops=1000, bytes_accessed=1000, transcendentals=0),
    )(a, b, *waits, x, y)


def mlp_kernel(tile, waits, moves, hid_ref, cot_ref, wf_ref, wp_ref, bias_ref, *refs):
    refs = refs[waits:]
    act_ref, gin_ref, res_ref, back_ref, gb_ref = refs[moves:moves + 5]
    if moves:
        step, steps = pl.program_id(0), pl.num_programs(0)
        rows = RowTransfer(refs[0], *refs[moves + 5:])
        pl.when(step == 0)(rows.start)
        for n in range(1, rows.blocks):
            pl.when(step == jnp.minimum(n, steps - 1))(lambda: rows.onward(n))
    hid, cot = hid_ref[...], cot_ref[...]

    @pl.when(pl.program_id(0) == 0)
    def _():
        gb_ref[...] = jnp.zeros_like(gb_ref)

    res = back = None
    for n in range(wf_ref.shape[1] // tile):
        cols = slice(n * tile, (n + 1) * tile)
        wf, wp = wf_ref[:, cols], wp_ref[:, cols]
        inner = nn(hid, wf) + bias_ref[:, cols]
        grad_act = nn(cot, wp)
        size = jnp.abs(inner)
        t = 1.0 / (1.0 + (0.3275911 * 0.7071067811865476) * size)
        bell = jnp.exp2((-0.5 * 1.4426950408889634) * inner * inner)
        tail = ((((0.5 * 1.061405429 * t - 0.5 * 1.453152027) * t + 0.5 * 1.421413741) * t
                 - 0.5 * 0.284496736) * t + 0.5 * 0.254829592) * t * bell
        below = jnp.where(inner < 0, tail, 1.0 - tail)
        act = (inner * below).astype(BF)
        grad_inner = (grad_act * (below + inner * (bell * 0.3989422804014327))).astype(BF)
        act_ref[:, cols] = act
        gin_ref[:, cols] = grad_inner
        gb_ref[:, cols] += jnp.sum(grad_inner.astype(F32), 0, keepdims=True)
        r, b = nt(act, wp), nt(grad_inner, wf)
        res, back = (r, b) if res is None else (res + r, back + b)
    res_ref[...] = res.astype(BF)
    back_ref[...] = back.astype(BF)
    if moves:
        pl.when(step == steps - 1)(rows.finish)


def mlp(hidden, cot, weights, first_block, bias, waits=(), moved=None, size=256, tile=512):
    count, model = hidden.shape
    inner = bias.shape[1]
    tile = min(tile, inner)
    rows = lambda n: pl.BlockSpec((size, n), lambda i: (i, 0))
    matrix = lambda n: pl.BlockSpec((model, inner), lambda i: (0, first_block + n), pipeline_mode=pl.Buffered(1))
    vector = pl.BlockSpec((1, inner), lambda i: (0, 0))
    hbm = pl.BlockSpec(memory_space=pl.ANY)
    shape = lambda n: jax.ShapeDtypeStruct((count, n), BF)
    moves, outs, scratch, params = (), [], [], {}
    if moved is not None:
        blocks, dma = lax.axis_size("blk"), pltpu.SemaphoreType.DMA
        part = moved.shape[1] // 2
        moves, outs = (moved,), [jax.ShapeDtypeStruct((blocks * part, model), BF)] * 2
        scratch = [pltpu.VMEM((part, model), BF), dma((2 * blocks,))] + [dma((blocks,))] * 4
        params = dict(collective_id=2, has_side_effects=True)
    return pl.pallas_call(
        functools.partial(mlp_kernel, tile, len(waits), len(moves)),
        grid=(count // size,),
        out_shape=[shape(inner), shape(inner), shape(model), shape(model), jax.ShapeDtypeStruct((1, inner), F32)] + outs,
        in_specs=[rows(model), rows(model), matrix(0), matrix(1), vector] + [hbm] * (len(waits) + len(moves)),
        out_specs=[rows(inner), rows(inner), rows(model), rows(model), vector] + [hbm] * len(outs),
        scratch_shapes=scratch,
        compiler_params=pltpu.CompilerParams(vmem_limit_bytes=56 * MIB, **params),
        cost_estimate=pl.CostEstimate(flops=1000, bytes_accessed=1000, transcendentals=0),
    )(hidden, cot, weights, weights, bias, *waits, *moves)


def normalize(values):
    center = values - jnp.mean(values, -1, keepdims=True)
    spread = jnp.mean(center * center, -1, keepdims=True)
    scale = lax.rsqrt(spread + EPSILON)
    return center * scale, scale


def swap(value):
    return lax.ppermute(value, "tensor", [(0, 1), (1, 0)])


def split_tensor(value, axis):
    shape = value.shape
    parts = lax.axis_size("tensor")
    return value.reshape(shape[:axis] + (parts, shape[axis] // parts) + shape[axis + 1:])


def part_of(value, axis, which):
    return lax.dynamic_index_in_dim(split_tensor(value, axis), which, axis, keepdims=False)


def sum_parts(value, axis):
    mine = lax.axis_index("tensor")
    if lax.axis_size("tensor") == 2:
        other = swap(part_of(value, axis, 1 - mine).astype(BF))
        return part_of(value, axis, mine).astype(F32) + other.astype(F32)
    return lax.psum_scatter(
        value.astype(BF), "tensor", scatter_dimension=axis, tiled=True
    ).astype(F32)


def join_parts(value, axis):
    if lax.axis_size("tensor") != 2:
        return lax.all_gather(value, "tensor", axis=axis, tiled=True)
    other = swap(value)
    first = lax.axis_index("tensor") == 0
    low, high = jnp.where(first, value, other), jnp.where(first, other, value)
    return jnp.concatenate([low, high], axis)


def to_rows(value):
    blocks = lax.axis_size("blk")
    pad = jnp.zeros((blocks - value.shape[0],) + value.shape[1:], value.dtype)
    return lax.all_to_all(jnp.concatenate([value, pad], 0), "blk", 0, 0, tiled=True)


def to_blocks(value, rows):
    return lax.all_to_all(value, "blk", 0, 0, tiled=True)[:rows]


def sum_all(value, axes):
    for axis in axes:
        size = lax.axis_size(axis)
        step = 1
        while step < size:
            value = value + lax.ppermute(value, axis, [(i, i ^ step) for i in range(size)])
            step *= 2
    return value


def by_pair(value, width):
    count = value.shape[0]
    return value.reshape(count, 3, width // LANES, LANES).transpose(0, 2, 1, 3).reshape(count, 3 * width)


def by_kind(value, width):
    count = value.shape[0]
    return value.reshape(count, width // LANES, 3, LANES).transpose(0, 2, 1, 3).reshape(count, 3, width)


def scatter(value):
    return lax.psum_scatter(value, ("dp", "blk"), scatter_dimension=0, tiled=True).astype(F32)


def dot(a, b):
    return jnp.dot(a, b, preferred_element_type=F32)


def local(
    tokens, ln_gain, ln_bias, w_qkv, b_qkv, w_out, w_fc, b_fc, w_proj, b_out, bounds, cotangent
):
    rows, group, model = tokens.shape
    width, inner = b_qkv.shape[1], b_fc.shape[0]
    blocks, parts = lax.axis_size("blk"), lax.axis_size("tensor")
    length = blocks * group
    count = rows * group
    part = group // parts

    mine = lax.axis_index("tensor")
    pair = parts == 2 and (lax.axis_size("dp"), blocks) == (2, 8)
    cot = cotangent.reshape(count, model)

    shard = jnp.concatenate([by_pair(w_qkv, width), w_out.T, w_fc, w_proj.T], 1)
    if pair:
        weights, hidden = gather_weights(shard, tokens, ln_gain[None], ln_bias[None])
    else:
        hidden = (normalize(tokens.astype(F32))[0] * ln_gain + ln_bias).astype(BF)
        weights = lax.all_gather(shard, ("dp", "blk"), axis=0, tiled=True)
        row_hidden = [join_parts(to_rows(part_of(hidden, 1, mine)), 1).reshape(length, model)]
    flat_hidden = hidden.reshape(count, model)
    full_qkv, full_out = weights[:, :3 * width], weights[:, 3 * width:4 * width]

    row_bounds = lax.dynamic_index_in_dim(
        bounds, jnp.minimum(lax.axis_index("blk"), rows - 1), 0, keepdims=False
    )
    index = jnp.arange(length, dtype=jnp.int32)
    start = jnp.max(jnp.where(row_bounds[:, None] <= index[None], row_bounds[:, None], 0), 0)

    groups = max(1, width // (2 * LANES))
    wide = width // groups
    cuts = [slice(n * wide, (n + 1) * wide) for n in range(groups)]
    grad_mixed = dot(cot, full_out).astype(BF).reshape(rows, group, width)
    row_grads = [to_rows(grad_mixed[:, :, cut]).reshape(length, wide) for cut in cuts]

    activated, grad_inner, mlp_out, mlp_back, grad_bfc, *moved = mlp(
        flat_hidden, cot, weights, 4 * width // inner, b_fc[None], (grad_mixed,), hidden if pair else None
    )
    row_hidden = moved or row_hidden
    mlp_back = sum_parts(mlp_back.reshape(rows, group, model), 1)
    grad_fc, grad_proj = weight_grads(flat_hidden, grad_inner, cot, activated, [row_grads[0]])
    grad_fc_sum, grad_proj_sum = scatter(grad_fc), scatter(grad_proj)
    if pair:
        mlp_back = mlp_back.astype(BF)
        other_out = swap(full_out)
        other_mlp = swap(mlp_out)

    bias = by_pair(b_qkv[None], width)
    own_tokens, own_cot = part_of(tokens, 1, mine), part_of(cotangent, 1, mine)
    grad_packed, grad_qkv, attended = [], [], []
    waits = [grad_fc, own_tokens, own_cot]
    for n, row_grad in enumerate(row_grads):
        out, grads = attention(
            row_hidden, weights, bias, n * (wide // LANES), row_grad, index - start, start,
            part if pair else 0, waits,
        )
        attended.append(out)
        grad_packed.append(grads)
        grad_qkv.append(sum(dot(h.T, g) for h, g in zip(row_hidden, grads)).astype(BF))
        waits = [out, grad_fc_sum]
    grad_bqkv = jnp.concatenate([sum(jnp.sum(g.astype(F32), 0) for g in grads) for grads in grad_packed])
    grad_qkv = jnp.concatenate(grad_qkv, 1)
    grad_qkv_sum = scatter(grad_qkv)

    tensor_sums = jnp.sum(own_cot.astype(F32), (0, 1)).reshape(-1, LANES)
    bias_sums = jnp.concatenate([grad_bfc[0], grad_bqkv]).reshape(-1, LANES)
    lines = model // LANES
    if pair:
        used = 3 * lines + bias_sums.shape[0]
        extra = jnp.zeros((8 * (model // shard.shape[0]), LANES), F32)
        extra = extra.at[2 * lines:3 * lines].set(tensor_sums).at[3 * lines:used].set(bias_sums)
        grad_tokens, sums, grad_out_sum, mixed, other_mixed = go_home(
            [g[0] for g in grad_packed], [g[1] for g in grad_packed], attended, weights, own_tokens, cotangent,
            mlp_back, ln_gain[None], extra, [grad_qkv, grad_proj_sum, other_mlp, other_out],
        )
        norm_sums, bias_sums = sums[:3 * lines].reshape(3, model), sums[3 * lines:used].reshape(-1)
        mixed, other_mixed = mixed.reshape(count, width), other_mixed.reshape(count, width)
        branches = mlp_out.astype(F32) + other_mlp.astype(F32)
        branches += tokens.reshape(count, model).astype(F32) + b_out
        branches += nt(mixed, full_out) + nt(other_mixed, other_out)
        result = branches.astype(BF).reshape(rows, group, model)
    else:
        mixed = jnp.concatenate(attended, 1).reshape(blocks, group, width)
        mixed = to_blocks(mixed, rows).reshape(count, width)
        grads = jnp.concatenate([g[0] for g in grad_packed], 1)
        back = sum_parts(nt(grads, full_qkv).reshape(blocks, group, model), 1).astype(BF)
        grad_hidden = mlp_back + to_blocks(back, rows).astype(F32)
        branches = mlp_out.astype(F32) + nt(mixed, full_out)
        branches = sum_parts(branches.reshape(rows, group, model), 1)
        result = join_parts((own_tokens.astype(F32) + branches + b_out).astype(BF), 1)
        normal, scale = normalize(own_tokens.astype(F32))
        grad_normal = grad_hidden * ln_gain
        grad_inputs = scale * (
            grad_normal
            - jnp.mean(grad_normal, -1, keepdims=True)
            - normal * jnp.mean(grad_normal * normal, -1, keepdims=True)
        )
        grad_tokens = join_parts((own_cot.astype(F32) + grad_inputs).astype(BF), 1)
        norm_sums = jnp.concatenate([jnp.sum(grad_hidden * normal, (0, 1)), jnp.sum(grad_hidden, (0, 1))])
        sums = jnp.concatenate([norm_sums.reshape(-1, LANES), tensor_sums, bias_sums], 0)
        sums = sum_all(sums, ("dp", "blk"))
        norm_sums = sum_all(sums[:3 * lines], ("tensor",)).reshape(3, model)
        bias_sums = sums[3 * lines:].reshape(-1)
        grad_out = lax.all_to_all(dot(cot.T, mixed).astype(BF), ("dp", "blk"), 0, 0, tiled=True)
        grad_out_sum = jnp.sum(grad_out.reshape(-1, shard.shape[0], width).astype(F32), 0)

    return (
        result,
        grad_tokens,
        norm_sums[0],
        norm_sums[1],
        by_kind(grad_qkv_sum, width),
        by_kind(bias_sums[None, inner:], width)[0],
        grad_out_sum.T,
        grad_fc_sum,
        bias_sums[:inner],
        grad_proj_sum.T,
        norm_sums[2],
    )


def solution(mesh):
    in_specs = (
        P("dp", "blk", None),
        P(),
        P(),
        P(("dp", "blk"), None, "tensor"),
        P(None, "tensor"),
        P("tensor", ("dp", "blk")),
        P(("dp", "blk"), "tensor"),
        P("tensor"),
        P("tensor", ("dp", "blk")),
        P(),
        P("dp", None),
        P("dp", "blk", None),
    )
    out_specs = (
        P("dp", "blk", None),
        P("dp", "blk", None),
        P(),
        P(),
        P(("dp", "blk"), None, "tensor"),
        P(None, "tensor"),
        P("tensor", ("dp", "blk")),
        P(("dp", "blk"), "tensor"),
        P("tensor"),
        P("tensor", ("dp", "blk")),
        P(),
    )
    return jax.shard_map(local, mesh=mesh, in_specs=in_specs, out_specs=out_specs, check_vma=False)
```

```python
import functools

import jax
import jax.numpy as jnp
from jax import lax
from jax.experimental import pallas as pl
from jax.experimental.pallas import tpu as pltpu
from jax.sharding import PartitionSpec as P

HEAD_DIM = 64
ROT_DIM = 16
LANES = 128
EPSILON = 1e-05
BF = jnp.bfloat16
F32 = jnp.float32
MIB = 1024 * 1024


def nt(a, b):
    return lax.dot_general(a, b, (((1,), (1,)), ((), ())), preferred_element_type=F32)


def nn(a, b):
    return lax.dot_general(a, b, (((1,), (0,)), ((), ())), preferred_element_type=F32)


def attn_kernel(bq, bk, part, waits, lo_ref, hi_ref, *refs):
    count = 2 if part else 1
    hidden, refs = refs[:count], refs[count + waits:]
    w_ref, bias_ref, do_ref, cos_ref, sin_ref, start_ref, o_ref = refs[:7]
    grads, refs = refs[7:7 + count], refs[7 + count:]
    (q2, qt, ks, vx, s_buf, p_buf, d_buf, dkt, dvt, keep, ahead, behind, starts) = refs
    length = do_ref.shape[0]
    nq = length // bq
    lane = lax.broadcasted_iota(jnp.int32, (1, LANES), 1)
    first = lane < HEAD_DIM
    half = ROT_DIM // 2
    to_score = HEAD_DIM ** (-0.5) * 1.4426950408889634
    mine_first = lax.axis_index("tensor") == 0 if part else None

    def load(base, size):
        if part:
            rows = []
            for n in range(size // (2 * part)):
                at = pl.ds(pl.multiple_of(base // 2 + n * part, part), part)
                a, b = hidden[0][at, :], hidden[1][at, :]
                rows += [jnp.where(mine_first, a, b), jnp.where(mine_first, b, a)]
            rows = jnp.concatenate(rows, 0)
        else:
            rows = hidden[0][pl.ds(base, size), :]
        packed = nn(rows, w_ref[...]) + bias_ref[...]
        return [packed[:, n * LANES:(n + 1) * LANES] for n in range(3)]

    def store(base, which, value):
        cols = slice(which * LANES, (which + 1) * LANES)
        size = value.shape[0]
        if not part:
            grads[0][pl.ds(base, size), cols] = value.astype(BF)
            return
        for n in range(size // (2 * part)):
            at = pl.ds(pl.multiple_of(base // 2 + n * part, part), part)
            a = value[2 * n * part:(2 * n + 1) * part]
            b = value[(2 * n + 1) * part:(2 * n + 2) * part]
            grads[0][at, cols] = jnp.where(mine_first, a, b).astype(BF)
            grads[1][at, cols] = jnp.where(mine_first, b, a).astype(BF)

    def rot(u, rows):
        return (u * keep[rows, :] + pltpu.roll(u, LANES - half, 1) * ahead[rows, :]
                + pltpu.roll(u, half, 1) * behind[rows, :])

    def rot_back(u, rows):
        return (u * keep[rows, :] + pltpu.roll(u * behind[rows, :], LANES - half, 1)
                + pltpu.roll(u * ahead[rows, :], half, 1))

    def tables(i, _):
        rows = pl.ds(pl.multiple_of(i * bq, bq), bq)
        c, s = cos_ref[:, rows], sin_ref[:, rows]
        rest = HEAD_DIM - ROT_DIM
        one, zero, gap = jnp.ones((rest, bq), F32), jnp.zeros((rest, bq), F32), jnp.zeros((half, bq), F32)
        keep[rows, :] = jnp.concatenate([c, c, one] * 2, 0).T
        ahead[rows, :] = jnp.concatenate([-s, gap, zero] * 2, 0).T
        behind[rows, :] = jnp.concatenate([gap, s, zero] * 2, 0).T
        starts[rows, :] = jnp.broadcast_to(start_ref[:, rows], (LANES, bq)).T
        return 0

    @pl.when(pl.program_id(0) == 0)
    def _():
        lax.fori_loop(0, nq, tables, 0)

    def prep(i, _):
        base = pl.multiple_of(i * bq, bq)
        rows = pl.ds(base, bq)
        q, k, v = load(base, bq)
        q = rot(q, rows)
        qs = (q * to_score).astype(BF)
        zero = jnp.zeros_like(qs)
        q2[0, rows, :] = jnp.where(first, qs, zero)
        q2[1, rows, :] = jnp.where(first, zero, qs)
        qt[:, rows] = q.T.astype(BF)
        ks[rows, :] = rot(k, rows).astype(BF)
        vx[rows, :LANES] = v.astype(BF)
        vx[rows, LANES:] = jnp.ones((bq, LANES), BF)
        dkt[:, rows] = jnp.zeros((LANES, bq), F32)
        dvt[:, rows] = jnp.zeros((LANES, bq), F32)
        return 0

    lax.fori_loop(0, nq, prep, 0)

    def q_block(i, _):
        rows = pl.ds(pl.multiple_of(i * bq, bq), bq)
        last = (i * bq) // bk
        least = lo_ref[i] // bk
        masked = jnp.clip((hi_ref[i] + bk - 1) // bk, least, last)
        q_h = (q2[0, rows, :], q2[1, rows, :])
        start = starts[rows, :]

        def scores(j, mx, mode):
            cols = pl.ds(pl.multiple_of(j * bk, bk), bk)
            k = ks[cols, :]
            out = []
            for h in range(2):
                s = nt(q_h[h], k)
                m = mx[h]
                for t in range(bk // LANES):
                    piece = s[:, t * LANES:(t + 1) * LANES]
                    if mode:
                        kidx = (j * bk + t * LANES + lane).astype(F32)
                        ok = kidx >= start
                        if mode == 2:
                            qidx = (i * bq + lax.broadcasted_iota(jnp.int32, (bq, 1), 0)).astype(F32)
                            ok = ok & (kidx <= qidx)
                        piece = jnp.where(ok, piece, -1e30)
                    s_buf[h, :, pl.ds(pl.multiple_of(j * bk + t * LANES, LANES), LANES)] = piece
                    m = jnp.maximum(m, piece)
                out.append(m)
            return tuple(out)

        mx = (jnp.full((bq, LANES), -1e30, F32),) * 2
        mx = lax.fori_loop(least, masked, lambda j, m: scores(j, m, 1), mx)
        mx = lax.fori_loop(masked, last, lambda j, m: scores(j, m, 0), mx)
        mx = scores(last, mx, 2)
        mx = [jnp.max(m, -1, keepdims=True) for m in mx]

        def weigh(j, acc):
            cols = pl.ds(pl.multiple_of(j * bk, bk), bk)
            v = vx[cols, :]
            out = []
            for h in range(2):
                p = jnp.exp2(s_buf[h, :, cols] - mx[h]).astype(BF)
                p_buf[h, :, cols] = p
                out.append(acc[h] + nn(p, v))
            return tuple(out)

        acc = (jnp.zeros((bq, 2 * LANES), F32),) * 2
        acc = lax.fori_loop(least, last + 1, weigh, acc)
        inv = [1.0 / a[:, LANES:] for a in acc]
        outs = [a[:, :LANES] * r for a, r in zip(acc, inv)]
        o = jnp.where(first, outs[0], outs[1])
        o_ref[rows, :] = o.astype(BF)
        do = do_ref[rows, :].astype(F32)
        dos, dots, deltas = [], [], []
        for h in range(2):
            mine = first if h == 0 else jnp.logical_not(first)
            d = jnp.where(mine, do * inv[h], 0.0).astype(BF)
            dos.append(d)
            df = d.astype(F32)
            deltas.append(jnp.sum(df * o, -1, keepdims=True))
            dots.append(df.T[h * HEAD_DIM:(h + 1) * HEAD_DIM].astype(BF))
        q_t = qt[:, rows]

        def back(j, acc):
            cols = pl.ds(pl.multiple_of(j * bk, bk), bk)
            v = vx[cols, :LANES]
            k = ks[cols, :]
            out = []
            for h in range(2):
                rows_h = slice(h * HEAD_DIM, (h + 1) * HEAD_DIM)
                p = p_buf[h, :, cols]
                dp = nt(dos[h], v)
                ds = (p.astype(F32) * (dp - deltas[h])).astype(BF)
                dvt[rows_h, cols] += nn(dots[h], p)
                dkt[rows_h, cols] += nn(q_t[rows_h], ds)
                out.append(acc[h] + nn(ds, k))
            return tuple(out)

        acc = (jnp.zeros((bq, LANES), F32),) * 2
        acc = lax.fori_loop(least, last + 1, back, acc)
        dq = jnp.where(first, acc[0], acc[1]) * HEAD_DIM ** (-0.5)
        store(i * bq, 0, rot_back(dq, rows))
        return 0

    def static_block(i):
        rows = slice(i * bq, (i + 1) * bq)
        width = (i + 1) * bq
        start = starts[rows, :]
        q_h = (q2[0, rows, :], q2[1, rows, :])
        mx = []
        for h in range(2):
            m = jnp.full((bq, LANES), -1e30, F32)
            for j in range(0, width, bk):
                s = nt(q_h[h], ks[j:j + bk, :])
                for t in range(0, bk, LANES):
                    kidx = (j + t + lane).astype(F32)
                    ok = kidx >= start
                    if j + t + LANES > i * bq:
                        qidx = (i * bq + lax.broadcasted_iota(jnp.int32, (bq, 1), 0)).astype(F32)
                        ok = ok & (kidx <= qidx)
                    piece = jnp.where(ok, s[:, t:t + LANES], -1e30)
                    s_buf[h, :, j + t:j + t + LANES] = piece
                    m = jnp.maximum(m, piece)
            mx.append(jnp.broadcast_to(jnp.max(m, -1, keepdims=True), (bq, LANES)))
        acc = []
        for h in range(2):
            for t in range(0, width, LANES):
                p_buf[h, :, t:t + LANES] = jnp.exp2(s_buf[h, :, t:t + LANES] - mx[h]).astype(BF)
            acc.append(nn(p_buf[h, :, :width], vx[:width, :]))
        inv = [1.0 / v[:, LANES:] for v in acc]
        outs = [v[:, :LANES] * r for v, r in zip(acc, inv)]
        o = jnp.where(first, outs[0], outs[1])
        o_ref[rows, :] = o.astype(BF)
        do = do_ref[rows, :].astype(F32)
        dq = []
        for h in range(2):
            mine = first if h == 0 else jnp.logical_not(first)
            rows_h = slice(h * HEAD_DIM, (h + 1) * HEAD_DIM)
            d = jnp.where(mine, do * inv[h], 0.0).astype(BF)
            df = d.astype(F32)
            delta = jnp.broadcast_to(jnp.sum(df * o, -1, keepdims=True), (bq, LANES))
            d_t = df.T[rows_h].astype(BF)
            q_t = qt[rows_h, rows]
            for j in range(0, width, bk):
                cols = slice(j, j + bk)
                dp = nt(d, vx[cols, :LANES])
                dvt[rows_h, cols] += nn(d_t, p_buf[h, :, cols])
                for t in range(0, bk, LANES):
                    at = slice(j + t, j + t + LANES)
                    d_buf[h, :, at] = (p_buf[h, :, at].astype(F32) * (dp[:, t:t + LANES] - delta)).astype(BF)
                dkt[rows_h, cols] += nn(q_t, d_buf[h, :, cols])
            dq.append(nn(d_buf[h, :, :width], ks[:width, :]))
        dq = jnp.where(first, dq[0], dq[1]) * HEAD_DIM ** (-0.5)
        store(i * bq, 0, rot_back(dq, rows))

    if nq <= 4:
        for i in range(nq):
            static_block(i)
    else:
        lax.fori_loop(0, nq, q_block, 0)

    def finish(i, _):
        base = pl.multiple_of(i * bq, bq)
        rows = pl.ds(base, bq)
        store(base, 1, rot_back(dkt[:, rows].T * HEAD_DIM ** (-0.5), rows))
        store(base, 2, dvt[:, rows].T)
        return 0

    lax.fori_loop(0, nq, finish, 0)


def attention(hidden, weights, bias, first_pair, do, position, start, part=0, waits=(), bq=512, bk=512):
    length, width = do.shape
    bq = min(bq, 2 ** 20 // length)
    bk = max(bq, min(bk, length))
    pairs = width // LANES
    freqs = 10000.0 ** (-jnp.arange(0, ROT_DIM, 2, dtype=F32) / ROT_DIM)
    phase = position.astype(F32)[None] * freqs[:, None]
    by_block = start.reshape(length // bq, bq)
    rows, model = hidden[0].shape
    once = pl.Buffered(1)
    columns = pl.BlockSpec((length, LANES), lambda g, *_: (0, g))
    triple = pl.BlockSpec((rows, 3 * LANES), lambda g, *_: (0, g))
    whole = lambda n: pl.BlockSpec((n, length), lambda g, *_: (0, 0), pipeline_mode=once)
    tri_out = jax.ShapeDtypeStruct((rows, 3 * width), BF)
    static = length // bq <= 4
    out = pl.pallas_call(
        functools.partial(attn_kernel, bq, bk, part, len(waits)),
        out_shape=[jax.ShapeDtypeStruct((length, width), BF)] + [tri_out] * len(hidden),
        grid_spec=pltpu.PrefetchScalarGridSpec(
            num_scalar_prefetch=2,
            grid=(pairs,),
            in_specs=[pl.BlockSpec((rows, model), lambda g, *_: (0, 0), pipeline_mode=once)] * len(hidden)
            + [pl.BlockSpec(memory_space=pl.ANY)] * len(waits)
            + [
                pl.BlockSpec((model, 3 * LANES), lambda g, *_: (0, first_pair + g)),
                pl.BlockSpec((1, 3 * LANES), lambda g, *_: (0, first_pair + g)),
                columns, whole(ROT_DIM // 2), whole(ROT_DIM // 2), whole(1),
            ],
            out_specs=[columns] + [triple] * len(hidden),
            scratch_shapes=[
                pltpu.VMEM((2, length, LANES), BF),
                pltpu.VMEM((LANES, length), BF),
                pltpu.VMEM((length, LANES), BF),
                pltpu.VMEM((length, 2 * LANES), BF),
                pltpu.VMEM((2, bq, length), F32),
                pltpu.VMEM((2, bq, length), BF),
                pltpu.VMEM((2, bq, length) if static else (8, LANES), BF),
                pltpu.VMEM((LANES, length), F32),
                pltpu.VMEM((LANES, length), F32),
            ] + [pltpu.VMEM((length, LANES), F32)] * 4,
        ),
        compiler_params=pltpu.CompilerParams(vmem_limit_bytes=56 * MIB),
        cost_estimate=pl.CostEstimate(flops=1000, bytes_accessed=1000, transcendentals=0),
    )(by_block.min(1), by_block.max(1), *hidden, *waits, weights, bias, do, jnp.cos(phase), jnp.sin(phase),
      start.astype(F32)[None])
    return out[0], list(out[1:])


MESH = pl.DeviceIdType.MESH


def remote(src, dst, send, recv, target):
    return pltpu.make_async_remote_copy(
        src_ref=src, dst_ref=dst, send_sem=send, recv_sem=recv, device_id=target, device_id_type=MESH
    )


def meet(others):
    barrier = pltpu.get_barrier_semaphore()
    for target in others:
        pl.semaphore_signal(barrier, inc=1, device_id=target, device_id_type=MESH)
    pl.semaphore_wait(barrier, len(others))


def gather_kernel(x_ref, tok_ref, gain_ref, bias_ref, out_ref, hid_ref, local_sem, recv, up, down, across, over):
    size = x_ref.shape[0]
    core, block = lax.axis_index("dp"), lax.axis_index("blk")
    z, y = block // 2, lax.rem(block, 2)
    depth = lax.axis_size("blk") // 2
    above, below = {"blk": block + 2}, {"blk": block - 2}
    beside, sibling = {"blk": block + 1 - 2 * y}, {"dp": 1 - core}

    def place(c, zz, yy):
        return (c * depth + zz) * 2 + yy

    def chunk(at):
        return out_ref.at[pl.ds(pl.multiple_of(at * size, size), size)]

    def copy(src, at, sem, target):
        return pltpu.make_async_remote_copy(
            src_ref=src, dst_ref=chunk(at), send_sem=sem, recv_sem=recv.at[at],
            device_id=target, device_id_type=pl.DeviceIdType.MESH,
        )

    def arrived(at):
        copy(chunk(at), at, local_sem, sibling).wait_recv()

    barrier = pltpu.get_barrier_semaphore()

    def greet(target):
        pl.semaphore_signal(barrier, inc=1, device_id=target, device_id_type=pl.DeviceIdType.MESH)

    def not_top(action):
        pl.when(z < depth - 1)(action)

    def not_bottom(action):
        pl.when(z > 0)(action)

    not_top(lambda: greet(above))
    not_bottom(lambda: greet(below))
    greet(beside)
    greet(sibling)
    pl.semaphore_wait(barrier, 2 + jnp.where(z > 0, 1, 0) + jnp.where(z < depth - 1, 1, 0))

    mine = place(core, z, y)
    keep = pltpu.make_async_copy(x_ref, chunk(mine), local_sem)
    not_top(lambda: copy(x_ref, mine, up.at[z], above).start())
    not_bottom(lambda: copy(x_ref, mine, down.at[z], below).start())
    copy(x_ref, mine, across.at[z], beside).start()
    copy(x_ref, mine, over.at[z * 2 + y], sibling).start()
    keep.start()

    for r in range(tok_ref.shape[0]):
        x = tok_ref[r].astype(F32)
        x = x - jnp.mean(x, -1, keepdims=True)
        x = x * lax.rsqrt(jnp.mean(x * x, -1, keepdims=True) + EPSILON)
        hid_ref[r] = (x * gain_ref[...] + bias_ref[...]).astype(BF)

    def from_beside(zz):
        at = place(core, zz, 1 - y)
        arrived(at)
        copy(chunk(at), at, over.at[zz * 2 + 1 - y], sibling).start()

    def from_line(zz, onward, sems, target):
        at = place(core, zz, y)
        arrived(at)
        onward(lambda: copy(chunk(at), at, sems.at[zz], target).start())
        copy(chunk(at), at, across.at[zz], beside).start()
        copy(chunk(at), at, over.at[zz * 2 + y], sibling).start()

    for step in range(1, depth):
        pl.when(z >= step)(lambda: from_line(z - step, not_top, up, above))
        pl.when(z + step < depth)(lambda: from_line(z + step, not_bottom, down, below))
    from_beside(z)
    for step in range(1, depth):
        pl.when(z >= step)(lambda: from_beside(z - step))
        pl.when(z + step < depth)(lambda: from_beside(z + step))

    keep.wait()
    for zz in range(depth):
        for yy in range(2):
            arrived(place(1 - core, zz, yy))
            copy(x_ref, mine, over.at[zz * 2 + yy], sibling).wait_send()
        copy(x_ref, mine, across.at[zz], beside).wait_send()
        pl.when((zz <= z) & (z < depth - 1))(lambda: copy(x_ref, mine, up.at[zz], above).wait_send())
        pl.when((zz >= z) & (z > 0))(lambda: copy(x_ref, mine, down.at[zz], below).wait_send())


def gather_weights(shard, tokens, gain, bias):
    cores, blocks = lax.axis_size("dp"), lax.axis_size("blk")
    rows, columns = shard.shape
    dma = pltpu.SemaphoreType.DMA
    hbm, vmem = pl.BlockSpec(memory_space=pl.ANY), pl.BlockSpec(memory_space=pltpu.VMEM)
    return pl.pallas_call(
        gather_kernel,
        out_shape=[
            jax.ShapeDtypeStruct((cores * blocks * rows, columns), shard.dtype),
            jax.ShapeDtypeStruct(tokens.shape, BF),
        ],
        in_specs=[hbm, vmem, vmem, vmem],
        out_specs=[hbm, vmem],
        scratch_shapes=[
            dma, dma((cores * blocks,)), dma((blocks // 2,)), dma((blocks // 2,)),
            dma((blocks // 2,)), dma((blocks,)),
        ],
        compiler_params=pltpu.CompilerParams(
            collective_id=0, has_side_effects=True, vmem_limit_bytes=32 * MIB
        ),
    )(shard, tokens, gain, bias)


class RowTransfer:
    def __init__(self, hid_ref, mine_ref, other_ref, blank, blank_sem, hid_send, hid_recv, side_send, side_recv):
        self.refs = hid_ref, mine_ref, other_ref, blank
        self.sems = blank_sem, hid_send, hid_recv, side_send, side_recv
        self.rows, group, _ = hid_ref.shape
        self.part = group // 2
        self.block, self.half = lax.axis_index("blk"), lax.axis_index("tensor")
        self.blocks = lax.axis_size("blk")
        self.has_row = self.block < self.rows
        self.facing = {"tensor": 1 - self.half}

    def piece(self, ref, at):
        return ref.at[pl.ds(pl.multiple_of(at * self.part, self.part), self.part)]

    def source(self, r):
        return self.refs[0].at[r, pl.ds(pl.multiple_of(self.half * self.part, self.part), self.part)]

    def row_copy(self, r):
        _, hid_send, hid_recv, _, _ = self.sems
        mine = self.piece(self.refs[1], self.block)
        return remote(self.source(r), mine, hid_send.at[r], hid_recv.at[self.block], {"blk": r})

    def own_row(self):
        return pltpu.make_async_copy(
            self.source(self.block), self.piece(self.refs[1], self.block), self.sems[1].at[self.block]
        )

    def side_copy(self, s):
        _, _, _, side_send, side_recv = self.sems
        _, mine, other, _ = self.refs
        return remote(self.piece(mine, s), self.piece(other, s), side_send.at[s], side_recv.at[s], self.facing)

    def blanks(self):
        _, mine, other, blank = self.refs
        return [
            pltpu.make_async_copy(blank, self.piece(ref, s), self.sems[0].at[n * self.blocks + s])
            for n, ref in enumerate((mine, other)) for s in range(self.blocks)
        ]

    def to_block(self, n, action):
        r = lax.rem(self.block + n, self.blocks)
        pl.when(r < self.rows)(lambda: action(self.row_copy(r)))

    def start(self):
        meet([{"blk": lax.rem(self.block + n, self.blocks)} for n in range(1, self.blocks)] + [self.facing])
        for n in range(1, self.blocks):
            self.to_block(n, lambda copy: copy.start())

        @pl.when(self.has_row)
        def _():
            self.own_row().start()
            self.own_row().wait()
            self.side_copy(self.block).start()

        @pl.when(jnp.logical_not(self.has_row))
        def _():
            self.refs[3][...] = jnp.zeros_like(self.refs[3])
            for copy in self.blanks():
                copy.start()

    def onward(self, n):
        @pl.when(self.has_row)
        def _():
            s = lax.rem(self.block + self.blocks - n, self.blocks)
            mine = self.piece(self.refs[1], s)
            remote(mine, mine, self.sems[3].at[s], self.sems[2].at[s], self.facing).wait_recv()
            self.side_copy(s).start()

    def finish(self):
        for n in range(1, self.blocks):
            self.to_block(n, lambda copy: copy.wait_send())

        @pl.when(self.has_row)
        def _():
            for s in range(self.blocks):
                self.side_copy(s).wait()

        @pl.when(jnp.logical_not(self.has_row))
        def _():
            for copy in self.blanks():
                copy.wait()


def tail_kernel(groups, waits, *refs):
    g_mine, g_other, heads = refs[:groups], refs[groups:2 * groups], refs[2 * groups:3 * groups]
    (w_ref, tok_ref, cot_ref, add_ref, gain_ref, extra_ref, out_ref, sum_ref, wgrad_ref, mixed_ref, facing_ref,
     sent, got, home_send, home, grads, mix, total, terms, inbox, norms, small, small_in, small_box, small_out,
     a_send, a_recv, b_send, b_recv, c_send, c_recv, c_local, d_send, d_recv, e_send, e_recv, e_local,
     f_send, f_recv, g_send, g_recv, h_send, h_recv, i_send, i_recv) = refs[3 * groups + waits:]
    rows, part, model = tok_ref.shape
    block, half = lax.axis_index("blk"), lax.axis_index("tensor")
    blocks = lax.axis_size("blk")
    facing = {"tensor": 1 - half}
    has_row = block < rows
    count = lax.axis_size("dp") * blocks
    me = lax.axis_index("dp") * blocks + block

    def peers():
        return [lax.rem(me + n, count) for n in range(1, count)]

    def device(j):
        return {"dp": j // blocks, "blk": lax.rem(j, blocks)}

    meet([device(j) for j in peers()] + [facing])

    def product(parts, s):
        at, total, first = pl.ds(pl.multiple_of(s * part, part), part), None, 0
        for g in parts:
            width = g.shape[1]
            term = nt(g[at, :], w_ref[:, first:first + width])
            total, first = term if total is None else total + term, first + width
        return total

    def across(s):
        return remote(sent.at[s], got.at[s], a_send.at[s], a_recv.at[s], facing)

    def homeward(s):
        return remote(home_send.at[s], home.at[block], b_send.at[s], b_recv.at[block], {"blk": s})

    def own_half(ref, r):
        return ref.at[r, pl.ds(pl.multiple_of(half * part, part), part)]

    def share(r):
        return remote(grads.at[r], own_half(out_ref, r), c_send.at[r], c_recv.at[r], facing)

    def keep(r):
        return pltpu.make_async_copy(grads.at[r], own_half(out_ref, r), c_local.at[r])

    def heads_of(ref, k, r):
        wide = heads[k].shape[1]
        return ref.at[r, :, k * wide:(k + 1) * wide]

    def attended(k, s):
        return heads[k].at[pl.ds(pl.multiple_of(s * 2 * part, 2 * part), 2 * part)]

    def heads_home(k, s):
        return remote(attended(k, s), heads_of(mix, k, block), d_send.at[k * blocks + s],
                      d_recv.at[k * blocks + block], {"blk": s})

    def own_heads(k):
        return pltpu.make_async_copy(attended(k, block), heads_of(mix, k, block), d_send.at[k * blocks + block])

    def send_heads(k, n):
        if n == 0:
            own_heads(k).start()
        else:
            heads_home(k, lax.rem(block + n, blocks)).start()

    def heads_across(k, r):
        return remote(heads_of(mix, k, r), heads_of(facing_ref, k, r), e_send.at[k * blocks + r],
                      e_recv.at[k * blocks + r], facing)

    @pl.when(has_row)
    def _():
        for n in range(blocks):
            s = lax.rem(block + n, blocks)
            sent[s] = product(g_other, s).astype(BF)
            across(s).start()
            send_heads(0, n)

    def keep_heads(r):
        return pltpu.make_async_copy(mix.at[r], mixed_ref.at[r], e_local.at[r])

    norms[...] = jnp.zeros_like(norms)
    total[...] = jnp.zeros_like(total)

    def forward(n):
        s = lax.rem(block + n, blocks)

        @pl.when(has_row)
        def _():
            grad = product(g_mine, s)
            across(s).wait_recv()
            grad = (grad + got[s].astype(F32)).astype(BF)
            if n == 0:
                home[s] = grad
            else:
                home_send[s] = grad
                homeward(s).start()

    def heads_arrive(k, n, r):
        if n:
            here = heads_of(mix, k, r)
            remote(here, here, e_send.at[k * blocks + r], d_recv.at[k * blocks + r], facing).wait_recv()
        else:
            own_heads(k).wait()
        heads_across(k, r).start()

    def norm(n):
        r = lax.rem(block + blocks - n, blocks)

        @pl.when(r < rows)
        def _():
            heads_arrive(0, n, r)
            if n:
                remote(home_send.at[r], home.at[r], b_send.at[r], b_recv.at[r], facing).wait_recv()
            grad = home[r].astype(F32) + add_ref[r].astype(F32)
            x = tok_ref[r].astype(F32)
            x = x - jnp.mean(x, -1, keepdims=True)
            scale = lax.rsqrt(jnp.mean(x * x, -1, keepdims=True) + EPSILON)
            x = x * scale
            norms[0:1, :] += jnp.sum(grad * x, 0, keepdims=True)
            norms[1:2, :] += jnp.sum(grad, 0, keepdims=True)
            grad = grad * gain_ref[...]
            grad = grad - jnp.mean(grad, -1, keepdims=True) - x * jnp.mean(grad * x, -1, keepdims=True)
            own = cot_ref[r, pl.ds(pl.multiple_of(half * part, part), part), :]
            grads[r] = (own.astype(F32) + scale * grad).astype(BF)
            keep(r).start()

    lag = 2
    for n in range(blocks + lag):
        if n < blocks:
            forward(n)
        if n >= lag:
            norm(n - lag)
        if n == blocks - 1:
            @pl.when(has_row)
            def _():
                for k in range(1, groups):
                    for other in range(blocks):
                        send_heads(k, other)

    small[...] = extra_ref[...]
    lines = norms.shape[1] // LANES
    for n in range(2):
        for k in range(lines):
            small[n * lines + k:n * lines + k + 1, :] = norms[n:n + 1, k * LANES:(k + 1) * LANES]
    shared = small.at[pl.ds(0, 3 * lines)]
    swapped = remote(shared, small_in, g_send, g_recv, facing)
    swapped.start()
    for r in range(rows):
        share(r).start()

    for n in range(blocks):
        r = lax.rem(block + blocks - n, blocks)

        @pl.when(r < rows)
        def _():
            for k in range(1, groups):
                heads_arrive(k, n, r)
            keep_heads(r).start()
            total[...] += nn(cot_ref[r].T, mix[r])

    size = terms.shape[1]
    for j in range(count):
        terms[j] = total[j * size:(j + 1) * size].astype(BF)

    def term(j):
        return remote(terms.at[j], inbox.at[me], f_send.at[j], f_recv.at[me], device(j))

    for j in peers():
        term(j).start()

    swapped.wait()
    small[:3 * lines, :] += small_in[...]

    def line(ref, j):
        return ref.at[pl.ds(pl.multiple_of(j * 8, 8), 8)]

    def small_term(j):
        return remote(line(small, j), small_box.at[me], h_send.at[j], h_recv.at[me], device(j))

    def small_sum(j):
        return remote(line(small_out, me), line(small_out, me), i_send.at[j], i_recv.at[me], device(j))

    for j in peers():
        small_term(j).start()
    small_box[me] = small[pl.ds(pl.multiple_of(me * 8, 8), 8), :]
    for j in peers():
        remote(small_box.at[j], small_box.at[j], h_send.at[j], h_recv.at[j], device(j)).wait_recv()
    added = small_box[0]
    for j in range(1, count):
        added = added + small_box[j]
    small_out[pl.ds(pl.multiple_of(me * 8, 8), 8), :] = added
    for j in peers():
        small_sum(j).start()
    inbox[me] = terms[me]
    for j in peers():
        remote(inbox.at[j], inbox.at[j], f_send.at[j], f_recv.at[j], device(j)).wait_recv()
    added = inbox[0].astype(F32)
    for j in range(1, count):
        added = added + inbox[j].astype(F32)
    wgrad_ref[...] = added
    for j in peers():
        remote(line(small_out, j), line(small_out, j), i_send.at[j], i_recv.at[j], device(j)).wait_recv()
    sum_ref[...] = small_out[...]
    for j in peers():
        term(j).wait_send()
        small_term(j).wait_send()
        small_sum(j).wait_send()

    for r in range(rows):
        share(r).wait()
        keep(r).wait()
        keep_heads(r).wait()
        for k in range(groups):
            heads_across(k, r).wait()

    @pl.when(has_row)
    def _():
        for s in range(blocks):
            across(s).wait_send()
        for n in range(1, blocks):
            homeward(lax.rem(block + n, blocks)).wait_send()
            for k in range(groups):
                heads_home(k, lax.rem(block + n, blocks)).wait_send()


def go_home(g_mine, g_other, attended, weights, tokens, cot, add, gain, extra, waits=()):
    rows, part, model = tokens.shape
    blocks = lax.axis_size("blk")
    wide = sum(g.shape[1] for g in g_mine)
    dma = pltpu.SemaphoreType.DMA
    groups, hbm = len(g_mine), pl.BlockSpec(memory_space=pl.ANY)
    count = lax.axis_size("dp") * blocks
    wide_heads = sum(o.shape[1] for o in attended)
    lines = 3 * model // LANES
    heads = jax.ShapeDtypeStruct((rows, 2 * part, wide_heads), BF)
    vmem = pl.BlockSpec(memory_space=pltpu.VMEM)
    return pl.pallas_call(
        functools.partial(tail_kernel, groups, len(waits)),
        grid=(1,),
        out_shape=[jax.ShapeDtypeStruct((rows, 2 * part, model), BF), jax.ShapeDtypeStruct((8 * count, LANES), F32),
                   jax.ShapeDtypeStruct((model // count, wide_heads), F32), heads, heads],
        in_specs=[vmem] * (2 * groups) + [hbm] * (groups + len(waits))
        + [pl.BlockSpec((model, wide), lambda i: (0, 0))] + [vmem] * 5,
        out_specs=[hbm, vmem, vmem, hbm, hbm],
        scratch_shapes=[pltpu.VMEM((blocks, part, model), BF)] * 4 + [pltpu.VMEM((rows, part, model), BF)]
        + [pltpu.VMEM(heads.shape, BF), pltpu.VMEM((model, wide_heads), F32)]
        + [pltpu.VMEM((count, model // count, wide_heads), BF)] * 2
        + [pltpu.VMEM((8, model), F32), pltpu.VMEM((8 * count, LANES), F32), pltpu.VMEM((lines, LANES), F32)]
        + [pltpu.VMEM((count, 8, LANES), F32), pltpu.VMEM((8 * count, LANES), F32)]
        + [dma((blocks,))] * 4 + [dma((rows,))] * 3 + [dma((groups * blocks,))] * 4 + [dma((rows,))]
        + [dma((count,))] * 2 + [dma] * 2 + [dma((count,))] * 4,
        compiler_params=pltpu.CompilerParams(
            collective_id=1, has_side_effects=True, vmem_limit_bytes=56 * MIB
        ),
        cost_estimate=pl.CostEstimate(flops=1000, bytes_accessed=1000, transcendentals=0),
    )(*g_mine, *g_other, *attended, *waits, weights, tokens, cot, add, gain, extra)


def weight_grad_kernel(half, waits, a_ref, b_ref, *refs):
    x_ref, y_ref, ax_ref, by_ref, turned = refs[waits:]
    step = pl.program_id(0)

    @pl.when(step == 0)
    def _():
        turned[...] = a_ref[...].T

    @pl.when(step == half)
    def _():
        turned[...] = b_ref[...].T

    @pl.when(step < half)
    def _():
        ax_ref[...] = nn(turned[...], x_ref[...]).astype(BF)

    @pl.when(step >= half)
    def _():
        by_ref[...] = nn(turned[...], y_ref[...]).astype(BF)


def weight_grads(a, x, b, y, waits=(), tile=512):
    count, model = a.shape
    inner = x.shape[1]
    tile = min(tile, inner)
    half = inner // tile
    whole = pl.BlockSpec((count, model), lambda i: (0, 0), pipeline_mode=pl.Buffered(1))
    return pl.pallas_call(
        functools.partial(weight_grad_kernel, half, len(waits)),
        grid=(2 * half,),
        out_shape=[jax.ShapeDtypeStruct((model, inner), BF)] * 2,
        in_specs=[
            whole, whole, *[pl.BlockSpec(memory_space=pl.ANY)] * len(waits),
            pl.BlockSpec((count, tile), lambda i: (0, jnp.minimum(i, half - 1))),
            pl.BlockSpec((count, tile), lambda i: (0, jnp.maximum(i - half, 0))),
        ],
        out_specs=[
            pl.BlockSpec((model, tile), lambda i: (0, jnp.minimum(i, half - 1))),
            pl.BlockSpec((model, tile), lambda i: (0, jnp.maximum(i - half, 0))),
        ],
        scratch_shapes=[pltpu.VMEM((model, count), BF)],
        compiler_params=pltpu.CompilerParams(vmem_limit_bytes=48 * MIB),
        cost_estimate=pl.CostEstimate(flops=1000, bytes_accessed=1000, transcendentals=0),
    )(a, b, *waits, x, y)


def mlp_kernel(tile, waits, moves, hid_ref, cot_ref, wf_ref, wp_ref, bias_ref, *refs):
    refs = refs[waits:]
    act_ref, gin_ref, res_ref, back_ref, gb_ref = refs[moves:moves + 5]
    if moves:
        step, steps = pl.program_id(0), pl.num_programs(0)
        rows = RowTransfer(refs[0], *refs[moves + 5:])
        pl.when(step == 0)(rows.start)
        for n in range(1, rows.blocks):
            pl.when(step == jnp.minimum(n, steps - 1))(lambda: rows.onward(n))
    hid, cot = hid_ref[...], cot_ref[...]

    @pl.when(pl.program_id(0) == 0)
    def _():
        gb_ref[...] = jnp.zeros_like(gb_ref)

    res = back = None
    for n in range(wf_ref.shape[1] // tile):
        cols = slice(n * tile, (n + 1) * tile)
        wf, wp = wf_ref[:, cols], wp_ref[:, cols]
        inner = nn(hid, wf) + bias_ref[:, cols]
        grad_act = nn(cot, wp)
        size = jnp.abs(inner)
        t = 1.0 / (1.0 + (0.3275911 * 0.7071067811865476) * size)
        bell = jnp.exp2((-0.5 * 1.4426950408889634) * inner * inner)
        tail = ((((0.5 * 1.061405429 * t - 0.5 * 1.453152027) * t + 0.5 * 1.421413741) * t
                 - 0.5 * 0.284496736) * t + 0.5 * 0.254829592) * t * bell
        below = jnp.where(inner < 0, tail, 1.0 - tail)
        act = (inner * below).astype(BF)
        grad_inner = (grad_act * (below + inner * (bell * 0.3989422804014327))).astype(BF)
        act_ref[:, cols] = act
        gin_ref[:, cols] = grad_inner
        gb_ref[:, cols] += jnp.sum(grad_inner.astype(F32), 0, keepdims=True)
        r, b = nt(act, wp), nt(grad_inner, wf)
        res, back = (r, b) if res is None else (res + r, back + b)
    res_ref[...] = res.astype(BF)
    back_ref[...] = back.astype(BF)
    if moves:
        pl.when(step == steps - 1)(rows.finish)


def mlp(hidden, cot, weights, first_block, bias, waits=(), moved=None, size=256, tile=512):
    count, model = hidden.shape
    inner = bias.shape[1]
    tile = min(tile, inner)
    rows = lambda n: pl.BlockSpec((size, n), lambda i: (i, 0))
    matrix = lambda n: pl.BlockSpec((model, inner), lambda i: (0, first_block + n), pipeline_mode=pl.Buffered(1))
    vector = pl.BlockSpec((1, inner), lambda i: (0, 0))
    hbm = pl.BlockSpec(memory_space=pl.ANY)
    shape = lambda n: jax.ShapeDtypeStruct((count, n), BF)
    moves, outs, scratch, params = (), [], [], {}
    if moved is not None:
        blocks, dma = lax.axis_size("blk"), pltpu.SemaphoreType.DMA
        part = moved.shape[1] // 2
        moves, outs = (moved,), [jax.ShapeDtypeStruct((blocks * part, model), BF)] * 2
        scratch = [pltpu.VMEM((part, model), BF), dma((2 * blocks,))] + [dma((blocks,))] * 4
        params = dict(collective_id=2, has_side_effects=True)
    return pl.pallas_call(
        functools.partial(mlp_kernel, tile, len(waits), len(moves)),
        grid=(count // size,),
        out_shape=[shape(inner), shape(inner), shape(model), shape(model), jax.ShapeDtypeStruct((1, inner), F32)] + outs,
        in_specs=[rows(model), rows(model), matrix(0), matrix(1), vector] + [hbm] * (len(waits) + len(moves)),
        out_specs=[rows(inner), rows(inner), rows(model), rows(model), vector] + [hbm] * len(outs),
        scratch_shapes=scratch,
        compiler_params=pltpu.CompilerParams(vmem_limit_bytes=56 * MIB, **params),
        cost_estimate=pl.CostEstimate(flops=1000, bytes_accessed=1000, transcendentals=0),
    )(hidden, cot, weights, weights, bias, *waits, *moves)


def normalize(values):
    center = values - jnp.mean(values, -1, keepdims=True)
    spread = jnp.mean(center * center, -1, keepdims=True)
    scale = lax.rsqrt(spread + EPSILON)
    return center * scale, scale


def swap(value):
    return lax.ppermute(value, "tensor", [(0, 1), (1, 0)])


def split_tensor(value, axis):
    shape = value.shape
    parts = lax.axis_size("tensor")
    return value.reshape(shape[:axis] + (parts, shape[axis] // parts) + shape[axis + 1:])


def part_of(value, axis, which):
    return lax.dynamic_index_in_dim(split_tensor(value, axis), which, axis, keepdims=False)


def sum_parts(value, axis):
    mine = lax.axis_index("tensor")
    if lax.axis_size("tensor") == 2:
        other = swap(part_of(value, axis, 1 - mine).astype(BF))
        return part_of(value, axis, mine).astype(F32) + other.astype(F32)
    return lax.psum_scatter(
        value.astype(BF), "tensor", scatter_dimension=axis, tiled=True
    ).astype(F32)


def join_parts(value, axis):
    if lax.axis_size("tensor") != 2:
        return lax.all_gather(value, "tensor", axis=axis, tiled=True)
    other = swap(value)
    first = lax.axis_index("tensor") == 0
    low, high = jnp.where(first, value, other), jnp.where(first, other, value)
    return jnp.concatenate([low, high], axis)


def to_rows(value):
    blocks = lax.axis_size("blk")
    pad = jnp.zeros((blocks - value.shape[0],) + value.shape[1:], value.dtype)
    return lax.all_to_all(jnp.concatenate([value, pad], 0), "blk", 0, 0, tiled=True)


def to_blocks(value, rows):
    return lax.all_to_all(value, "blk", 0, 0, tiled=True)[:rows]


def sum_all(value, axes):
    for axis in axes:
        size = lax.axis_size(axis)
        step = 1
        while step < size:
            value = value + lax.ppermute(value, axis, [(i, i ^ step) for i in range(size)])
            step *= 2
    return value


def by_pair(value, width):
    count = value.shape[0]
    return value.reshape(count, 3, width // LANES, LANES).transpose(0, 2, 1, 3).reshape(count, 3 * width)


def by_kind(value, width):
    count = value.shape[0]
    return value.reshape(count, width // LANES, 3, LANES).transpose(0, 2, 1, 3).reshape(count, 3, width)


def scatter(value):
    return lax.psum_scatter(value, ("dp", "blk"), scatter_dimension=0, tiled=True).astype(F32)


def dot(a, b):
    return jnp.dot(a, b, preferred_element_type=F32)


def local(
    tokens, ln_gain, ln_bias, w_qkv, b_qkv, w_out, w_fc, b_fc, w_proj, b_out, bounds, cotangent
):
    rows, group, model = tokens.shape
    width, inner = b_qkv.shape[1], b_fc.shape[0]
    blocks, parts = lax.axis_size("blk"), lax.axis_size("tensor")
    length = blocks * group
    count = rows * group
    part = group // parts

    mine = lax.axis_index("tensor")
    pair = parts == 2 and (lax.axis_size("dp"), blocks) == (2, 8)
    cot = cotangent.reshape(count, model)

    shard = jnp.concatenate([by_pair(w_qkv, width), w_out.T, w_fc, w_proj.T], 1)
    if pair:
        weights, hidden = gather_weights(shard, tokens, ln_gain[None], ln_bias[None])
    else:
        hidden = (normalize(tokens.astype(F32))[0] * ln_gain + ln_bias).astype(BF)
        weights = lax.all_gather(shard, ("dp", "blk"), axis=0, tiled=True)
        row_hidden = [join_parts(to_rows(part_of(hidden, 1, mine)), 1).reshape(length, model)]
    flat_hidden = hidden.reshape(count, model)
    full_qkv, full_out = weights[:, :3 * width], weights[:, 3 * width:4 * width]

    row_bounds = lax.dynamic_index_in_dim(
        bounds, jnp.minimum(lax.axis_index("blk"), rows - 1), 0, keepdims=False
    )
    index = jnp.arange(length, dtype=jnp.int32)
    start = jnp.max(jnp.where(row_bounds[:, None] <= index[None], row_bounds[:, None], 0), 0)

    groups = max(1, width // (2 * LANES))
    wide = width // groups
    cuts = [slice(n * wide, (n + 1) * wide) for n in range(groups)]
    grad_mixed = dot(cot, full_out).astype(BF).reshape(rows, group, width)
    row_grads = [to_rows(grad_mixed[:, :, cut]).reshape(length, wide) for cut in cuts]

    other_out = swap(full_out) if pair else None
    activated, grad_inner, mlp_out, mlp_back, grad_bfc, *moved = mlp(
        flat_hidden, cot, weights, 4 * width // inner, b_fc[None], (grad_mixed,), hidden if pair else None
    )
    row_hidden = moved or row_hidden
    mlp_back = sum_parts(mlp_back.reshape(rows, group, model), 1)
    grad_fc, grad_proj = weight_grads(
        flat_hidden, grad_inner, cot, activated, [row_grads[0]] + [other_out] * pair
    )
    grad_fc_sum, grad_proj_sum = scatter(grad_fc), scatter(grad_proj)
    if pair:
        mlp_back = mlp_back.astype(BF)
        other_mlp = swap(mlp_out)

    bias = by_pair(b_qkv[None], width)
    own_tokens, own_cot = part_of(tokens, 1, mine), part_of(cotangent, 1, mine)
    grad_packed, grad_qkv, attended = [], [], []
    waits = [grad_fc, own_tokens, own_cot]
    for n, row_grad in enumerate(row_grads):
        out, grads = attention(
            row_hidden, weights, bias, n * (wide // LANES), row_grad, index - start, start,
            part if pair else 0, waits,
        )
        attended.append(out)
        grad_packed.append(grads)
        grad_qkv.append(sum(dot(h.T, g) for h, g in zip(row_hidden, grads)).astype(BF))
        waits = [out, grad_fc_sum]
    grad_bqkv = jnp.concatenate([sum(jnp.sum(g.astype(F32), 0) for g in grads) for grads in grad_packed])
    grad_qkv = jnp.concatenate(grad_qkv, 1)
    grad_qkv_sum = scatter(grad_qkv)

    tensor_sums = jnp.sum(own_cot.astype(F32), (0, 1)).reshape(-1, LANES)
    bias_sums = jnp.concatenate([grad_bfc[0], grad_bqkv]).reshape(-1, LANES)
    lines = model // LANES
    if pair:
        used = 3 * lines + bias_sums.shape[0]
        extra = jnp.zeros((8 * (model // shard.shape[0]), LANES), F32)
        extra = extra.at[2 * lines:3 * lines].set(tensor_sums).at[3 * lines:used].set(bias_sums)
        grad_tokens, sums, grad_out_sum, mixed, other_mixed = go_home(
            [g[0] for g in grad_packed], [g[1] for g in grad_packed], attended, weights, own_tokens, cotangent,
            mlp_back, ln_gain[None], extra, [grad_qkv, grad_proj_sum, other_mlp, other_out],
        )
        norm_sums, bias_sums = sums[:3 * lines].reshape(3, model), sums[3 * lines:used].reshape(-1)
        mixed, other_mixed = mixed.reshape(count, width), other_mixed.reshape(count, width)
        branches = mlp_out.astype(F32) + other_mlp.astype(F32)
        branches += tokens.reshape(count, model).astype(F32) + b_out
        branches += nt(mixed, full_out) + nt(other_mixed, other_out)
        result = branches.astype(BF).reshape(rows, group, model)
    else:
        mixed = jnp.concatenate(attended, 1).reshape(blocks, group, width)
        mixed = to_blocks(mixed, rows).reshape(count, width)
        grads = jnp.concatenate([g[0] for g in grad_packed], 1)
        back = sum_parts(nt(grads, full_qkv).reshape(blocks, group, model), 1).astype(BF)
        grad_hidden = mlp_back + to_blocks(back, rows).astype(F32)
        branches = mlp_out.astype(F32) + nt(mixed, full_out)
        branches = sum_parts(branches.reshape(rows, group, model), 1)
        result = join_parts((own_tokens.astype(F32) + branches + b_out).astype(BF), 1)
        normal, scale = normalize(own_tokens.astype(F32))
        grad_normal = grad_hidden * ln_gain
        grad_inputs = scale * (
            grad_normal
            - jnp.mean(grad_normal, -1, keepdims=True)
            - normal * jnp.mean(grad_normal * normal, -1, keepdims=True)
        )
        grad_tokens = join_parts((own_cot.astype(F32) + grad_inputs).astype(BF), 1)
        norm_sums = jnp.concatenate([jnp.sum(grad_hidden * normal, (0, 1)), jnp.sum(grad_hidden, (0, 1))])
        sums = jnp.concatenate([norm_sums.reshape(-1, LANES), tensor_sums, bias_sums], 0)
        sums = sum_all(sums, ("dp", "blk"))
        norm_sums = sum_all(sums[:3 * lines], ("tensor",)).reshape(3, model)
        bias_sums = sums[3 * lines:].reshape(-1)
        grad_out = lax.all_to_all(dot(cot.T, mixed).astype(BF), ("dp", "blk"), 0, 0, tiled=True)
        grad_out_sum = jnp.sum(grad_out.reshape(-1, shard.shape[0], width).astype(F32), 0)

    return (
        result,
        grad_tokens,
        norm_sums[0],
        norm_sums[1],
        by_kind(grad_qkv_sum, width),
        by_kind(bias_sums[None, inner:], width)[0],
        grad_out_sum.T,
        grad_fc_sum,
        bias_sums[:inner],
        grad_proj_sum.T,
        norm_sums[2],
    )


def solution(mesh):
    in_specs = (
        P("dp", "blk", None),
        P(),
        P(),
        P(("dp", "blk"), None, "tensor"),
        P(None, "tensor"),
        P("tensor", ("dp", "blk")),
        P(("dp", "blk"), "tensor"),
        P("tensor"),
        P("tensor", ("dp", "blk")),
        P(),
        P("dp", None),
        P("dp", "blk", None),
    )
    out_specs = (
        P("dp", "blk", None),
        P("dp", "blk", None),
        P(),
        P(),
        P(("dp", "blk"), None, "tensor"),
        P(None, "tensor"),
        P("tensor", ("dp", "blk")),
        P(("dp", "blk"), "tensor"),
        P("tensor"),
        P("tensor", ("dp", "blk")),
        P(),
    )
    return jax.shard_map(local, mesh=mesh, in_specs=in_specs, out_specs=out_specs, check_vma=False)
```

```python
import functools

import jax
import jax.numpy as jnp
from jax import lax
from jax.experimental import pallas as pl
from jax.experimental.pallas import tpu as pltpu
from jax.sharding import PartitionSpec as P

HEAD_DIM = 64
ROT_DIM = 16
LANES = 128
EPSILON = 1e-05
BF = jnp.bfloat16
F32 = jnp.float32
MIB = 1024 * 1024


def nt(a, b):
    return lax.dot_general(a, b, (((1,), (1,)), ((), ())), preferred_element_type=F32)


def nn(a, b):
    return lax.dot_general(a, b, (((1,), (0,)), ((), ())), preferred_element_type=F32)


def attn_kernel(bq, bk, part, waits, lo_ref, hi_ref, *refs):
    count = 2 if part else 1
    hidden, refs = refs[:count], refs[count + waits:]
    w_ref, bias_ref, do_ref, cos_ref, sin_ref, start_ref, o_ref = refs[:7]
    grads, refs = refs[7:7 + count], refs[7 + count:]
    (q2, qt, ks, vx, s_buf, p_buf, d_buf, dkt, dvt, keep, ahead, behind, starts) = refs
    length = do_ref.shape[0]
    nq = length // bq
    lane = lax.broadcasted_iota(jnp.int32, (1, LANES), 1)
    first = lane < HEAD_DIM
    half = ROT_DIM // 2
    to_score = HEAD_DIM ** (-0.5) * 1.4426950408889634
    mine_first = lax.axis_index("tensor") == 0 if part else None

    def load(base, size):
        if part:
            rows = []
            for n in range(size // (2 * part)):
                at = pl.ds(pl.multiple_of(base // 2 + n * part, part), part)
                a, b = hidden[0][at, :], hidden[1][at, :]
                rows += [jnp.where(mine_first, a, b), jnp.where(mine_first, b, a)]
            rows = jnp.concatenate(rows, 0)
        else:
            rows = hidden[0][pl.ds(base, size), :]
        packed = nn(rows, w_ref[...]) + bias_ref[...]
        return [packed[:, n * LANES:(n + 1) * LANES] for n in range(3)]

    def store(base, which, value):
        cols = slice(which * LANES, (which + 1) * LANES)
        size = value.shape[0]
        if not part:
            grads[0][pl.ds(base, size), cols] = value.astype(BF)
            return
        for n in range(size // (2 * part)):
            at = pl.ds(pl.multiple_of(base // 2 + n * part, part), part)
            a = value[2 * n * part:(2 * n + 1) * part]
            b = value[(2 * n + 1) * part:(2 * n + 2) * part]
            grads[0][at, cols] = jnp.where(mine_first, a, b).astype(BF)
            grads[1][at, cols] = jnp.where(mine_first, b, a).astype(BF)

    def rot(u, rows):
        return (u * keep[rows, :] + pltpu.roll(u, LANES - half, 1) * ahead[rows, :]
                + pltpu.roll(u, half, 1) * behind[rows, :])

    def rot_back(u, rows):
        return (u * keep[rows, :] + pltpu.roll(u * behind[rows, :], LANES - half, 1)
                + pltpu.roll(u * ahead[rows, :], half, 1))

    def tables(i, _):
        rows = pl.ds(pl.multiple_of(i * bq, bq), bq)
        c, s = cos_ref[:, rows], sin_ref[:, rows]
        rest = HEAD_DIM - ROT_DIM
        one, zero, gap = jnp.ones((rest, bq), F32), jnp.zeros((rest, bq), F32), jnp.zeros((half, bq), F32)
        keep[rows, :] = jnp.concatenate([c, c, one] * 2, 0).T
        ahead[rows, :] = jnp.concatenate([-s, gap, zero] * 2, 0).T
        behind[rows, :] = jnp.concatenate([gap, s, zero] * 2, 0).T
        starts[rows, :] = jnp.broadcast_to(start_ref[:, rows], (LANES, bq)).T
        return 0

    @pl.when(pl.program_id(0) == 0)
    def _():
        lax.fori_loop(0, nq, tables, 0)

    def prep(i, _):
        base = pl.multiple_of(i * bq, bq)
        rows = pl.ds(base, bq)
        q, k, v = load(base, bq)
        q = rot(q, rows)
        qs = (q * to_score).astype(BF)
        zero = jnp.zeros_like(qs)
        q2[0, rows, :] = jnp.where(first, qs, zero)
        q2[1, rows, :] = jnp.where(first, zero, qs)
        qt[:, rows] = q.T.astype(BF)
        ks[rows, :] = rot(k, rows).astype(BF)
        vx[rows, :LANES] = v.astype(BF)
        vx[rows, LANES:] = jnp.ones((bq, LANES), BF)
        dkt[:, rows] = jnp.zeros((LANES, bq), F32)
        dvt[:, rows] = jnp.zeros((LANES, bq), F32)
        return 0

    lax.fori_loop(0, nq, prep, 0)

    def q_block(i, _):
        rows = pl.ds(pl.multiple_of(i * bq, bq), bq)
        last = (i * bq) // bk
        least = lo_ref[i] // bk
        masked = jnp.clip((hi_ref[i] + bk - 1) // bk, least, last)
        q_h = (q2[0, rows, :], q2[1, rows, :])
        start = starts[rows, :]

        def scores(j, mx, mode):
            cols = pl.ds(pl.multiple_of(j * bk, bk), bk)
            k = ks[cols, :]
            out = []
            for h in range(2):
                s = nt(q_h[h], k)
                m = mx[h]
                for t in range(bk // LANES):
                    piece = s[:, t * LANES:(t + 1) * LANES]
                    if mode:
                        kidx = (j * bk + t * LANES + lane).astype(F32)
                        ok = kidx >= start
                        if mode == 2:
                            qidx = (i * bq + lax.broadcasted_iota(jnp.int32, (bq, 1), 0)).astype(F32)
                            ok = ok & (kidx <= qidx)
                        piece = jnp.where(ok, piece, -1e30)
                    s_buf[h, :, pl.ds(pl.multiple_of(j * bk + t * LANES, LANES), LANES)] = piece
                    m = jnp.maximum(m, piece)
                out.append(m)
            return tuple(out)

        mx = (jnp.full((bq, LANES), -1e30, F32),) * 2
        mx = lax.fori_loop(least, masked, lambda j, m: scores(j, m, 1), mx)
        mx = lax.fori_loop(masked, last, lambda j, m: scores(j, m, 0), mx)
        mx = scores(last, mx, 2)
        mx = [jnp.max(m, -1, keepdims=True) for m in mx]

        def weigh(j, acc):
            cols = pl.ds(pl.multiple_of(j * bk, bk), bk)
            v = vx[cols, :]
            out = []
            for h in range(2):
                p = jnp.exp2(s_buf[h, :, cols] - mx[h]).astype(BF)
                p_buf[h, :, cols] = p
                out.append(acc[h] + nn(p, v))
            return tuple(out)

        acc = (jnp.zeros((bq, 2 * LANES), F32),) * 2
        acc = lax.fori_loop(least, last + 1, weigh, acc)
        inv = [1.0 / a[:, LANES:] for a in acc]
        outs = [a[:, :LANES] * r for a, r in zip(acc, inv)]
        o = jnp.where(first, outs[0], outs[1])
        o_ref[rows, :] = o.astype(BF)
        do = do_ref[rows, :].astype(F32)
        dos, dots, deltas = [], [], []
        for h in range(2):
            mine = first if h == 0 else jnp.logical_not(first)
            d = jnp.where(mine, do * inv[h], 0.0).astype(BF)
            dos.append(d)
            df = d.astype(F32)
            deltas.append(jnp.sum(df * o, -1, keepdims=True))
            dots.append(df.T[h * HEAD_DIM:(h + 1) * HEAD_DIM].astype(BF))
        q_t = qt[:, rows]

        def back(j, acc):
            cols = pl.ds(pl.multiple_of(j * bk, bk), bk)
            v = vx[cols, :LANES]
            k = ks[cols, :]
            out = []
            for h in range(2):
                rows_h = slice(h * HEAD_DIM, (h + 1) * HEAD_DIM)
                p = p_buf[h, :, cols]
                dp = nt(dos[h], v)
                ds = (p.astype(F32) * (dp - deltas[h])).astype(BF)
                dvt[rows_h, cols] += nn(dots[h], p)
                dkt[rows_h, cols] += nn(q_t[rows_h], ds)
                out.append(acc[h] + nn(ds, k))
            return tuple(out)

        acc = (jnp.zeros((bq, LANES), F32),) * 2
        acc = lax.fori_loop(least, last + 1, back, acc)
        dq = jnp.where(first, acc[0], acc[1]) * HEAD_DIM ** (-0.5)
        store(i * bq, 0, rot_back(dq, rows))
        return 0

    def static_block(i):
        rows = slice(i * bq, (i + 1) * bq)
        width = (i + 1) * bq
        start = starts[rows, :]
        q_h = (q2[0, rows, :], q2[1, rows, :])
        mx = []
        for h in range(2):
            m = jnp.full((bq, LANES), -1e30, F32)
            for j in range(0, width, bk):
                s = nt(q_h[h], ks[j:j + bk, :])
                for t in range(0, bk, LANES):
                    kidx = (j + t + lane).astype(F32)
                    ok = kidx >= start
                    if j + t + LANES > i * bq:
                        qidx = (i * bq + lax.broadcasted_iota(jnp.int32, (bq, 1), 0)).astype(F32)
                        ok = ok & (kidx <= qidx)
                    piece = jnp.where(ok, s[:, t:t + LANES], -1e30)
                    s_buf[h, :, j + t:j + t + LANES] = piece
                    m = jnp.maximum(m, piece)
            mx.append(jnp.broadcast_to(jnp.max(m, -1, keepdims=True), (bq, LANES)))
        acc = []
        for h in range(2):
            for t in range(0, width, LANES):
                p_buf[h, :, t:t + LANES] = jnp.exp2(s_buf[h, :, t:t + LANES] - mx[h]).astype(BF)
            acc.append(nn(p_buf[h, :, :width], vx[:width, :]))
        inv = [1.0 / v[:, LANES:] for v in acc]
        outs = [v[:, :LANES] * r for v, r in zip(acc, inv)]
        o = jnp.where(first, outs[0], outs[1])
        o_ref[rows, :] = o.astype(BF)
        do = do_ref[rows, :].astype(F32)
        dq = []
        for h in range(2):
            mine = first if h == 0 else jnp.logical_not(first)
            rows_h = slice(h * HEAD_DIM, (h + 1) * HEAD_DIM)
            d = jnp.where(mine, do * inv[h], 0.0).astype(BF)
            df = d.astype(F32)
            delta = jnp.broadcast_to(jnp.sum(df * o, -1, keepdims=True), (bq, LANES))
            d_t = df.T[rows_h].astype(BF)
            q_t = qt[rows_h, rows]
            for j in range(0, width, bk):
                cols = slice(j, j + bk)
                dp = nt(d, vx[cols, :LANES])
                dvt[rows_h, cols] += nn(d_t, p_buf[h, :, cols])
                for t in range(0, bk, LANES):
                    at = slice(j + t, j + t + LANES)
                    d_buf[h, :, at] = (p_buf[h, :, at].astype(F32) * (dp[:, t:t + LANES] - delta)).astype(BF)
                dkt[rows_h, cols] += nn(q_t, d_buf[h, :, cols])
            dq.append(nn(d_buf[h, :, :width], ks[:width, :]))
        dq = jnp.where(first, dq[0], dq[1]) * HEAD_DIM ** (-0.5)
        store(i * bq, 0, rot_back(dq, rows))

    if nq <= 4:
        for i in range(nq):
            static_block(i)
    else:
        lax.fori_loop(0, nq, q_block, 0)

    def finish(i, _):
        base = pl.multiple_of(i * bq, bq)
        rows = pl.ds(base, bq)
        store(base, 1, rot_back(dkt[:, rows].T * HEAD_DIM ** (-0.5), rows))
        store(base, 2, dvt[:, rows].T)
        return 0

    lax.fori_loop(0, nq, finish, 0)


def attention(hidden, weights, bias, first_pair, do, position, start, part=0, waits=(), bq=512, bk=512):
    length, width = do.shape
    bq = min(bq, 2 ** 20 // length)
    bk = max(bq, min(bk, length))
    pairs = width // LANES
    freqs = 10000.0 ** (-jnp.arange(0, ROT_DIM, 2, dtype=F32) / ROT_DIM)
    phase = position.astype(F32)[None] * freqs[:, None]
    by_block = start.reshape(length // bq, bq)
    rows, model = hidden[0].shape
    once = pl.Buffered(1)
    columns = pl.BlockSpec((length, LANES), lambda g, *_: (0, g))
    triple = pl.BlockSpec((rows, 3 * LANES), lambda g, *_: (0, g))
    whole = lambda n: pl.BlockSpec((n, length), lambda g, *_: (0, 0), pipeline_mode=once)
    tri_out = jax.ShapeDtypeStruct((rows, 3 * width), BF)
    static = length // bq <= 4
    out = pl.pallas_call(
        functools.partial(attn_kernel, bq, bk, part, len(waits)),
        out_shape=[jax.ShapeDtypeStruct((length, width), BF)] + [tri_out] * len(hidden),
        grid_spec=pltpu.PrefetchScalarGridSpec(
            num_scalar_prefetch=2,
            grid=(pairs,),
            in_specs=[pl.BlockSpec((rows, model), lambda g, *_: (0, 0), pipeline_mode=once)] * len(hidden)
            + [pl.BlockSpec(memory_space=pl.ANY)] * len(waits)
            + [
                pl.BlockSpec((model, 3 * LANES), lambda g, *_: (0, first_pair + g)),
                pl.BlockSpec((1, 3 * LANES), lambda g, *_: (0, first_pair + g)),
                columns, whole(ROT_DIM // 2), whole(ROT_DIM // 2), whole(1),
            ],
            out_specs=[columns] + [triple] * len(hidden),
            scratch_shapes=[
                pltpu.VMEM((2, length, LANES), BF),
                pltpu.VMEM((LANES, length), BF),
                pltpu.VMEM((length, LANES), BF),
                pltpu.VMEM((length, 2 * LANES), BF),
                pltpu.VMEM((2, bq, length), F32),
                pltpu.VMEM((2, bq, length), BF),
                pltpu.VMEM((2, bq, length) if static else (8, LANES), BF),
                pltpu.VMEM((LANES, length), F32),
                pltpu.VMEM((LANES, length), F32),
            ] + [pltpu.VMEM((length, LANES), F32)] * 4,
        ),
        compiler_params=pltpu.CompilerParams(vmem_limit_bytes=56 * MIB),
        cost_estimate=pl.CostEstimate(flops=1000, bytes_accessed=1000, transcendentals=0),
    )(by_block.min(1), by_block.max(1), *hidden, *waits, weights, bias, do, jnp.cos(phase), jnp.sin(phase),
      start.astype(F32)[None])
    return out[0], list(out[1:])


MESH = pl.DeviceIdType.MESH


def remote(src, dst, send, recv, target):
    return pltpu.make_async_remote_copy(
        src_ref=src, dst_ref=dst, send_sem=send, recv_sem=recv, device_id=target, device_id_type=MESH
    )


def meet(others):
    barrier = pltpu.get_barrier_semaphore()
    for target in others:
        pl.semaphore_signal(barrier, inc=1, device_id=target, device_id_type=MESH)
    pl.semaphore_wait(barrier, len(others))


def gather_kernel(x_ref, tok_ref, gain_ref, bias_ref, out_ref, hid_ref, local_sem, recv, up, down, across, over):
    size = x_ref.shape[0]
    core, block = lax.axis_index("dp"), lax.axis_index("blk")
    z, y = block // 2, lax.rem(block, 2)
    depth = lax.axis_size("blk") // 2
    above, below = {"blk": block + 2}, {"blk": block - 2}
    beside, sibling = {"blk": block + 1 - 2 * y}, {"dp": 1 - core}

    def place(c, zz, yy):
        return (c * depth + zz) * 2 + yy

    def chunk(at):
        return out_ref.at[pl.ds(pl.multiple_of(at * size, size), size)]

    def copy(src, at, sem, target):
        return pltpu.make_async_remote_copy(
            src_ref=src, dst_ref=chunk(at), send_sem=sem, recv_sem=recv.at[at],
            device_id=target, device_id_type=pl.DeviceIdType.MESH,
        )

    def arrived(at):
        copy(chunk(at), at, local_sem, sibling).wait_recv()

    barrier = pltpu.get_barrier_semaphore()

    def greet(target):
        pl.semaphore_signal(barrier, inc=1, device_id=target, device_id_type=pl.DeviceIdType.MESH)

    def not_top(action):
        pl.when(z < depth - 1)(action)

    def not_bottom(action):
        pl.when(z > 0)(action)

    not_top(lambda: greet(above))
    not_bottom(lambda: greet(below))
    greet(beside)
    greet(sibling)
    pl.semaphore_wait(barrier, 2 + jnp.where(z > 0, 1, 0) + jnp.where(z < depth - 1, 1, 0))

    mine = place(core, z, y)
    keep = pltpu.make_async_copy(x_ref, chunk(mine), local_sem)
    not_top(lambda: copy(x_ref, mine, up.at[z], above).start())
    not_bottom(lambda: copy(x_ref, mine, down.at[z], below).start())
    copy(x_ref, mine, across.at[z], beside).start()
    copy(x_ref, mine, over.at[z * 2 + y], sibling).start()
    keep.start()

    for r in range(tok_ref.shape[0]):
        x = tok_ref[r].astype(F32)
        x = x - jnp.mean(x, -1, keepdims=True)
        x = x * lax.rsqrt(jnp.mean(x * x, -1, keepdims=True) + EPSILON)
        hid_ref[r] = (x * gain_ref[...] + bias_ref[...]).astype(BF)

    def from_beside(zz):
        at = place(core, zz, 1 - y)
        arrived(at)
        copy(chunk(at), at, over.at[zz * 2 + 1 - y], sibling).start()

    def from_line(zz, onward, sems, target):
        at = place(core, zz, y)
        arrived(at)
        onward(lambda: copy(chunk(at), at, sems.at[zz], target).start())
        copy(chunk(at), at, across.at[zz], beside).start()
        copy(chunk(at), at, over.at[zz * 2 + y], sibling).start()

    for step in range(1, depth):
        pl.when(z >= step)(lambda: from_line(z - step, not_top, up, above))
        pl.when(z + step < depth)(lambda: from_line(z + step, not_bottom, down, below))
    from_beside(z)
    for step in range(1, depth):
        pl.when(z >= step)(lambda: from_beside(z - step))
        pl.when(z + step < depth)(lambda: from_beside(z + step))

    keep.wait()
    for zz in range(depth):
        for yy in range(2):
            arrived(place(1 - core, zz, yy))
            copy(x_ref, mine, over.at[zz * 2 + yy], sibling).wait_send()
        copy(x_ref, mine, across.at[zz], beside).wait_send()
        pl.when((zz <= z) & (z < depth - 1))(lambda: copy(x_ref, mine, up.at[zz], above).wait_send())
        pl.when((zz >= z) & (z > 0))(lambda: copy(x_ref, mine, down.at[zz], below).wait_send())


def gather_weights(shard, tokens, gain, bias):
    cores, blocks = lax.axis_size("dp"), lax.axis_size("blk")
    rows, columns = shard.shape
    dma = pltpu.SemaphoreType.DMA
    hbm, vmem = pl.BlockSpec(memory_space=pl.ANY), pl.BlockSpec(memory_space=pltpu.VMEM)
    return pl.pallas_call(
        gather_kernel,
        out_shape=[
            jax.ShapeDtypeStruct((cores * blocks * rows, columns), shard.dtype),
            jax.ShapeDtypeStruct(tokens.shape, BF),
        ],
        in_specs=[hbm, vmem, vmem, vmem],
        out_specs=[hbm, vmem],
        scratch_shapes=[
            dma, dma((cores * blocks,)), dma((blocks // 2,)), dma((blocks // 2,)),
            dma((blocks // 2,)), dma((blocks,)),
        ],
        compiler_params=pltpu.CompilerParams(
            collective_id=0, has_side_effects=True, vmem_limit_bytes=32 * MIB
        ),
    )(shard, tokens, gain, bias)


class RowTransfer:
    def __init__(self, hid_ref, mine_ref, other_ref, blank, blank_sem, hid_send, hid_recv, side_send, side_recv):
        self.refs = hid_ref, mine_ref, other_ref, blank
        self.sems = blank_sem, hid_send, hid_recv, side_send, side_recv
        self.rows, group, _ = hid_ref.shape
        self.part = group // 2
        self.block, self.half = lax.axis_index("blk"), lax.axis_index("tensor")
        self.blocks = lax.axis_size("blk")
        self.has_row = self.block < self.rows
        self.facing = {"tensor": 1 - self.half}

    def piece(self, ref, at):
        return ref.at[pl.ds(pl.multiple_of(at * self.part, self.part), self.part)]

    def source(self, r):
        return self.refs[0].at[r, pl.ds(pl.multiple_of(self.half * self.part, self.part), self.part)]

    def row_copy(self, r):
        _, hid_send, hid_recv, _, _ = self.sems
        mine = self.piece(self.refs[1], self.block)
        return remote(self.source(r), mine, hid_send.at[r], hid_recv.at[self.block], {"blk": r})

    def own_row(self):
        return pltpu.make_async_copy(
            self.source(self.block), self.piece(self.refs[1], self.block), self.sems[1].at[self.block]
        )

    def side_copy(self, s):
        _, _, _, side_send, side_recv = self.sems
        _, mine, other, _ = self.refs
        return remote(self.piece(mine, s), self.piece(other, s), side_send.at[s], side_recv.at[s], self.facing)

    def blanks(self):
        _, mine, other, blank = self.refs
        return [
            pltpu.make_async_copy(blank, self.piece(ref, s), self.sems[0].at[n * self.blocks + s])
            for n, ref in enumerate((mine, other)) for s in range(self.blocks)
        ]

    def to_block(self, n, action):
        r = lax.rem(self.block + n, self.blocks)
        pl.when(r < self.rows)(lambda: action(self.row_copy(r)))

    def start(self):
        meet([{"blk": lax.rem(self.block + n, self.blocks)} for n in range(1, self.blocks)] + [self.facing])
        for n in range(1, self.blocks):
            self.to_block(n, lambda copy: copy.start())

        @pl.when(self.has_row)
        def _():
            self.own_row().start()
            self.own_row().wait()
            self.side_copy(self.block).start()

        @pl.when(jnp.logical_not(self.has_row))
        def _():
            self.refs[3][...] = jnp.zeros_like(self.refs[3])
            for copy in self.blanks():
                copy.start()

    def onward(self, n):
        @pl.when(self.has_row)
        def _():
            s = lax.rem(self.block + self.blocks - n, self.blocks)
            mine = self.piece(self.refs[1], s)
            remote(mine, mine, self.sems[3].at[s], self.sems[2].at[s], self.facing).wait_recv()
            self.side_copy(s).start()

    def finish(self):
        for n in range(1, self.blocks):
            self.to_block(n, lambda copy: copy.wait_send())

        @pl.when(self.has_row)
        def _():
            for s in range(self.blocks):
                self.side_copy(s).wait()

        @pl.when(jnp.logical_not(self.has_row))
        def _():
            for copy in self.blanks():
                copy.wait()


def tail_kernel(groups, waits, *refs):
    g_mine, g_other, heads = refs[:groups], refs[groups:2 * groups], refs[2 * groups:3 * groups]
    (w_ref, tok_ref, cot_ref, add_ref, gain_ref, extra_ref, out_ref, sum_ref, wgrad_ref, mixed_ref, facing_ref,
     sent, got, home_send, home, grads, mix, total, terms, paired, merged, inbox, norms, small, small_in, small_box, small_out,
     a_send, a_recv, b_send, b_recv, c_send, c_recv, c_local, d_send, d_recv, e_send, e_recv, e_local,
     f_send, f_recv, g_send, g_recv, h_send, h_recv, i_send, i_recv) = refs[3 * groups + waits:]
    rows, part, model = tok_ref.shape
    block, half = lax.axis_index("blk"), lax.axis_index("tensor")
    blocks = lax.axis_size("blk")
    facing = {"tensor": 1 - half}
    has_row = block < rows
    count = lax.axis_size("dp") * blocks
    me = lax.axis_index("dp") * blocks + block

    def peers():
        return [lax.rem(me + n, count) for n in range(1, count)]

    def device(j):
        return {"dp": j // blocks, "blk": lax.rem(j, blocks)}

    meet([device(j) for j in peers()] + [facing])

    def product(parts, s):
        at, total, first = pl.ds(pl.multiple_of(s * part, part), part), None, 0
        for g in parts:
            width = g.shape[1]
            term = nt(g[at, :], w_ref[:, first:first + width])
            total, first = term if total is None else total + term, first + width
        return total

    def across(s):
        return remote(sent.at[s], got.at[s], a_send.at[s], a_recv.at[s], facing)

    def homeward(s):
        return remote(home_send.at[s], home.at[block], b_send.at[s], b_recv.at[block], {"blk": s})

    def own_half(ref, r):
        return ref.at[r, pl.ds(pl.multiple_of(half * part, part), part)]

    def share(r):
        return remote(grads.at[r], own_half(out_ref, r), c_send.at[r], c_recv.at[r], facing)

    def keep(r):
        return pltpu.make_async_copy(grads.at[r], own_half(out_ref, r), c_local.at[r])

    def heads_of(ref, k, r):
        wide = heads[-1].shape[1]
        return ref.at[r, :, k * wide:(k + 1) * wide]

    def attended(k, s):
        return heads[k].at[pl.ds(pl.multiple_of(s * 2 * part, 2 * part), 2 * part)]

    def heads_home(k, s):
        return remote(attended(k, s), heads_of(mix, k, block), d_send.at[k * blocks + s],
                      d_recv.at[k * blocks + block], {"blk": s})

    def own_heads(k):
        return pltpu.make_async_copy(attended(k, block), heads_of(mix, k, block), d_send.at[k * blocks + block])

    def send_heads(k, n):
        if n == 0:
            own_heads(k).start()
        else:
            heads_home(k, lax.rem(block + n, blocks)).start()

    def landed(r):
        return pltpu.make_async_copy(heads[0].at[r], heads_of(mix, 0, r), d_send.at[r])

    def heads_across(k, r):
        return remote(heads_of(mix, k, r), heads_of(facing_ref, k, r), e_send.at[k * blocks + r],
                      e_recv.at[k * blocks + r], facing)

    @pl.when(has_row)
    def _():
        for n in range(blocks):
            s = lax.rem(block + n, blocks)
            sent[s] = product(g_other, s).astype(BF)
            across(s).start()

    for r in range(rows):
        landed(r).start()

    def keep_heads(r):
        return pltpu.make_async_copy(mix.at[r], mixed_ref.at[r], e_local.at[r])

    norms[...] = jnp.zeros_like(norms)
    total[...] = jnp.zeros_like(total)

    def forward(n):
        s = lax.rem(block + n, blocks)

        @pl.when(has_row)
        def _():
            grad = product(g_mine, s)
            across(s).wait_recv()
            grad = (grad + got[s].astype(F32)).astype(BF)
            if n == 0:
                home[s] = grad
            else:
                home_send[s] = grad
                homeward(s).start()

    def heads_arrive(k, n, r):
        if n:
            here = heads_of(mix, k, r)
            remote(here, here, e_send.at[k * blocks + r], d_recv.at[k * blocks + r], facing).wait_recv()
        else:
            own_heads(k).wait()
        heads_across(k, r).start()

    def norm(n):
        r = lax.rem(block + blocks - n, blocks)

        @pl.when(r < rows)
        def _():
            landed(r).wait()
            heads_across(0, r).start()
            if n:
                remote(home_send.at[r], home.at[r], b_send.at[r], b_recv.at[r], facing).wait_recv()
            grad = home[r].astype(F32) + add_ref[r].astype(F32)
            x = tok_ref[r].astype(F32)
            x = x - jnp.mean(x, -1, keepdims=True)
            scale = lax.rsqrt(jnp.mean(x * x, -1, keepdims=True) + EPSILON)
            x = x * scale
            norms[0:1, :] += jnp.sum(grad * x, 0, keepdims=True)
            norms[1:2, :] += jnp.sum(grad, 0, keepdims=True)
            grad = grad * gain_ref[...]
            grad = grad - jnp.mean(grad, -1, keepdims=True) - x * jnp.mean(grad * x, -1, keepdims=True)
            own = cot_ref[r, pl.ds(pl.multiple_of(half * part, part), part), :]
            grads[r] = (own.astype(F32) + scale * grad).astype(BF)
            keep(r).start()

    lag = 2
    for n in range(blocks + lag):
        if n < blocks:
            forward(n)
        if n >= lag:
            norm(n - lag)
        if n == blocks - 1:
            @pl.when(has_row)
            def _():
                for k in range(1, groups):
                    for other in range(blocks):
                        send_heads(k, other)

    small[...] = extra_ref[...]
    lines = norms.shape[1] // LANES
    for n in range(2):
        for k in range(lines):
            small[n * lines + k:n * lines + k + 1, :] = norms[n:n + 1, k * LANES:(k + 1) * LANES]
    shared = small.at[pl.ds(0, 3 * lines)]
    swapped = remote(shared, small_in, g_send, g_recv, facing)
    swapped.start()
    for r in range(rows):
        share(r).start()

    for n in range(blocks):
        r = lax.rem(block + blocks - n, blocks)

        @pl.when(r < rows)
        def _():
            for k in range(1, groups):
                heads_arrive(k, n, r)
            keep_heads(r).start()
            total[...] += nn(cot_ref[r].T, mix[r])

    size = terms.shape[1]
    core = lax.axis_index("dp")
    for j in range(count):
        terms[j] = total[j * size:(j + 1) * size].astype(BF)

    def to_sibling():
        theirs = terms.at[pl.ds((1 - core) * blocks, blocks)]
        return remote(theirs, paired, f_send.at[blocks], f_recv.at[blocks], {"dp": 1 - core})

    to_sibling().start()

    swapped.wait()
    small[:3 * lines, :] += small_in[...]
    to_sibling().wait()

    def term(s):
        return remote(merged.at[s], inbox.at[block], f_send.at[s], f_recv.at[block], {"blk": s})

    for s in range(blocks):
        merged[s] = (terms[core * blocks + s].astype(F32) + paired[s].astype(F32)).astype(BF)
    for n in range(1, blocks):
        term(lax.rem(block + n, blocks)).start()

    def line(ref, j):
        return ref.at[pl.ds(pl.multiple_of(j * 8, 8), 8)]

    def small_term(j):
        return remote(line(small, j), small_box.at[me], h_send.at[j], h_recv.at[me], device(j))

    def small_sum(j):
        return remote(line(small_out, me), line(small_out, me), i_send.at[j], i_recv.at[me], device(j))

    for j in peers():
        small_term(j).start()
    small_box[me] = small[pl.ds(pl.multiple_of(me * 8, 8), 8), :]
    for j in peers():
        remote(small_box.at[j], small_box.at[j], h_send.at[j], h_recv.at[j], device(j)).wait_recv()
    added = small_box[0]
    for j in range(1, count):
        added = added + small_box[j]
    small_out[pl.ds(pl.multiple_of(me * 8, 8), 8), :] = added
    for j in peers():
        small_sum(j).start()
    inbox[block] = merged[block]
    for n in range(1, blocks):
        s = lax.rem(block + n, blocks)
        remote(inbox.at[s], inbox.at[s], f_send.at[s], f_recv.at[s], facing).wait_recv()
    added = inbox[0].astype(F32)
    for s in range(1, blocks):
        added = added + inbox[s].astype(F32)
    wgrad_ref[...] = added
    for j in peers():
        remote(line(small_out, j), line(small_out, j), i_send.at[j], i_recv.at[j], device(j)).wait_recv()
    sum_ref[...] = small_out[...]
    for j in peers():
        small_term(j).wait_send()
        small_sum(j).wait_send()
    for n in range(1, blocks):
        term(lax.rem(block + n, blocks)).wait_send()

    for r in range(rows):
        share(r).wait()
        keep(r).wait()
        keep_heads(r).wait()
        for k in range(groups):
            heads_across(k, r).wait()

    @pl.when(has_row)
    def _():
        for s in range(blocks):
            across(s).wait_send()
        for n in range(1, blocks):
            homeward(lax.rem(block + n, blocks)).wait_send()
            for k in range(1, groups):
                heads_home(k, lax.rem(block + n, blocks)).wait_send()


def go_home(g_mine, g_other, attended, weights, tokens, cot, add, gain, extra, waits=()):
    rows, part, model = tokens.shape
    blocks = lax.axis_size("blk")
    wide = sum(g.shape[1] for g in g_mine)
    dma = pltpu.SemaphoreType.DMA
    groups, hbm = len(g_mine), pl.BlockSpec(memory_space=pl.ANY)
    count = lax.axis_size("dp") * blocks
    wide_heads = sum(o.shape[-1] for o in attended)
    lines = 3 * model // LANES
    heads = jax.ShapeDtypeStruct((rows, 2 * part, wide_heads), BF)
    vmem = pl.BlockSpec(memory_space=pltpu.VMEM)
    return pl.pallas_call(
        functools.partial(tail_kernel, groups, len(waits)),
        grid=(1,),
        out_shape=[jax.ShapeDtypeStruct((rows, 2 * part, model), BF), jax.ShapeDtypeStruct((8 * count, LANES), F32),
                   jax.ShapeDtypeStruct((model // count, wide_heads), F32), heads, heads],
        in_specs=[vmem] * (2 * groups) + [hbm] * (groups + len(waits))
        + [pl.BlockSpec((model, wide), lambda i: (0, 0))] + [vmem] * 5,
        out_specs=[hbm, vmem, vmem, hbm, hbm],
        scratch_shapes=[pltpu.VMEM((blocks, part, model), BF)] * 4 + [pltpu.VMEM((rows, part, model), BF)]
        + [pltpu.VMEM(heads.shape, BF), pltpu.VMEM((model, wide_heads), F32)]
        + [pltpu.VMEM((count, model // count, wide_heads), BF)]
        + [pltpu.VMEM((blocks, model // count, wide_heads), BF)] * 3
        + [pltpu.VMEM((8, model), F32), pltpu.VMEM((8 * count, LANES), F32), pltpu.VMEM((lines, LANES), F32)]
        + [pltpu.VMEM((count, 8, LANES), F32), pltpu.VMEM((8 * count, LANES), F32)]
        + [dma((blocks,))] * 4 + [dma((rows,))] * 3 + [dma((groups * blocks,))] * 4 + [dma((rows,))]
        + [dma((count,))] * 2 + [dma] * 2 + [dma((count,))] * 4,
        compiler_params=pltpu.CompilerParams(
            collective_id=1, has_side_effects=True, vmem_limit_bytes=56 * MIB
        ),
        cost_estimate=pl.CostEstimate(flops=1000, bytes_accessed=1000, transcendentals=0),
    )(*g_mine, *g_other, *attended, *waits, weights, tokens, cot, add, gain, extra)


def weight_grad_kernel(half, waits, a_ref, b_ref, *refs):
    x_ref, y_ref, ax_ref, by_ref, turned = refs[waits:]
    step = pl.program_id(0)

    @pl.when(step == 0)
    def _():
        turned[...] = a_ref[...].T

    @pl.when(step == half)
    def _():
        turned[...] = b_ref[...].T

    @pl.when(step < half)
    def _():
        ax_ref[...] = nn(turned[...], x_ref[...]).astype(BF)

    @pl.when(step >= half)
    def _():
        by_ref[...] = nn(turned[...], y_ref[...]).astype(BF)


def weight_grads(a, x, b, y, waits=(), tile=512):
    count, model = a.shape
    inner = x.shape[1]
    tile = min(tile, inner)
    half = inner // tile
    whole = pl.BlockSpec((count, model), lambda i: (0, 0), pipeline_mode=pl.Buffered(1))
    return pl.pallas_call(
        functools.partial(weight_grad_kernel, half, len(waits)),
        grid=(2 * half,),
        out_shape=[jax.ShapeDtypeStruct((model, inner), BF)] * 2,
        in_specs=[
            whole, whole, *[pl.BlockSpec(memory_space=pl.ANY)] * len(waits),
            pl.BlockSpec((count, tile), lambda i: (0, jnp.minimum(i, half - 1))),
            pl.BlockSpec((count, tile), lambda i: (0, jnp.maximum(i - half, 0))),
        ],
        out_specs=[
            pl.BlockSpec((model, tile), lambda i: (0, jnp.minimum(i, half - 1))),
            pl.BlockSpec((model, tile), lambda i: (0, jnp.maximum(i - half, 0))),
        ],
        scratch_shapes=[pltpu.VMEM((model, count), BF)],
        compiler_params=pltpu.CompilerParams(vmem_limit_bytes=48 * MIB),
        cost_estimate=pl.CostEstimate(flops=1000, bytes_accessed=1000, transcendentals=0),
    )(a, b, *waits, x, y)


def mlp_kernel(tile, waits, moves, hid_ref, cot_ref, wf_ref, wp_ref, bias_ref, *refs):
    refs = refs[waits:]
    act_ref, gin_ref, res_ref, back_ref, gb_ref = refs[moves:moves + 5]
    if moves:
        step, steps = pl.program_id(0), pl.num_programs(0)
        rows = RowTransfer(refs[0], *refs[moves + 5:])
        pl.when(step == 0)(rows.start)
        for n in range(1, rows.blocks):
            pl.when(step == jnp.minimum(n, steps - 1))(lambda: rows.onward(n))
    hid, cot = hid_ref[...], cot_ref[...]

    @pl.when(pl.program_id(0) == 0)
    def _():
        gb_ref[...] = jnp.zeros_like(gb_ref)

    res = back = None
    for n in range(wf_ref.shape[1] // tile):
        cols = slice(n * tile, (n + 1) * tile)
        wf, wp = wf_ref[:, cols], wp_ref[:, cols]
        inner = nn(hid, wf) + bias_ref[:, cols]
        grad_act = nn(cot, wp)
        size = jnp.abs(inner)
        t = 1.0 / (1.0 + (0.3275911 * 0.7071067811865476) * size)
        bell = jnp.exp2((-0.5 * 1.4426950408889634) * inner * inner)
        tail = ((((0.5 * 1.061405429 * t - 0.5 * 1.453152027) * t + 0.5 * 1.421413741) * t
                 - 0.5 * 0.284496736) * t + 0.5 * 0.254829592) * t * bell
        below = jnp.where(inner < 0, tail, 1.0 - tail)
        act = (inner * below).astype(BF)
        grad_inner = (grad_act * (below + inner * (bell * 0.3989422804014327))).astype(BF)
        act_ref[:, cols] = act
        gin_ref[:, cols] = grad_inner
        gb_ref[:, cols] += jnp.sum(grad_inner.astype(F32), 0, keepdims=True)
        r, b = nt(act, wp), nt(grad_inner, wf)
        res, back = (r, b) if res is None else (res + r, back + b)
    res_ref[...] = res.astype(BF)
    back_ref[...] = back.astype(BF)
    if moves:
        pl.when(step == steps - 1)(rows.finish)


def mlp(hidden, cot, weights, first_block, bias, waits=(), moved=None, size=256, tile=512):
    count, model = hidden.shape
    inner = bias.shape[1]
    tile = min(tile, inner)
    rows = lambda n: pl.BlockSpec((size, n), lambda i: (i, 0))
    matrix = lambda n: pl.BlockSpec((model, inner), lambda i: (0, first_block + n), pipeline_mode=pl.Buffered(1))
    vector = pl.BlockSpec((1, inner), lambda i: (0, 0))
    hbm = pl.BlockSpec(memory_space=pl.ANY)
    shape = lambda n: jax.ShapeDtypeStruct((count, n), BF)
    moves, outs, scratch, params = (), [], [], {}
    if moved is not None:
        blocks, dma = lax.axis_size("blk"), pltpu.SemaphoreType.DMA
        part = moved.shape[1] // 2
        moves, outs = (moved,), [jax.ShapeDtypeStruct((blocks * part, model), BF)] * 2
        scratch = [pltpu.VMEM((part, model), BF), dma((2 * blocks,))] + [dma((blocks,))] * 4
        params = dict(collective_id=2, has_side_effects=True)
    return pl.pallas_call(
        functools.partial(mlp_kernel, tile, len(waits), len(moves)),
        grid=(count // size,),
        out_shape=[shape(inner), shape(inner), shape(model), shape(model), jax.ShapeDtypeStruct((1, inner), F32)] + outs,
        in_specs=[rows(model), rows(model), matrix(0), matrix(1), vector] + [hbm] * (len(waits) + len(moves)),
        out_specs=[rows(inner), rows(inner), rows(model), rows(model), vector] + [hbm] * len(outs),
        scratch_shapes=scratch,
        compiler_params=pltpu.CompilerParams(vmem_limit_bytes=56 * MIB, **params),
        cost_estimate=pl.CostEstimate(flops=1000, bytes_accessed=1000, transcendentals=0),
    )(hidden, cot, weights, weights, bias, *waits, *moves)


def normalize(values):
    center = values - jnp.mean(values, -1, keepdims=True)
    spread = jnp.mean(center * center, -1, keepdims=True)
    scale = lax.rsqrt(spread + EPSILON)
    return center * scale, scale


def swap(value):
    return lax.ppermute(value, "tensor", [(0, 1), (1, 0)])


def split_tensor(value, axis):
    shape = value.shape
    parts = lax.axis_size("tensor")
    return value.reshape(shape[:axis] + (parts, shape[axis] // parts) + shape[axis + 1:])


def part_of(value, axis, which):
    return lax.dynamic_index_in_dim(split_tensor(value, axis), which, axis, keepdims=False)


def sum_parts(value, axis):
    mine = lax.axis_index("tensor")
    if lax.axis_size("tensor") == 2:
        other = swap(part_of(value, axis, 1 - mine).astype(BF))
        return part_of(value, axis, mine).astype(F32) + other.astype(F32)
    return lax.psum_scatter(
        value.astype(BF), "tensor", scatter_dimension=axis, tiled=True
    ).astype(F32)


def join_parts(value, axis):
    if lax.axis_size("tensor") != 2:
        return lax.all_gather(value, "tensor", axis=axis, tiled=True)
    other = swap(value)
    first = lax.axis_index("tensor") == 0
    low, high = jnp.where(first, value, other), jnp.where(first, other, value)
    return jnp.concatenate([low, high], axis)


def to_rows(value):
    blocks = lax.axis_size("blk")
    pad = jnp.zeros((blocks - value.shape[0],) + value.shape[1:], value.dtype)
    return lax.all_to_all(jnp.concatenate([value, pad], 0), "blk", 0, 0, tiled=True)


def to_blocks(value, rows):
    return lax.all_to_all(value, "blk", 0, 0, tiled=True)[:rows]


def sum_all(value, axes):
    for axis in axes:
        size = lax.axis_size(axis)
        step = 1
        while step < size:
            value = value + lax.ppermute(value, axis, [(i, i ^ step) for i in range(size)])
            step *= 2
    return value


def by_pair(value, width):
    count = value.shape[0]
    return value.reshape(count, 3, width // LANES, LANES).transpose(0, 2, 1, 3).reshape(count, 3 * width)


def by_kind(value, width):
    count = value.shape[0]
    return value.reshape(count, width // LANES, 3, LANES).transpose(0, 2, 1, 3).reshape(count, 3, width)


def scatter(value):
    return lax.psum_scatter(value, ("dp", "blk"), scatter_dimension=0, tiled=True).astype(F32)


def dot(a, b):
    return jnp.dot(a, b, preferred_element_type=F32)


def local(
    tokens, ln_gain, ln_bias, w_qkv, b_qkv, w_out, w_fc, b_fc, w_proj, b_out, bounds, cotangent
):
    rows, group, model = tokens.shape
    width, inner = b_qkv.shape[1], b_fc.shape[0]
    blocks, parts = lax.axis_size("blk"), lax.axis_size("tensor")
    length = blocks * group
    count = rows * group
    part = group // parts

    mine = lax.axis_index("tensor")
    pair = parts == 2 and (lax.axis_size("dp"), blocks) == (2, 8)
    cot = cotangent.reshape(count, model)

    shard = jnp.concatenate([by_pair(w_qkv, width), w_out.T, w_fc, w_proj.T], 1)
    if pair:
        weights, hidden = gather_weights(shard, tokens, ln_gain[None], ln_bias[None])
    else:
        hidden = (normalize(tokens.astype(F32))[0] * ln_gain + ln_bias).astype(BF)
        weights = lax.all_gather(shard, ("dp", "blk"), axis=0, tiled=True)
        row_hidden = [join_parts(to_rows(part_of(hidden, 1, mine)), 1).reshape(length, model)]
    flat_hidden = hidden.reshape(count, model)
    full_qkv, full_out = weights[:, :3 * width], weights[:, 3 * width:4 * width]

    row_bounds = lax.dynamic_index_in_dim(
        bounds, jnp.minimum(lax.axis_index("blk"), rows - 1), 0, keepdims=False
    )
    index = jnp.arange(length, dtype=jnp.int32)
    start = jnp.max(jnp.where(row_bounds[:, None] <= index[None], row_bounds[:, None], 0), 0)

    groups = max(1, width // (2 * LANES))
    wide = width // groups
    cuts = [slice(n * wide, (n + 1) * wide) for n in range(groups)]
    grad_mixed = dot(cot, full_out).astype(BF).reshape(rows, group, width)
    row_grads = [to_rows(grad_mixed[:, :, cut]).reshape(length, wide) for cut in cuts]

    other_out = swap(full_out) if pair else None
    activated, grad_inner, mlp_out, mlp_back, grad_bfc, *moved = mlp(
        flat_hidden, cot, weights, 4 * width // inner, b_fc[None], (grad_mixed,), hidden if pair else None
    )
    row_hidden = moved or row_hidden
    mlp_back = sum_parts(mlp_back.reshape(rows, group, model), 1)
    grad_fc, grad_proj = weight_grads(
        flat_hidden, grad_inner, cot, activated, [row_grads[0]] + [other_out] * pair
    )
    grad_fc_sum, grad_proj_sum = scatter(grad_fc), scatter(grad_proj)
    if pair:
        mlp_back = mlp_back.astype(BF)
        other_mlp = swap(mlp_out)

    bias = by_pair(b_qkv[None], width)
    own_tokens, own_cot = part_of(tokens, 1, mine), part_of(cotangent, 1, mine)
    grad_packed, grad_qkv, attended = [], [], []
    waits = [grad_fc, own_tokens, own_cot]
    for n, row_grad in enumerate(row_grads):
        out, grads = attention(
            row_hidden, weights, bias, n * (wide // LANES), row_grad, index - start, start,
            part if pair else 0, waits,
        )
        attended.append(out)
        grad_packed.append(grads)
        grad_qkv.append(sum(dot(h.T, g) for h, g in zip(row_hidden, grads)).astype(BF))
        waits = [out, grad_fc_sum]
    grad_bqkv = jnp.concatenate([sum(jnp.sum(g.astype(F32), 0) for g in grads) for grads in grad_packed])
    grad_qkv = jnp.concatenate(grad_qkv, 1)
    grad_qkv_sum = scatter(grad_qkv)

    tensor_sums = jnp.sum(own_cot.astype(F32), (0, 1)).reshape(-1, LANES)
    bias_sums = jnp.concatenate([grad_bfc[0], grad_bqkv]).reshape(-1, LANES)
    lines = model // LANES
    if pair:
        used = 3 * lines + bias_sums.shape[0]
        extra = jnp.zeros((8 * (model // shard.shape[0]), LANES), F32)
        extra = extra.at[2 * lines:3 * lines].set(tensor_sums).at[3 * lines:used].set(bias_sums)
        grad_tokens, sums, grad_out_sum, mixed, other_mixed = go_home(
            [g[0] for g in grad_packed], [g[1] for g in grad_packed],
            [to_blocks(attended[0].reshape(blocks, group, wide), rows)] + attended[1:], weights, own_tokens, cotangent,
            mlp_back, ln_gain[None], extra, [grad_qkv, grad_proj_sum, other_mlp, other_out],
        )
        norm_sums, bias_sums = sums[:3 * lines].reshape(3, model), sums[3 * lines:used].reshape(-1)
        mixed, other_mixed = mixed.reshape(count, width), other_mixed.reshape(count, width)
        branches = mlp_out.astype(F32) + other_mlp.astype(F32)
        branches += tokens.reshape(count, model).astype(F32) + b_out
        branches += nt(mixed, full_out) + nt(other_mixed, other_out)
        result = branches.astype(BF).reshape(rows, group, model)
    else:
        mixed = jnp.concatenate(attended, 1).reshape(blocks, group, width)
        mixed = to_blocks(mixed, rows).reshape(count, width)
        grads = jnp.concatenate([g[0] for g in grad_packed], 1)
        back = sum_parts(nt(grads, full_qkv).reshape(blocks, group, model), 1).astype(BF)
        grad_hidden = mlp_back + to_blocks(back, rows).astype(F32)
        branches = mlp_out.astype(F32) + nt(mixed, full_out)
        branches = sum_parts(branches.reshape(rows, group, model), 1)
        result = join_parts((own_tokens.astype(F32) + branches + b_out).astype(BF), 1)
        normal, scale = normalize(own_tokens.astype(F32))
        grad_normal = grad_hidden * ln_gain
        grad_inputs = scale * (
            grad_normal
            - jnp.mean(grad_normal, -1, keepdims=True)
            - normal * jnp.mean(grad_normal * normal, -1, keepdims=True)
        )
        grad_tokens = join_parts((own_cot.astype(F32) + grad_inputs).astype(BF), 1)
        norm_sums = jnp.concatenate([jnp.sum(grad_hidden * normal, (0, 1)), jnp.sum(grad_hidden, (0, 1))])
        sums = jnp.concatenate([norm_sums.reshape(-1, LANES), tensor_sums, bias_sums], 0)
        sums = sum_all(sums, ("dp", "blk"))
        norm_sums = sum_all(sums[:3 * lines], ("tensor",)).reshape(3, model)
        bias_sums = sums[3 * lines:].reshape(-1)
        grad_out = lax.all_to_all(dot(cot.T, mixed).astype(BF), ("dp", "blk"), 0, 0, tiled=True)
        grad_out_sum = jnp.sum(grad_out.reshape(-1, shard.shape[0], width).astype(F32), 0)

    return (
        result,
        grad_tokens,
        norm_sums[0],
        norm_sums[1],
        by_kind(grad_qkv_sum, width),
        by_kind(bias_sums[None, inner:], width)[0],
        grad_out_sum.T,
        grad_fc_sum,
        bias_sums[:inner],
        grad_proj_sum.T,
        norm_sums[2],
    )


def solution(mesh):
    in_specs = (
        P("dp", "blk", None),
        P(),
        P(),
        P(("dp", "blk"), None, "tensor"),
        P(None, "tensor"),
        P("tensor", ("dp", "blk")),
        P(("dp", "blk"), "tensor"),
        P("tensor"),
        P("tensor", ("dp", "blk")),
        P(),
        P("dp", None),
        P("dp", "blk", None),
    )
    out_specs = (
        P("dp", "blk", None),
        P("dp", "blk", None),
        P(),
        P(),
        P(("dp", "blk"), None, "tensor"),
        P(None, "tensor"),
        P("tensor", ("dp", "blk")),
        P(("dp", "blk"), "tensor"),
        P("tensor"),
        P("tensor", ("dp", "blk")),
        P(),
    )
    return jax.shard_map(local, mesh=mesh, in_specs=in_specs, out_specs=out_specs, check_vma=False)
```

```python
import functools

import jax
import jax.numpy as jnp
from jax import lax
from jax.experimental import pallas as pl
from jax.experimental.pallas import tpu as pltpu
from jax.sharding import PartitionSpec as P

HEAD_DIM = 64
ROT_DIM = 16
LANES = 128
EPSILON = 1e-05
BF = jnp.bfloat16
F32 = jnp.float32
MIB = 1024 * 1024


def nt(a, b):
    return lax.dot_general(a, b, (((1,), (1,)), ((), ())), preferred_element_type=F32)


def nn(a, b):
    return lax.dot_general(a, b, (((1,), (0,)), ((), ())), preferred_element_type=F32)


def attn_kernel(bq, bk, part, waits, lo_ref, hi_ref, *refs):
    count = 2 if part else 1
    hidden, refs = refs[:count], refs[count + waits:]
    w_ref, bias_ref, do_ref, cos_ref, sin_ref, start_ref, o_ref = refs[:7]
    grads, refs = refs[7:7 + count], refs[7 + count:]
    (q2, qt, ks, vx, s_buf, p_buf, d_buf, dkt, dvt, keep, ahead, behind, starts) = refs
    length = do_ref.shape[0]
    nq = length // bq
    lane = lax.broadcasted_iota(jnp.int32, (1, LANES), 1)
    first = lane < HEAD_DIM
    half = ROT_DIM // 2
    to_score = HEAD_DIM ** (-0.5) * 1.4426950408889634
    mine_first = lax.axis_index("tensor") == 0 if part else None

    def load(base, size):
        if part:
            rows = []
            for n in range(size // (2 * part)):
                at = pl.ds(pl.multiple_of(base // 2 + n * part, part), part)
                a, b = hidden[0][at, :], hidden[1][at, :]
                rows += [jnp.where(mine_first, a, b), jnp.where(mine_first, b, a)]
            rows = jnp.concatenate(rows, 0)
        else:
            rows = hidden[0][pl.ds(base, size), :]
        packed = nn(rows, w_ref[...]) + bias_ref[...]
        return [packed[:, n * LANES:(n + 1) * LANES] for n in range(3)]

    def store(base, which, value):
        cols = slice(which * LANES, (which + 1) * LANES)
        size = value.shape[0]
        if not part:
            grads[0][pl.ds(base, size), cols] = value.astype(BF)
            return
        for n in range(size // (2 * part)):
            at = pl.ds(pl.multiple_of(base // 2 + n * part, part), part)
            a = value[2 * n * part:(2 * n + 1) * part]
            b = value[(2 * n + 1) * part:(2 * n + 2) * part]
            grads[0][at, cols] = jnp.where(mine_first, a, b).astype(BF)
            grads[1][at, cols] = jnp.where(mine_first, b, a).astype(BF)

    def rot(u, rows):
        return (u * keep[rows, :] + pltpu.roll(u, LANES - half, 1) * ahead[rows, :]
                + pltpu.roll(u, half, 1) * behind[rows, :])

    def rot_back(u, rows):
        return (u * keep[rows, :] + pltpu.roll(u * behind[rows, :], LANES - half, 1)
                + pltpu.roll(u * ahead[rows, :], half, 1))

    def tables(i, _):
        rows = pl.ds(pl.multiple_of(i * bq, bq), bq)
        c, s = cos_ref[:, rows], sin_ref[:, rows]
        rest = HEAD_DIM - ROT_DIM
        one, zero, gap = jnp.ones((rest, bq), F32), jnp.zeros((rest, bq), F32), jnp.zeros((half, bq), F32)
        keep[rows, :] = jnp.concatenate([c, c, one] * 2, 0).T
        ahead[rows, :] = jnp.concatenate([-s, gap, zero] * 2, 0).T
        behind[rows, :] = jnp.concatenate([gap, s, zero] * 2, 0).T
        starts[rows, :] = jnp.broadcast_to(start_ref[:, rows], (LANES, bq)).T
        return 0

    @pl.when(pl.program_id(0) == 0)
    def _():
        lax.fori_loop(0, nq, tables, 0)

    def prep(i, _):
        base = pl.multiple_of(i * bq, bq)
        rows = pl.ds(base, bq)
        q, k, v = load(base, bq)
        q = rot(q, rows)
        qs = (q * to_score).astype(BF)
        zero = jnp.zeros_like(qs)
        q2[0, rows, :] = jnp.where(first, qs, zero)
        q2[1, rows, :] = jnp.where(first, zero, qs)
        qt[:, rows] = q.T.astype(BF)
        ks[rows, :] = rot(k, rows).astype(BF)
        vx[rows, :LANES] = v.astype(BF)
        vx[rows, LANES:] = jnp.ones((bq, LANES), BF)
        dkt[:, rows] = jnp.zeros((LANES, bq), F32)
        dvt[:, rows] = jnp.zeros((LANES, bq), F32)
        return 0

    lax.fori_loop(0, nq, prep, 0)

    def q_block(i, _):
        rows = pl.ds(pl.multiple_of(i * bq, bq), bq)
        last = (i * bq) // bk
        least = lo_ref[i] // bk
        masked = jnp.clip((hi_ref[i] + bk - 1) // bk, least, last)
        q_h = (q2[0, rows, :], q2[1, rows, :])
        start = starts[rows, :]

        def scores(j, mx, mode):
            cols = pl.ds(pl.multiple_of(j * bk, bk), bk)
            k = ks[cols, :]
            out = []
            for h in range(2):
                s = nt(q_h[h], k)
                m = mx[h]
                for t in range(bk // LANES):
                    piece = s[:, t * LANES:(t + 1) * LANES]
                    if mode:
                        kidx = (j * bk + t * LANES + lane).astype(F32)
                        ok = kidx >= start
                        if mode == 2:
                            qidx = (i * bq + lax.broadcasted_iota(jnp.int32, (bq, 1), 0)).astype(F32)
                            ok = ok & (kidx <= qidx)
                        piece = jnp.where(ok, piece, -1e30)
                    s_buf[h, :, pl.ds(pl.multiple_of(j * bk + t * LANES, LANES), LANES)] = piece
                    m = jnp.maximum(m, piece)
                out.append(m)
            return tuple(out)

        mx = (jnp.full((bq, LANES), -1e30, F32),) * 2
        mx = lax.fori_loop(least, masked, lambda j, m: scores(j, m, 1), mx)
        mx = lax.fori_loop(masked, last, lambda j, m: scores(j, m, 0), mx)
        mx = scores(last, mx, 2)
        mx = [jnp.max(m, -1, keepdims=True) for m in mx]

        def weigh(j, acc):
            cols = pl.ds(pl.multiple_of(j * bk, bk), bk)
            v = vx[cols, :]
            out = []
            for h in range(2):
                p = jnp.exp2(s_buf[h, :, cols] - mx[h]).astype(BF)
                p_buf[h, :, cols] = p
                out.append(acc[h] + nn(p, v))
            return tuple(out)

        acc = (jnp.zeros((bq, 2 * LANES), F32),) * 2
        acc = lax.fori_loop(least, last + 1, weigh, acc)
        inv = [1.0 / a[:, LANES:] for a in acc]
        outs = [a[:, :LANES] * r for a, r in zip(acc, inv)]
        o = jnp.where(first, outs[0], outs[1])
        o_ref[rows, :] = o.astype(BF)
        do = do_ref[rows, :].astype(F32)
        dos, dots, deltas = [], [], []
        for h in range(2):
            mine = first if h == 0 else jnp.logical_not(first)
            d = jnp.where(mine, do * inv[h], 0.0).astype(BF)
            dos.append(d)
            df = d.astype(F32)
            deltas.append(jnp.sum(df * o, -1, keepdims=True))
            dots.append(df.T[h * HEAD_DIM:(h + 1) * HEAD_DIM].astype(BF))
        q_t = qt[:, rows]

        def back(j, acc):
            cols = pl.ds(pl.multiple_of(j * bk, bk), bk)
            v = vx[cols, :LANES]
            k = ks[cols, :]
            out = []
            for h in range(2):
                rows_h = slice(h * HEAD_DIM, (h + 1) * HEAD_DIM)
                p = p_buf[h, :, cols]
                dp = nt(dos[h], v)
                ds = (p.astype(F32) * (dp - deltas[h])).astype(BF)
                dvt[rows_h, cols] += nn(dots[h], p)
                dkt[rows_h, cols] += nn(q_t[rows_h], ds)
                out.append(acc[h] + nn(ds, k))
            return tuple(out)

        acc = (jnp.zeros((bq, LANES), F32),) * 2
        acc = lax.fori_loop(least, last + 1, back, acc)
        dq = jnp.where(first, acc[0], acc[1]) * HEAD_DIM ** (-0.5)
        store(i * bq, 0, rot_back(dq, rows))
        return 0

    def static_block(i):
        rows = slice(i * bq, (i + 1) * bq)
        width = (i + 1) * bq
        start = starts[rows, :]
        q_h = (q2[0, rows, :], q2[1, rows, :])
        mx = []
        for h in range(2):
            m = jnp.full((bq, LANES), -1e30, F32)
            for j in range(0, width, bk):
                s = nt(q_h[h], ks[j:j + bk, :])
                for t in range(0, bk, LANES):
                    kidx = (j + t + lane).astype(F32)
                    ok = kidx >= start
                    if j + t + LANES > i * bq:
                        qidx = (i * bq + lax.broadcasted_iota(jnp.int32, (bq, 1), 0)).astype(F32)
                        ok = ok & (kidx <= qidx)
                    piece = jnp.where(ok, s[:, t:t + LANES], -1e30)
                    s_buf[h, :, j + t:j + t + LANES] = piece
                    m = jnp.maximum(m, piece)
            mx.append(jnp.broadcast_to(jnp.max(m, -1, keepdims=True), (bq, LANES)))
        acc = []
        for h in range(2):
            for t in range(0, width, LANES):
                p_buf[h, :, t:t + LANES] = jnp.exp2(s_buf[h, :, t:t + LANES] - mx[h]).astype(BF)
            acc.append(nn(p_buf[h, :, :width], vx[:width, :]))
        inv = [1.0 / v[:, LANES:] for v in acc]
        outs = [v[:, :LANES] * r for v, r in zip(acc, inv)]
        o = jnp.where(first, outs[0], outs[1])
        o_ref[rows, :] = o.astype(BF)
        do = do_ref[rows, :].astype(F32)
        dq = []
        for h in range(2):
            mine = first if h == 0 else jnp.logical_not(first)
            rows_h = slice(h * HEAD_DIM, (h + 1) * HEAD_DIM)
            d = jnp.where(mine, do * inv[h], 0.0).astype(BF)
            df = d.astype(F32)
            delta = jnp.broadcast_to(jnp.sum(df * o, -1, keepdims=True), (bq, LANES))
            d_t = df.T[rows_h].astype(BF)
            q_t = qt[rows_h, rows]
            for j in range(0, width, bk):
                cols = slice(j, j + bk)
                dp = nt(d, vx[cols, :LANES])
                dvt[rows_h, cols] += nn(d_t, p_buf[h, :, cols])
                for t in range(0, bk, LANES):
                    at = slice(j + t, j + t + LANES)
                    d_buf[h, :, at] = (p_buf[h, :, at].astype(F32) * (dp[:, t:t + LANES] - delta)).astype(BF)
                dkt[rows_h, cols] += nn(q_t, d_buf[h, :, cols])
            dq.append(nn(d_buf[h, :, :width], ks[:width, :]))
        dq = jnp.where(first, dq[0], dq[1]) * HEAD_DIM ** (-0.5)
        store(i * bq, 0, rot_back(dq, rows))

    if nq <= 4:
        for i in range(nq):
            static_block(i)
    else:
        lax.fori_loop(0, nq, q_block, 0)

    def finish(i, _):
        base = pl.multiple_of(i * bq, bq)
        rows = pl.ds(base, bq)
        store(base, 1, rot_back(dkt[:, rows].T * HEAD_DIM ** (-0.5), rows))
        store(base, 2, dvt[:, rows].T)
        return 0

    lax.fori_loop(0, nq, finish, 0)


def attention(hidden, weights, bias, first_pair, do, position, start, part=0, waits=(), bq=512, bk=512):
    length, width = do.shape
    bq = min(bq, 2 ** 20 // length)
    bk = max(bq, min(bk, length))
    pairs = width // LANES
    freqs = 10000.0 ** (-jnp.arange(0, ROT_DIM, 2, dtype=F32) / ROT_DIM)
    phase = position.astype(F32)[None] * freqs[:, None]
    by_block = start.reshape(length // bq, bq)
    rows, model = hidden[0].shape
    once = pl.Buffered(1)
    columns = pl.BlockSpec((length, LANES), lambda g, *_: (0, g))
    triple = pl.BlockSpec((rows, 3 * LANES), lambda g, *_: (0, g))
    whole = lambda n: pl.BlockSpec((n, length), lambda g, *_: (0, 0), pipeline_mode=once)
    tri_out = jax.ShapeDtypeStruct((rows, 3 * width), BF)
    static = length // bq <= 4
    out = pl.pallas_call(
        functools.partial(attn_kernel, bq, bk, part, len(waits)),
        out_shape=[jax.ShapeDtypeStruct((length, width), BF)] + [tri_out] * len(hidden),
        grid_spec=pltpu.PrefetchScalarGridSpec(
            num_scalar_prefetch=2,
            grid=(pairs,),
            in_specs=[pl.BlockSpec((rows, model), lambda g, *_: (0, 0), pipeline_mode=once)] * len(hidden)
            + [pl.BlockSpec(memory_space=pl.ANY)] * len(waits)
            + [
                pl.BlockSpec((model, 3 * LANES), lambda g, *_: (0, first_pair + g)),
                pl.BlockSpec((1, 3 * LANES), lambda g, *_: (0, first_pair + g)),
                columns, whole(ROT_DIM // 2), whole(ROT_DIM // 2), whole(1),
            ],
            out_specs=[columns] + [triple] * len(hidden),
            scratch_shapes=[
                pltpu.VMEM((2, length, LANES), BF),
                pltpu.VMEM((LANES, length), BF),
                pltpu.VMEM((length, LANES), BF),
                pltpu.VMEM((length, 2 * LANES), BF),
                pltpu.VMEM((2, bq, length), F32),
                pltpu.VMEM((2, bq, length), BF),
                pltpu.VMEM((2, bq, length) if static else (8, LANES), BF),
                pltpu.VMEM((LANES, length), F32),
                pltpu.VMEM((LANES, length), F32),
            ] + [pltpu.VMEM((length, LANES), F32)] * 4,
        ),
        compiler_params=pltpu.CompilerParams(vmem_limit_bytes=56 * MIB),
        cost_estimate=pl.CostEstimate(flops=1000, bytes_accessed=1000, transcendentals=0),
    )(by_block.min(1), by_block.max(1), *hidden, *waits, weights, bias, do, jnp.cos(phase), jnp.sin(phase),
      start.astype(F32)[None])
    return out[0], list(out[1:])


MESH = pl.DeviceIdType.MESH


def remote(src, dst, send, recv, target):
    return pltpu.make_async_remote_copy(
        src_ref=src, dst_ref=dst, send_sem=send, recv_sem=recv, device_id=target, device_id_type=MESH
    )


def meet(others):
    barrier = pltpu.get_barrier_semaphore()
    for target in others:
        pl.semaphore_signal(barrier, inc=1, device_id=target, device_id_type=MESH)
    pl.semaphore_wait(barrier, len(others))


def gather_kernel(x_ref, tok_ref, gain_ref, bias_ref, out_ref, hid_ref, local_sem, recv, up, down, across, over):
    size = x_ref.shape[0]
    core, block = lax.axis_index("dp"), lax.axis_index("blk")
    z, y = block // 2, lax.rem(block, 2)
    depth = lax.axis_size("blk") // 2
    above, below = {"blk": block + 2}, {"blk": block - 2}
    beside, sibling = {"blk": block + 1 - 2 * y}, {"dp": 1 - core}

    def place(c, zz, yy):
        return (c * depth + zz) * 2 + yy

    def chunk(at):
        return out_ref.at[pl.ds(pl.multiple_of(at * size, size), size)]

    def copy(src, at, sem, target):
        return pltpu.make_async_remote_copy(
            src_ref=src, dst_ref=chunk(at), send_sem=sem, recv_sem=recv.at[at],
            device_id=target, device_id_type=pl.DeviceIdType.MESH,
        )

    def arrived(at):
        copy(chunk(at), at, local_sem, sibling).wait_recv()

    barrier = pltpu.get_barrier_semaphore()

    def greet(target):
        pl.semaphore_signal(barrier, inc=1, device_id=target, device_id_type=pl.DeviceIdType.MESH)

    def not_top(action):
        pl.when(z < depth - 1)(action)

    def not_bottom(action):
        pl.when(z > 0)(action)

    not_top(lambda: greet(above))
    not_bottom(lambda: greet(below))
    greet(beside)
    greet(sibling)
    pl.semaphore_wait(barrier, 2 + jnp.where(z > 0, 1, 0) + jnp.where(z < depth - 1, 1, 0))

    mine = place(core, z, y)
    keep = pltpu.make_async_copy(x_ref, chunk(mine), local_sem)
    not_top(lambda: copy(x_ref, mine, up.at[z], above).start())
    not_bottom(lambda: copy(x_ref, mine, down.at[z], below).start())
    copy(x_ref, mine, across.at[z], beside).start()
    copy(x_ref, mine, over.at[z * 2 + y], sibling).start()
    keep.start()

    for r in range(tok_ref.shape[0]):
        x = tok_ref[r].astype(F32)
        x = x - jnp.mean(x, -1, keepdims=True)
        x = x * lax.rsqrt(jnp.mean(x * x, -1, keepdims=True) + EPSILON)
        hid_ref[r] = (x * gain_ref[...] + bias_ref[...]).astype(BF)

    def from_beside(zz):
        at = place(core, zz, 1 - y)
        arrived(at)
        copy(chunk(at), at, over.at[zz * 2 + 1 - y], sibling).start()

    def from_line(zz, onward, sems, target):
        at = place(core, zz, y)
        arrived(at)
        onward(lambda: copy(chunk(at), at, sems.at[zz], target).start())
        copy(chunk(at), at, across.at[zz], beside).start()
        copy(chunk(at), at, over.at[zz * 2 + y], sibling).start()

    for step in range(1, depth):
        pl.when(z >= step)(lambda: from_line(z - step, not_top, up, above))
        pl.when(z + step < depth)(lambda: from_line(z + step, not_bottom, down, below))
    from_beside(z)
    for step in range(1, depth):
        pl.when(z >= step)(lambda: from_beside(z - step))
        pl.when(z + step < depth)(lambda: from_beside(z + step))

    keep.wait()
    for zz in range(depth):
        for yy in range(2):
            arrived(place(1 - core, zz, yy))
            copy(x_ref, mine, over.at[zz * 2 + yy], sibling).wait_send()
        copy(x_ref, mine, across.at[zz], beside).wait_send()
        pl.when((zz <= z) & (z < depth - 1))(lambda: copy(x_ref, mine, up.at[zz], above).wait_send())
        pl.when((zz >= z) & (z > 0))(lambda: copy(x_ref, mine, down.at[zz], below).wait_send())


def gather_weights(shard, tokens, gain, bias):
    cores, blocks = lax.axis_size("dp"), lax.axis_size("blk")
    rows, columns = shard.shape
    dma = pltpu.SemaphoreType.DMA
    hbm, vmem = pl.BlockSpec(memory_space=pl.ANY), pl.BlockSpec(memory_space=pltpu.VMEM)
    return pl.pallas_call(
        gather_kernel,
        out_shape=[
            jax.ShapeDtypeStruct((cores * blocks * rows, columns), shard.dtype),
            jax.ShapeDtypeStruct(tokens.shape, BF),
        ],
        in_specs=[hbm, vmem, vmem, vmem],
        out_specs=[hbm, vmem],
        scratch_shapes=[
            dma, dma((cores * blocks,)), dma((blocks // 2,)), dma((blocks // 2,)),
            dma((blocks // 2,)), dma((blocks,)),
        ],
        compiler_params=pltpu.CompilerParams(
            collective_id=0, has_side_effects=True, vmem_limit_bytes=32 * MIB
        ),
    )(shard, tokens, gain, bias)


class RowTransfer:
    def __init__(self, hid_ref, mine_ref, other_ref, blank, blank_sem, hid_send, hid_recv, side_send, side_recv):
        self.refs = hid_ref, mine_ref, other_ref, blank
        self.sems = blank_sem, hid_send, hid_recv, side_send, side_recv
        self.rows, group, _ = hid_ref.shape
        self.part = group // 2
        self.block, self.half = lax.axis_index("blk"), lax.axis_index("tensor")
        self.blocks = lax.axis_size("blk")
        self.has_row = self.block < self.rows
        self.facing = {"tensor": 1 - self.half}

    def piece(self, ref, at):
        return ref.at[pl.ds(pl.multiple_of(at * self.part, self.part), self.part)]

    def source(self, r):
        return self.refs[0].at[r, pl.ds(pl.multiple_of(self.half * self.part, self.part), self.part)]

    def row_copy(self, r):
        _, hid_send, hid_recv, _, _ = self.sems
        mine = self.piece(self.refs[1], self.block)
        return remote(self.source(r), mine, hid_send.at[r], hid_recv.at[self.block], {"blk": r})

    def own_row(self):
        return pltpu.make_async_copy(
            self.source(self.block), self.piece(self.refs[1], self.block), self.sems[1].at[self.block]
        )

    def side_copy(self, s):
        _, _, _, side_send, side_recv = self.sems
        _, mine, other, _ = self.refs
        return remote(self.piece(mine, s), self.piece(other, s), side_send.at[s], side_recv.at[s], self.facing)

    def blanks(self):
        _, mine, other, blank = self.refs
        return [
            pltpu.make_async_copy(blank, self.piece(ref, s), self.sems[0].at[n * self.blocks + s])
            for n, ref in enumerate((mine, other)) for s in range(self.blocks)
        ]

    def to_block(self, n, action):
        r = lax.rem(self.block + n, self.blocks)
        pl.when(r < self.rows)(lambda: action(self.row_copy(r)))

    def start(self):
        meet([{"blk": lax.rem(self.block + n, self.blocks)} for n in range(1, self.blocks)] + [self.facing])
        for n in range(1, self.blocks):
            self.to_block(n, lambda copy: copy.start())

        @pl.when(self.has_row)
        def _():
            self.own_row().start()
            self.own_row().wait()
            self.side_copy(self.block).start()

        @pl.when(jnp.logical_not(self.has_row))
        def _():
            self.refs[3][...] = jnp.zeros_like(self.refs[3])
            for copy in self.blanks():
                copy.start()

    def onward(self, n):
        @pl.when(self.has_row)
        def _():
            s = lax.rem(self.block + self.blocks - n, self.blocks)
            mine = self.piece(self.refs[1], s)
            remote(mine, mine, self.sems[3].at[s], self.sems[2].at[s], self.facing).wait_recv()
            self.side_copy(s).start()

    def finish(self):
        for n in range(1, self.blocks):
            self.to_block(n, lambda copy: copy.wait_send())

        @pl.when(self.has_row)
        def _():
            for s in range(self.blocks):
                self.side_copy(s).wait()

        @pl.when(jnp.logical_not(self.has_row))
        def _():
            for copy in self.blanks():
                copy.wait()


def tail_kernel(groups, waits, *refs):
    g_mine, g_other, heads = refs[:groups], refs[groups:2 * groups], refs[2 * groups:3 * groups]
    (w_ref, tok_ref, cot_ref, add_ref, gain_ref, extra_ref, out_ref, sum_ref, wgrad_ref, mixed_ref, facing_ref,
     sent, got, home_send, home, grads, mix, total, terms, paired, merged, inbox, norms, small, small_in, small_box, small_out,
     a_send, a_recv, b_send, b_recv, c_send, c_recv, c_local, d_send, d_recv, e_send, e_recv, e_local,
     f_send, f_recv, g_send, g_recv, h_send, h_recv, i_send, i_recv) = refs[3 * groups + waits:]
    rows, part, model = tok_ref.shape[0], tok_ref.shape[1] // 2, tok_ref.shape[2]
    block, half = lax.axis_index("blk"), lax.axis_index("tensor")
    blocks = lax.axis_size("blk")
    facing = {"tensor": 1 - half}
    has_row = block < rows
    count = lax.axis_size("dp") * blocks
    me = lax.axis_index("dp") * blocks + block

    def peers():
        return [lax.rem(me + n, count) for n in range(1, count)]

    def device(j):
        return {"dp": j // blocks, "blk": lax.rem(j, blocks)}

    meet([device(j) for j in peers()] + [facing])

    def product(parts, s):
        at, total, first = pl.ds(pl.multiple_of(s * part, part), part), None, 0
        for g in parts:
            width = g.shape[1]
            term = nt(g[at, :], w_ref[:, first:first + width])
            total, first = term if total is None else total + term, first + width
        return total

    def across(s):
        return remote(sent.at[s], got.at[s], a_send.at[s], a_recv.at[s], facing)

    def homeward(s):
        return remote(home_send.at[s], home.at[block], b_send.at[s], b_recv.at[block], {"blk": s})

    def own_half(ref, r):
        return ref.at[r, pl.ds(pl.multiple_of(half * part, part), part)]

    def share(r):
        return remote(grads.at[r], own_half(out_ref, r), c_send.at[r], c_recv.at[r], facing)

    def keep(r):
        return pltpu.make_async_copy(grads.at[r], own_half(out_ref, r), c_local.at[r])

    def heads_of(ref, k, r):
        wide = heads[-1].shape[1]
        return ref.at[r, :, k * wide:(k + 1) * wide]

    def attended(k, s):
        return heads[k].at[pl.ds(pl.multiple_of(s * 2 * part, 2 * part), 2 * part)]

    def heads_home(k, s):
        return remote(attended(k, s), heads_of(mix, k, block), d_send.at[k * blocks + s],
                      d_recv.at[k * blocks + block], {"blk": s})

    def own_heads(k):
        return pltpu.make_async_copy(attended(k, block), heads_of(mix, k, block), d_send.at[k * blocks + block])

    def send_heads(k, n):
        if n == 0:
            own_heads(k).start()
        else:
            heads_home(k, lax.rem(block + n, blocks)).start()

    def landed(r):
        return pltpu.make_async_copy(heads[0].at[r], heads_of(mix, 0, r), d_send.at[r])

    def heads_across(k, r):
        return remote(heads_of(mix, k, r), heads_of(facing_ref, k, r), e_send.at[k * blocks + r],
                      e_recv.at[k * blocks + r], facing)

    @pl.when(has_row)
    def _():
        for n in range(blocks):
            s = lax.rem(block + n, blocks)
            sent[s] = product(g_other, s).astype(BF)
            across(s).start()

    for r in range(rows):
        landed(r).start()

    def keep_heads(r):
        return pltpu.make_async_copy(mix.at[r], mixed_ref.at[r], e_local.at[r])

    norms[...] = jnp.zeros_like(norms)
    total[...] = jnp.zeros_like(total)

    def forward(n):
        s = lax.rem(block + n, blocks)

        @pl.when(has_row)
        def _():
            grad = product(g_mine, s)
            across(s).wait_recv()
            grad = (grad + got[s].astype(F32)).astype(BF)
            if n == 0:
                home[s] = grad
            else:
                home_send[s] = grad
                homeward(s).start()

    def heads_arrive(k, n, r):
        if n:
            here = heads_of(mix, k, r)
            remote(here, here, e_send.at[k * blocks + r], d_recv.at[k * blocks + r], facing).wait_recv()
        else:
            own_heads(k).wait()
        heads_across(k, r).start()

    def norm(n):
        r = lax.rem(block + blocks - n, blocks)

        @pl.when(r < rows)
        def _():
            landed(r).wait()
            heads_across(0, r).start()
            if n:
                remote(home_send.at[r], home.at[r], b_send.at[r], b_recv.at[r], facing).wait_recv()
            grad = home[r].astype(F32) + add_ref[r].astype(F32)
            here = pl.ds(pl.multiple_of(half * part, part), part)
            x = tok_ref[r, here, :].astype(F32)
            x = x - jnp.mean(x, -1, keepdims=True)
            scale = lax.rsqrt(jnp.mean(x * x, -1, keepdims=True) + EPSILON)
            x = x * scale
            norms[0:1, :] += jnp.sum(grad * x, 0, keepdims=True)
            norms[1:2, :] += jnp.sum(grad, 0, keepdims=True)
            grad = grad * gain_ref[...]
            grad = grad - jnp.mean(grad, -1, keepdims=True) - x * jnp.mean(grad * x, -1, keepdims=True)
            own = cot_ref[r, here, :].astype(F32)
            norms[2:3, :] += jnp.sum(own, 0, keepdims=True)
            grads[r] = (own + scale * grad).astype(BF)
            keep(r).start()

    lag = 2
    for n in range(blocks + lag):
        if n < blocks:
            forward(n)
        if n >= lag:
            norm(n - lag)
        if n == blocks - 1:
            @pl.when(has_row)
            def _():
                for k in range(1, groups):
                    for other in range(blocks):
                        send_heads(k, other)

    small[...] = extra_ref[...]
    lines = norms.shape[1] // LANES
    for n in range(3):
        for k in range(lines):
            small[n * lines + k:n * lines + k + 1, :] = norms[n:n + 1, k * LANES:(k + 1) * LANES]
    shared = small.at[pl.ds(0, 3 * lines)]
    swapped = remote(shared, small_in, g_send, g_recv, facing)
    swapped.start()
    for r in range(rows):
        share(r).start()

    for n in range(blocks):
        r = lax.rem(block + blocks - n, blocks)

        @pl.when(r < rows)
        def _():
            for k in range(1, groups):
                heads_arrive(k, n, r)
            keep_heads(r).start()
            total[...] += nn(cot_ref[r].T, mix[r])

    size = terms.shape[1]
    core = lax.axis_index("dp")
    for j in range(count):
        terms[j] = total[j * size:(j + 1) * size].astype(BF)

    def to_sibling():
        theirs = terms.at[pl.ds((1 - core) * blocks, blocks)]
        return remote(theirs, paired, f_send.at[blocks], f_recv.at[blocks], {"dp": 1 - core})

    to_sibling().start()

    swapped.wait()
    small[:3 * lines, :] += small_in[...]
    to_sibling().wait()

    def term(s):
        return remote(merged.at[s], inbox.at[block], f_send.at[s], f_recv.at[block], {"blk": s})

    for s in range(blocks):
        merged[s] = (terms[core * blocks + s].astype(F32) + paired[s].astype(F32)).astype(BF)
    for n in range(1, blocks):
        term(lax.rem(block + n, blocks)).start()

    def line(ref, j):
        return ref.at[pl.ds(pl.multiple_of(j * 8, 8), 8)]

    def small_term(j):
        return remote(line(small, j), small_box.at[me], h_send.at[j], h_recv.at[me], device(j))

    def small_sum(j):
        return remote(line(small_out, me), line(small_out, me), i_send.at[j], i_recv.at[me], device(j))

    for j in peers():
        small_term(j).start()
    small_box[me] = small[pl.ds(pl.multiple_of(me * 8, 8), 8), :]
    for j in peers():
        remote(small_box.at[j], small_box.at[j], h_send.at[j], h_recv.at[j], device(j)).wait_recv()
    added = small_box[0]
    for j in range(1, count):
        added = added + small_box[j]
    small_out[pl.ds(pl.multiple_of(me * 8, 8), 8), :] = added
    for j in peers():
        small_sum(j).start()
    inbox[block] = merged[block]
    for n in range(1, blocks):
        s = lax.rem(block + n, blocks)
        remote(inbox.at[s], inbox.at[s], f_send.at[s], f_recv.at[s], facing).wait_recv()
    added = inbox[0].astype(F32)
    for s in range(1, blocks):
        added = added + inbox[s].astype(F32)
    wgrad_ref[...] = added
    for j in peers():
        remote(line(small_out, j), line(small_out, j), i_send.at[j], i_recv.at[j], device(j)).wait_recv()
    sum_ref[...] = small_out[...]
    for j in peers():
        small_term(j).wait_send()
        small_sum(j).wait_send()
    for n in range(1, blocks):
        term(lax.rem(block + n, blocks)).wait_send()

    for r in range(rows):
        share(r).wait()
        keep(r).wait()
        keep_heads(r).wait()
        for k in range(groups):
            heads_across(k, r).wait()

    @pl.when(has_row)
    def _():
        for s in range(blocks):
            across(s).wait_send()
        for n in range(1, blocks):
            homeward(lax.rem(block + n, blocks)).wait_send()
            for k in range(1, groups):
                heads_home(k, lax.rem(block + n, blocks)).wait_send()


def go_home(g_mine, g_other, attended, weights, tokens, cot, add, gain, extra, waits=()):
    rows, part, model = tokens.shape[0], tokens.shape[1] // 2, tokens.shape[2]
    blocks = lax.axis_size("blk")
    wide = sum(g.shape[1] for g in g_mine)
    dma = pltpu.SemaphoreType.DMA
    groups, hbm = len(g_mine), pl.BlockSpec(memory_space=pl.ANY)
    count = lax.axis_size("dp") * blocks
    wide_heads = sum(o.shape[-1] for o in attended)
    lines = 3 * model // LANES
    heads = jax.ShapeDtypeStruct((rows, 2 * part, wide_heads), BF)
    vmem = pl.BlockSpec(memory_space=pltpu.VMEM)
    return pl.pallas_call(
        functools.partial(tail_kernel, groups, len(waits)),
        grid=(1,),
        out_shape=[jax.ShapeDtypeStruct((rows, 2 * part, model), BF), jax.ShapeDtypeStruct((8 * count, LANES), F32),
                   jax.ShapeDtypeStruct((model // count, wide_heads), F32), heads, heads],
        in_specs=[vmem] * (2 * groups) + [hbm] * (groups + len(waits))
        + [pl.BlockSpec((model, wide), lambda i: (0, 0))] + [vmem] * 5,
        out_specs=[hbm, vmem, vmem, hbm, hbm],
        scratch_shapes=[pltpu.VMEM((blocks, part, model), BF)] * 4 + [pltpu.VMEM((rows, part, model), BF)]
        + [pltpu.VMEM(heads.shape, BF), pltpu.VMEM((model, wide_heads), F32)]
        + [pltpu.VMEM((count, model // count, wide_heads), BF)]
        + [pltpu.VMEM((blocks, model // count, wide_heads), BF)] * 3
        + [pltpu.VMEM((8, model), F32), pltpu.VMEM((8 * count, LANES), F32), pltpu.VMEM((lines, LANES), F32)]
        + [pltpu.VMEM((count, 8, LANES), F32), pltpu.VMEM((8 * count, LANES), F32)]
        + [dma((blocks,))] * 4 + [dma((rows,))] * 3 + [dma((groups * blocks,))] * 4 + [dma((rows,))]
        + [dma((count,))] * 2 + [dma] * 2 + [dma((count,))] * 4,
        compiler_params=pltpu.CompilerParams(
            collective_id=1, has_side_effects=True, vmem_limit_bytes=56 * MIB
        ),
        cost_estimate=pl.CostEstimate(flops=1000, bytes_accessed=1000, transcendentals=0),
    )(*g_mine, *g_other, *attended, *waits, weights, tokens, cot, add, gain, extra)


def weight_grad_kernel(half, waits, a_ref, b_ref, *refs):
    x_ref, y_ref, ax_ref, by_ref, turned = refs[waits:]
    step = pl.program_id(0)

    @pl.when(step == 0)
    def _():
        turned[...] = a_ref[...].T

    @pl.when(step == half)
    def _():
        turned[...] = b_ref[...].T

    @pl.when(step < half)
    def _():
        ax_ref[...] = nn(turned[...], x_ref[...]).astype(BF)

    @pl.when(step >= half)
    def _():
        by_ref[...] = nn(turned[...], y_ref[...]).astype(BF)


def weight_grads(a, x, b, y, waits=(), tile=512):
    count, model = a.shape
    inner = x.shape[1]
    tile = min(tile, inner)
    half = inner // tile
    whole = pl.BlockSpec((count, model), lambda i: (0, 0), pipeline_mode=pl.Buffered(1))
    return pl.pallas_call(
        functools.partial(weight_grad_kernel, half, len(waits)),
        grid=(2 * half,),
        out_shape=[jax.ShapeDtypeStruct((model, inner), BF)] * 2,
        in_specs=[
            whole, whole, *[pl.BlockSpec(memory_space=pl.ANY)] * len(waits),
            pl.BlockSpec((count, tile), lambda i: (0, jnp.minimum(i, half - 1))),
            pl.BlockSpec((count, tile), lambda i: (0, jnp.maximum(i - half, 0))),
        ],
        out_specs=[
            pl.BlockSpec((model, tile), lambda i: (0, jnp.minimum(i, half - 1))),
            pl.BlockSpec((model, tile), lambda i: (0, jnp.maximum(i - half, 0))),
        ],
        scratch_shapes=[pltpu.VMEM((model, count), BF)],
        compiler_params=pltpu.CompilerParams(vmem_limit_bytes=48 * MIB),
        cost_estimate=pl.CostEstimate(flops=1000, bytes_accessed=1000, transcendentals=0),
    )(a, b, *waits, x, y)


def mlp_kernel(tile, waits, moves, hid_ref, cot_ref, wf_ref, wp_ref, bias_ref, *refs):
    refs = refs[waits:]
    act_ref, gin_ref, res_ref, back_ref, gb_ref = refs[moves:moves + 5]
    if moves:
        step, steps = pl.program_id(0), pl.num_programs(0)
        rows = RowTransfer(refs[0], *refs[moves + 5:])
        pl.when(step == 0)(rows.start)
    hid, cot = hid_ref[...], cot_ref[...]

    @pl.when(pl.program_id(0) == 0)
    def _():
        gb_ref[...] = jnp.zeros_like(gb_ref)

    res = back = None
    for n in range(wf_ref.shape[1] // tile):
        cols = slice(n * tile, (n + 1) * tile)
        wf, wp = wf_ref[:, cols], wp_ref[:, cols]
        inner = nn(hid, wf) + bias_ref[:, cols]
        grad_act = nn(cot, wp)
        size = jnp.abs(inner)
        t = 1.0 / (1.0 + (0.3275911 * 0.7071067811865476) * size)
        bell = jnp.exp2((-0.5 * 1.4426950408889634) * inner * inner)
        tail = ((((0.5 * 1.061405429 * t - 0.5 * 1.453152027) * t + 0.5 * 1.421413741) * t
                 - 0.5 * 0.284496736) * t + 0.5 * 0.254829592) * t * bell
        below = jnp.where(inner < 0, tail, 1.0 - tail)
        act = (inner * below).astype(BF)
        grad_inner = (grad_act * (below + inner * (bell * 0.3989422804014327))).astype(BF)
        act_ref[:, cols] = act
        gin_ref[:, cols] = grad_inner
        gb_ref[:, cols] += jnp.sum(grad_inner.astype(F32), 0, keepdims=True)
        r, b = nt(act, wp), nt(grad_inner, wf)
        res, back = (r, b) if res is None else (res + r, back + b)
    res_ref[...] = res.astype(BF)
    back_ref[...] = back.astype(BF)
    if moves:
        for n in range(1, rows.blocks):
            pl.when(step == jnp.minimum(n, steps - 1))(lambda: rows.onward(n))
        pl.when(step == steps - 1)(rows.finish)


def mlp(hidden, cot, weights, first_block, bias, waits=(), moved=None, size=256, tile=512):
    count, model = hidden.shape
    inner = bias.shape[1]
    tile = min(tile, inner)
    rows = lambda n: pl.BlockSpec((size, n), lambda i: (i, 0))
    matrix = lambda n: pl.BlockSpec((model, inner), lambda i: (0, first_block + n), pipeline_mode=pl.Buffered(1))
    vector = pl.BlockSpec((1, inner), lambda i: (0, 0))
    hbm = pl.BlockSpec(memory_space=pl.ANY)
    shape = lambda n: jax.ShapeDtypeStruct((count, n), BF)
    moves, outs, scratch, params = (), [], [], {}
    if moved is not None:
        blocks, dma = lax.axis_size("blk"), pltpu.SemaphoreType.DMA
        part = moved.shape[1] // 2
        moves, outs = (moved,), [jax.ShapeDtypeStruct((blocks * part, model), BF)] * 2
        scratch = [pltpu.VMEM((part, model), BF), dma((2 * blocks,))] + [dma((blocks,))] * 4
        params = dict(collective_id=2, has_side_effects=True)
    return pl.pallas_call(
        functools.partial(mlp_kernel, tile, len(waits), len(moves)),
        grid=(count // size,),
        out_shape=[shape(inner), shape(inner), shape(model), shape(model), jax.ShapeDtypeStruct((1, inner), F32)] + outs,
        in_specs=[rows(model), rows(model), matrix(0), matrix(1), vector] + [hbm] * (len(waits) + len(moves)),
        out_specs=[rows(inner), rows(inner), rows(model), rows(model), vector] + [hbm] * len(outs),
        scratch_shapes=scratch,
        compiler_params=pltpu.CompilerParams(vmem_limit_bytes=56 * MIB, **params),
        cost_estimate=pl.CostEstimate(flops=1000, bytes_accessed=1000, transcendentals=0),
    )(hidden, cot, weights, weights, bias, *waits, *moves)


def normalize(values):
    center = values - jnp.mean(values, -1, keepdims=True)
    spread = jnp.mean(center * center, -1, keepdims=True)
    scale = lax.rsqrt(spread + EPSILON)
    return center * scale, scale


def swap(value):
    return lax.ppermute(value, "tensor", [(0, 1), (1, 0)])


def split_tensor(value, axis):
    shape = value.shape
    parts = lax.axis_size("tensor")
    return value.reshape(shape[:axis] + (parts, shape[axis] // parts) + shape[axis + 1:])


def part_of(value, axis, which):
    return lax.dynamic_index_in_dim(split_tensor(value, axis), which, axis, keepdims=False)


def sum_parts(value, axis):
    mine = lax.axis_index("tensor")
    if lax.axis_size("tensor") == 2:
        other = swap(part_of(value, axis, 1 - mine).astype(BF))
        return part_of(value, axis, mine).astype(F32) + other.astype(F32)
    return lax.psum_scatter(
        value.astype(BF), "tensor", scatter_dimension=axis, tiled=True
    ).astype(F32)


def join_parts(value, axis):
    if lax.axis_size("tensor") != 2:
        return lax.all_gather(value, "tensor", axis=axis, tiled=True)
    other = swap(value)
    first = lax.axis_index("tensor") == 0
    low, high = jnp.where(first, value, other), jnp.where(first, other, value)
    return jnp.concatenate([low, high], axis)


def to_rows(value):
    blocks = lax.axis_size("blk")
    pad = jnp.zeros((blocks - value.shape[0],) + value.shape[1:], value.dtype)
    return lax.all_to_all(jnp.concatenate([value, pad], 0), "blk", 0, 0, tiled=True)


def to_blocks(value, rows):
    return lax.all_to_all(value, "blk", 0, 0, tiled=True)[:rows]


def sum_all(value, axes):
    for axis in axes:
        size = lax.axis_size(axis)
        step = 1
        while step < size:
            value = value + lax.ppermute(value, axis, [(i, i ^ step) for i in range(size)])
            step *= 2
    return value


def by_pair(value, width):
    count = value.shape[0]
    return value.reshape(count, 3, width // LANES, LANES).transpose(0, 2, 1, 3).reshape(count, 3 * width)


def by_kind(value, width):
    count = value.shape[0]
    return value.reshape(count, width // LANES, 3, LANES).transpose(0, 2, 1, 3).reshape(count, 3, width)


def scatter(value):
    return lax.psum_scatter(value, ("dp", "blk"), scatter_dimension=0, tiled=True).astype(F32)


def dot(a, b):
    return jnp.dot(a, b, preferred_element_type=F32)


def local(
    tokens, ln_gain, ln_bias, w_qkv, b_qkv, w_out, w_fc, b_fc, w_proj, b_out, bounds, cotangent
):
    rows, group, model = tokens.shape
    width, inner = b_qkv.shape[1], b_fc.shape[0]
    blocks, parts = lax.axis_size("blk"), lax.axis_size("tensor")
    length = blocks * group
    count = rows * group
    part = group // parts

    mine = lax.axis_index("tensor")
    pair = parts == 2 and (lax.axis_size("dp"), blocks) == (2, 8)
    cot = cotangent.reshape(count, model)

    shard = jnp.concatenate([by_pair(w_qkv, width), w_out.T, w_fc, w_proj.T], 1)
    if pair:
        weights, hidden = gather_weights(shard, tokens, ln_gain[None], ln_bias[None])
    else:
        hidden = (normalize(tokens.astype(F32))[0] * ln_gain + ln_bias).astype(BF)
        weights = lax.all_gather(shard, ("dp", "blk"), axis=0, tiled=True)
        row_hidden = [join_parts(to_rows(part_of(hidden, 1, mine)), 1).reshape(length, model)]
    flat_hidden = hidden.reshape(count, model)
    full_qkv, full_out = weights[:, :3 * width], weights[:, 3 * width:4 * width]

    row_bounds = lax.dynamic_index_in_dim(
        bounds, jnp.minimum(lax.axis_index("blk"), rows - 1), 0, keepdims=False
    )
    index = jnp.arange(length, dtype=jnp.int32)
    start = jnp.max(jnp.where(row_bounds[:, None] <= index[None], row_bounds[:, None], 0), 0)

    groups = max(1, width // (2 * LANES))
    wide = width // groups
    cuts = [slice(n * wide, (n + 1) * wide) for n in range(groups)]
    grad_mixed = dot(cot, full_out).astype(BF).reshape(rows, group, width)
    row_grads = [to_rows(grad_mixed[:, :, cut]).reshape(length, wide) for cut in cuts]

    other_out = swap(full_out) if pair else None
    activated, grad_inner, mlp_out, mlp_back, grad_bfc, *moved = mlp(
        flat_hidden, cot, weights, 4 * width // inner, b_fc[None], (grad_mixed,), hidden if pair else None
    )
    row_hidden = moved or row_hidden
    mlp_back = sum_parts(mlp_back.reshape(rows, group, model), 1)
    grad_fc, grad_proj = weight_grads(
        flat_hidden, grad_inner, cot, activated, [row_grads[0]] + [other_out] * pair
    )
    grad_fc_sum, grad_proj_sum = scatter(grad_fc), scatter(grad_proj)
    if pair:
        mlp_back = mlp_back.astype(BF)
        other_mlp = swap(mlp_out)

    bias = by_pair(b_qkv[None], width)
    own_tokens, own_cot = part_of(tokens, 1, mine), part_of(cotangent, 1, mine)
    grad_packed, grad_qkv, attended = [], [], []
    waits = [grad_fc]
    for n, row_grad in enumerate(row_grads):
        out, grads = attention(
            row_hidden, weights, bias, n * (wide // LANES), row_grad, index - start, start,
            part if pair else 0, waits,
        )
        attended.append(out)
        grad_packed.append(grads)
        grad_qkv.append(sum(dot(h.T, g) for h, g in zip(row_hidden, grads)).astype(BF))
        waits = [out, grad_fc_sum]
    grad_bqkv = jnp.concatenate([sum(jnp.sum(g.astype(F32), 0) for g in grads) for grads in grad_packed])
    grad_qkv = jnp.concatenate(grad_qkv, 1)
    grad_qkv_sum = scatter(grad_qkv)

    tensor_sums = jnp.sum(own_cot.astype(F32), (0, 1)).reshape(-1, LANES)
    bias_sums = jnp.concatenate([grad_bfc[0], grad_bqkv]).reshape(-1, LANES)
    lines = model // LANES
    if pair:
        used = 3 * lines + bias_sums.shape[0]
        extra = jnp.zeros((8 * (model // shard.shape[0]), LANES), F32)
        extra = extra.at[3 * lines:used].set(bias_sums)
        grad_tokens, sums, grad_out_sum, mixed, other_mixed = go_home(
            [g[0] for g in grad_packed], [g[1] for g in grad_packed],
            [to_blocks(attended[0].reshape(blocks, group, wide), rows)] + attended[1:], weights, tokens, cotangent,
            mlp_back, ln_gain[None], extra, [grad_qkv, grad_proj_sum, other_mlp, other_out],
        )
        norm_sums, bias_sums = sums[:3 * lines].reshape(3, model), sums[3 * lines:used].reshape(-1)
        mixed, other_mixed = mixed.reshape(count, width), other_mixed.reshape(count, width)
        branches = mlp_out.astype(F32) + other_mlp.astype(F32)
        branches += tokens.reshape(count, model).astype(F32) + b_out
        branches += nt(mixed, full_out) + nt(other_mixed, other_out)
        result = branches.astype(BF).reshape(rows, group, model)
    else:
        mixed = jnp.concatenate(attended, 1).reshape(blocks, group, width)
        mixed = to_blocks(mixed, rows).reshape(count, width)
        grads = jnp.concatenate([g[0] for g in grad_packed], 1)
        back = sum_parts(nt(grads, full_qkv).reshape(blocks, group, model), 1).astype(BF)
        grad_hidden = mlp_back + to_blocks(back, rows).astype(F32)
        branches = mlp_out.astype(F32) + nt(mixed, full_out)
        branches = sum_parts(branches.reshape(rows, group, model), 1)
        result = join_parts((own_tokens.astype(F32) + branches + b_out).astype(BF), 1)
        normal, scale = normalize(own_tokens.astype(F32))
        grad_normal = grad_hidden * ln_gain
        grad_inputs = scale * (
            grad_normal
            - jnp.mean(grad_normal, -1, keepdims=True)
            - normal * jnp.mean(grad_normal * normal, -1, keepdims=True)
        )
        grad_tokens = join_parts((own_cot.astype(F32) + grad_inputs).astype(BF), 1)
        norm_sums = jnp.concatenate([jnp.sum(grad_hidden * normal, (0, 1)), jnp.sum(grad_hidden, (0, 1))])
        sums = jnp.concatenate([norm_sums.reshape(-1, LANES), tensor_sums, bias_sums], 0)
        sums = sum_all(sums, ("dp", "blk"))
        norm_sums = sum_all(sums[:3 * lines], ("tensor",)).reshape(3, model)
        bias_sums = sums[3 * lines:].reshape(-1)
        grad_out = lax.all_to_all(dot(cot.T, mixed).astype(BF), ("dp", "blk"), 0, 0, tiled=True)
        grad_out_sum = jnp.sum(grad_out.reshape(-1, shard.shape[0], width).astype(F32), 0)

    return (
        result,
        grad_tokens,
        norm_sums[0],
        norm_sums[1],
        by_kind(grad_qkv_sum, width),
        by_kind(bias_sums[None, inner:], width)[0],
        grad_out_sum.T,
        grad_fc_sum,
        bias_sums[:inner],
        grad_proj_sum.T,
        norm_sums[2],
    )


def solution(mesh):
    in_specs = (
        P("dp", "blk", None),
        P(),
        P(),
        P(("dp", "blk"), None, "tensor"),
        P(None, "tensor"),
        P("tensor", ("dp", "blk")),
        P(("dp", "blk"), "tensor"),
        P("tensor"),
        P("tensor", ("dp", "blk")),
        P(),
        P("dp", None),
        P("dp", "blk", None),
    )
    out_specs = (
        P("dp", "blk", None),
        P("dp", "blk", None),
        P(),
        P(),
        P(("dp", "blk"), None, "tensor"),
        P(None, "tensor"),
        P("tensor", ("dp", "blk")),
        P(("dp", "blk"), "tensor"),
        P("tensor"),
        P("tensor", ("dp", "blk")),
        P(),
    )
    return jax.shard_map(local, mesh=mesh, in_specs=in_specs, out_specs=out_specs, check_vma=False)
```
